32 devices in a mesh: dp: 8 (over z, x), tensor: 4 (over y, core).
Axes of the slice: x: 2, y: 2, z: 4, core: 2. Of those that a mesh axis runs over, the one named last changes fastest.
Arguments:
- patches: bfloat16 [64, 197, 768], P('dp'), may hold values from -6 to 6
- attn_gain: bfloat16 [768], replicated, may hold values from 0.25 to 1.75
- attn_shift: bfloat16 [768], replicated, may hold values from -3 to 3
- qkv_weight: bfloat16 [3, 768, 768], P(None, 'dp', 'tensor'), may hold values from -0.21875 to 0.21875
- qv_bias: bfloat16 [2, 768], P(None, 'tensor'), may hold values from -3 to 3
- out_weight: bfloat16 [768, 768], P('tensor', 'dp'), may hold values from -0.875 to 0.875
- out_bias: bfloat16 [768], replicated, may hold values from -3 to 3
- mlp_gain: bfloat16 [768], replicated, may hold values from 0.25 to 1.75
- mlp_shift: bfloat16 [768], replicated, may hold values from -3 to 3
- fc1_weight: bfloat16 [768, 3072], P('dp', 'tensor'), may hold values from -0.21875 to 0.21875
- fc1_bias: bfloat16 [3072], P('tensor'), may hold values from -3 to 3
- fc2_weight: bfloat16 [3072, 768], P('tensor', 'dp'), may hold values from -0.109375 to 0.109375
- fc2_bias: bfloat16 [768], replicated, may hold values from -3 to 3
- cotangent: bfloat16 [64, 197, 768], P('dp'), may hold values from -6 to 6
Outputs:
- encoded: bfloat16 [64, 197, 768], P('dp')
- patch_grad: bfloat16 [64, 197, 768], P('dp')
- attn_gain_grad: float32 [768], replicated
- attn_shift_grad: float32 [768], replicated
- qkv_weight_grad: float32 [3, 768, 768], P(None, 'dp', 'tensor')
- qv_bias_grad: float32 [2, 768], P(None, 'tensor')
- out_weight_grad: float32 [768, 768], P('tensor', 'dp')
- out_bias_grad: float32 [768], replicated
- mlp_gain_grad: float32 [768], replicated
- mlp_shift_grad: float32 [768], replicated
- fc1_weight_grad: float32 [768, 3072], P('dp', 'tensor')
- fc1_bias_grad: float32 [3072], P('tensor')
- fc2_weight_grad: float32 [3072, 768], P('tensor', 'dp')
- fc2_bias_grad: float32 [768], replicated
The draws below stay inside these ranges and needn't reach their ends.
All inputs are finite; a program needn't handle non-finite values.
Results may differ from the reference program's by a relative error of at most 0.02.
Values may be sent and summed in bfloat16 or wider, within the bound.
No kernel may reach another device: no remote copies, remote signals or barrier semaphores. Data moves between devices by JAX's collectives and lax.ppermute only.
A program may use at most 128 MiB of HBM per device.

```python
import jax
import jax.numpy as jnp
from jax import lax

D = 768
HEADS = 12
FF = 3072
SEQ = 197
HEAD_DIM = 64
IMAGES = 64


def raised(entries, rng, source, target, parts, factor):
    def block_of(dim):
        return (jnp.arange(entries.shape[dim]) // (entries.shape[dim] // parts)).reshape((-1,) + (1,) * (entries.ndim - 1 - dim))

    one_side = jax.random.permutation(rng, parts)[block_of(target)]
    far = (block_of(target) + parts // 2) % parts
    return jnp.where((block_of(source) == one_side) | (block_of(source) == far), factor * entries, entries)


def shard_levels(rng, shape, cuts, low, largest):
    def one(position, blocks):
        draws = jax.random.uniform(jax.random.fold_in(jax.random.fold_in(rng, 6), position), (blocks,), jnp.float32, low / len(cuts), largest / len(cuts))
        return jnp.repeat(jnp.exp(draws), shape[position] // blocks).reshape((-1,) + (1,) * (len(shape) - position - 1))

    factor_of = one(*cuts[0])
    for cut in cuts[1:]:
        factor_of = factor_of * one(*cut)
    return factor_of


def normal_values(stream_key, shape, deviation, most, cuts=(), dtype=jnp.bfloat16):
    entries = jax.random.normal(stream_key, shape, jnp.float32) * deviation
    if len(cuts) > 0:
        entries = shard_levels(stream_key, shape, cuts, -0.22, 0.18) * entries
    return jnp.clip(entries, min=-most, max=most).astype(dtype)


def heavy_noise(key, dims, spread, bound, cuts, heavy, kind=jnp.bfloat16):
    result = spread * jax.random.normal(key, dims, jnp.float32)
    if cuts:
        result = result * shard_levels(key, dims, cuts, -0.22, 0.18)
    return jnp.clip(raised(result, jax.random.fold_in(key, 3), *heavy), -bound, bound).astype(kind)


def setup_inputs(seed: int = 0) -> dict:
    splits = jax.random.split(jax.random.key(seed), 15)
    patches = normal_values(splits[0], (IMAGES, SEQ, D), 1.0, 6.0, ((0, 8),))
    attn_gain = jnp.clip(1.0 + 0.15 * jax.random.normal(splits[1], (D,), jnp.float32), 0.25, 1.75).astype(jnp.bfloat16)
    attn_shift = normal_values(splits[2], (D,), 0.3, 3.0)
    qkv_weight = normal_values(splits[3], (3, D, D), D ** -0.5, 0.21875, ((1, 8), (2, 4)))
    qv_bias = normal_values(splits[4], (2, D), 0.5, 3.0, ((1, 4),))
    out_weight = normal_values(splits[5], (D, D), (D // 16) ** -0.5, 0.875, ((0, 4), (1, 8)))
    out_bias = normal_values(splits[6], (D,), 0.3, 3.0)
    mlp_gain = jnp.clip(1.0 + 0.15 * jax.random.normal(splits[7], (D,), jnp.float32), 0.25, 1.75).astype(jnp.bfloat16)
    mlp_shift = normal_values(splits[8], (D,), 0.3, 3.0)
    fc1_weight = normal_values(splits[9], (D, FF), D ** -0.5, 0.21875, ((0, 8), (1, 4)))
    fc1_bias = normal_values(splits[10], (FF,), 0.5, 3.0, ((0, 4),))
    fc2_weight = normal_values(splits[11], (FF, D), FF ** -0.5, 0.109375, ((0, 4), (1, 8)))
    fc2_bias = normal_values(splits[12], (D,), 0.3, 3.0)
    cotangent = heavy_noise(splits[13], (IMAGES, SEQ, D), 1.0, 6.0, ((0, 8),), (0, 2, 8, 2.0))
    return {"patches": patches, "attn_gain": attn_gain, "attn_shift": attn_shift, "qkv_weight": qkv_weight, "qv_bias": qv_bias, "out_weight": out_weight, "out_bias": out_bias, "mlp_gain": mlp_gain, "mlp_shift": mlp_shift, "fc1_weight": fc1_weight, "fc1_bias": fc1_bias, "fc2_weight": fc2_weight, "fc2_bias": fc2_bias, "cotangent": cotangent}


EPS = 1e-06

@jax.custom_vjp
def low(v):
    return lax.optimization_barrier(v.astype(jnp.bfloat16)).astype(jnp.float32)

@jax.custom_vjp
def low_back(v):
    return v

def low_keep(v):
    return (low(v), None)

def low_pass(kept, grad):
    return (grad,)

def back_keep(v):
    return (v, None)

def back_low(kept, grad):
    return (low(grad),)
low.defvjp(low_keep, low_pass)
low_back.defvjp(back_keep, back_low)

def layer_norm(values, gain, shift):
    centre = values - lax.optimization_barrier(jnp.mean(values, -1, keepdims=True))
    inverse = lax.rsqrt(lax.optimization_barrier(jnp.mean(centre * centre, -1, keepdims=True)) + EPS)
    return centre * inverse * gain + shift

def matmul(left, right):
    return jnp.einsum('bsd,df->bsf', left, right, precision=lax.Precision.HIGHEST)

def attend_image(pieces):
    query, keyrow, value = pieces
    scores = low_back(jnp.einsum('qhe,khe->hqk', query, keyrow, precision=lax.Precision.HIGHEST) * HEAD_DIM ** (-0.5))
    probs = low(jax.nn.softmax(scores, -1))
    return jnp.einsum('hqk,khe->qhe', probs, value, precision=lax.Precision.HIGHEST)

def forward(patches, attn_gain, attn_shift, qkv_weight, qv_bias, out_weight, out_bias, mlp_gain, mlp_shift, fc1_weight, fc1_bias, fc2_weight, fc2_bias):
    count, length = (patches.shape[0], patches.shape[1])
    norm_one = low(layer_norm(patches, attn_gain, attn_shift))
    query = low(low_back(matmul(norm_one, qkv_weight[0]) + qv_bias[0]))
    keyrow = low(low_back(matmul(norm_one, qkv_weight[1])))
    value = low(low_back(matmul(norm_one, qkv_weight[2]) + qv_bias[1]))
    shape = (count, length, HEADS, HEAD_DIM)
    mixed = lax.map(jax.checkpoint(attend_image), (query.reshape(shape), keyrow.reshape(shape), value.reshape(shape)))
    attended = low(low_back(mixed.reshape(count, length, D)))
    hidden_state = patches + low_back(matmul(attended, out_weight)) + out_bias
    norm_two = low(layer_norm(hidden_state, mlp_gain, mlp_shift))
    pre_act = low_back(matmul(norm_two, fc1_weight) + fc1_bias)
    activated = low(jax.nn.gelu(pre_act, approximate=False))
    return hidden_state + low_back(matmul(activated, fc2_weight)) + fc2_bias

def reference(patches, attn_gain, attn_shift, qkv_weight, qv_bias, out_weight, out_bias, mlp_gain, mlp_shift, fc1_weight, fc1_bias, fc2_weight, fc2_bias, cotangent):
    inputs = [a.astype(jnp.float32) for a in (patches, attn_gain, attn_shift, qkv_weight, qv_bias, out_weight, out_bias, mlp_gain, mlp_shift, fc1_weight, fc1_bias, fc2_weight, fc2_bias)]
    encoded, pullback = jax.vjp(forward, *inputs)
    grads = pullback(cotangent.astype(jnp.float32))
    return (encoded.astype(jnp.bfloat16), grads[0].astype(jnp.bfloat16), grads[1], grads[2], grads[3], grads[4], grads[5], grads[6], grads[7], grads[8], grads[9], grads[10], grads[11], grads[12])
```

```python
from functools import partial

import jax
import jax.numpy as jnp
from jax import lax
from jax.sharding import PartitionSpec as P

HEAD_DIM = 64
EPS = 1e-06
AXES = ("dp", "tensor")
bf16 = jnp.bfloat16
f32 = jnp.float32


def layer_norm(values, gain, shift):
    centre = values - jnp.mean(values, -1, keepdims=True)
    inverse = lax.rsqrt(jnp.mean(centre * centre, -1, keepdims=True) + EPS)
    normed = centre * inverse
    return (normed * gain + shift, normed, inverse)


def row_total(values):
    return jnp.sum(values.reshape(-1, values.shape[-1]), 0)


def norm_back(upstream, normed, inverse, gain):
    scaled = upstream * gain
    inner = (
        scaled
        - jnp.mean(scaled, -1, keepdims=True)
        - normed * jnp.mean(scaled * normed, -1, keepdims=True)
    )
    return (inverse * inner, row_total(upstream * normed), row_total(upstream))


def dot(spec, left, right):
    return jnp.einsum(spec, left, right, preferred_element_type=f32)


def gather_weight(piece, n_dp, n_t):
    whole = lax.all_gather(piece, AXES, axis=0, tiled=False)
    whole = whole.reshape(n_dp, n_t, piece.shape[0], piece.shape[1]).transpose(1, 0, 2, 3)
    return whole.reshape(n_t, n_dp * piece.shape[0], piece.shape[1])


def scatter_grad(part, n_dp, n_t):
    rows = part.shape[1] // n_dp
    part = part.astype(bf16).reshape(n_t, n_dp, rows, part.shape[2]).transpose(1, 0, 2, 3)
    part = part.reshape(n_dp * n_t * rows, part.shape[3])
    return lax.psum_scatter(part, AXES, scatter_dimension=0, tiled=True).astype(f32)


def on_device(
    n_dp,
    n_t,
    patches,
    attn_gain,
    attn_shift,
    qkv_weight,
    qv_bias,
    out_weight,
    out_bias,
    mlp_gain,
    mlp_shift,
    fc1_weight,
    fc1_bias,
    fc2_weight,
    fc2_bias,
    cotangent,
):
    factor = HEAD_DIM ** (-0.5)
    t_me = lax.axis_index("tensor")
    width = qkv_weight.shape[2]
    heads = width // HEAD_DIM
    rows = qkv_weight.shape[1]
    attn_piece = jnp.concatenate(
        (qkv_weight[0], qkv_weight[1], qkv_weight[2], out_weight.T), axis=1
    )
    w_attn = gather_weight(attn_piece, n_dp, n_t)
    w_fc1 = gather_weight(fc1_weight, n_dp, n_t)
    w_fc2 = gather_weight(fc2_weight.T, n_dp, n_t)
    biases = lax.all_gather(
        jnp.concatenate((qv_bias.reshape(-1), fc1_bias)), "tensor", axis=0, tiled=False
    ).astype(f32)
    q_bias = biases[:, :width]
    v_bias = biases[:, width : 2 * width]
    f_bias = biases[:, 2 * width :]

    count = patches.shape[0] // n_t
    length = patches.shape[1]
    mine = lax.dynamic_slice_in_dim(patches, t_me * count, count, 0)
    cot = lax.dynamic_slice_in_dim(cotangent, t_me * count, count, 0)
    inputs = mine.astype(f32)
    gain_one = attn_gain.astype(f32)
    gain_two = mlp_gain.astype(f32)
    norm_one, normed_one, inverse_one = layer_norm(inputs, gain_one, attn_shift.astype(f32))
    norm_one_low = norm_one.astype(bf16)
    projected = dot("bsd,tde->tbse", norm_one_low, w_attn[:, :, : 3 * width])

    def heads_of(values):
        return values.reshape(n_t, count, length, heads, HEAD_DIM)

    query = heads_of((projected[..., :width] + q_bias[:, None, None, :]).astype(bf16))
    key = heads_of(projected[..., width : 2 * width].astype(bf16))
    value = heads_of((projected[..., 2 * width :] + v_bias[:, None, None, :]).astype(bf16))
    scores = dot("tbqhe,tbkhe->tbhqk", query, key) * factor
    lse = jax.nn.logsumexp(scores, -1, keepdims=True)
    probs = jnp.exp(scores - lse)
    mixed = dot("tbhqk,tbkhe->tbqhe", probs.astype(bf16), value)
    attended = mixed.reshape(n_t, count, length, width).astype(bf16)
    attn_full = dot("tbse,tde->bsd", attended, w_attn[:, :, 3 * width :])
    hidden_state = inputs + attn_full + out_bias.astype(f32)
    norm_two, normed_two, inverse_two = layer_norm(hidden_state, gain_two, mlp_shift.astype(f32))
    norm_two_low = norm_two.astype(bf16)
    pre_act = dot("bsd,tdf->tbsf", norm_two_low, w_fc1) + f_bias[:, None, None, :]
    activated, gelu_pull = jax.vjp(partial(jax.nn.gelu, approximate=False), pre_act)
    act_low = activated.astype(bf16)
    upstream = cot.astype(f32)
    fc2_grad = scatter_grad(dot("bsd,tbsf->tdf", cot, act_low), n_dp, n_t)
    dact = dot("bsd,tdf->tbsf", cot, w_fc2)
    dpre_low = gelu_pull(dact)[0].astype(bf16)
    fc1_grad = scatter_grad(dot("bsd,tbsf->tdf", norm_two_low, dpre_low), n_dp, n_t)
    dnorm_two = dot("tbsf,tdf->bsd", dpre_low, w_fc1)
    mlp_full = dot("tbsf,tdf->bsd", act_low, w_fc2)
    encoded_mine = (hidden_state + mlp_full + fc2_bias.astype(f32)).astype(bf16)
    encoded = lax.all_gather(encoded_mine, "tensor", axis=0, tiled=True)
    dhidden_norm, gain_two_part, shift_two_part = norm_back(
        dnorm_two, normed_two, inverse_two, gain_two
    )
    dhidden = upstream + dhidden_norm
    dhidden_low = dhidden.astype(bf16)
    out_grad_part = dot("bsd,tbse->tde", dhidden_low, attended)
    dattended = heads_of(dot("bsd,tde->tbse", dhidden_low, w_attn[:, :, 3 * width :]).astype(bf16))
    dvalue = dot("tbhqk,tbqhe->tbkhe", probs.astype(bf16), dattended)
    dprobs = dot("tbqhe,tbkhe->tbhqk", dattended, value)
    dscores = (probs * (dprobs - jnp.sum(dprobs * probs, -1, keepdims=True))).astype(bf16)
    dquery = dot("tbhqk,tbkhe->tbqhe", dscores, key) * factor
    dkey = dot("tbhqk,tbqhe->tbkhe", dscores, query) * factor
    shape = (n_t, count, length, width)
    dqkv = jnp.concatenate(
        (dquery.reshape(shape), dkey.reshape(shape), dvalue.reshape(shape)), -1
    ).astype(bf16)
    qkv_grad_part = dot("bsd,tbse->tde", norm_one_low, dqkv)
    attn_grad = scatter_grad(jnp.concatenate((qkv_grad_part, out_grad_part), -1), n_dp, n_t)
    dnorm_one = dot("tbse,tde->bsd", dqkv, w_attn[:, :, : 3 * width])
    dinput_norm, gain_one_part, shift_one_part = norm_back(
        dnorm_one, normed_one, inverse_one, gain_one
    )
    patch_mine = (dhidden + dinput_norm).astype(bf16)
    patch_grad = lax.all_gather(patch_mine, "tensor", axis=0, tiled=True)
    d_sums = jnp.sum(dqkv.astype(f32), (1, 2))
    small = jnp.concatenate(
        (
            gain_one_part,
            shift_one_part,
            row_total(dhidden),
            gain_two_part,
            shift_two_part,
            row_total(upstream),
            d_sums[:, :width].reshape(-1),
            d_sums[:, 2 * width :].reshape(-1),
            jnp.sum(dpre_low.astype(f32), (1, 2)).reshape(-1),
        )
    )
    small = lax.psum(small, AXES)
    d = gain_one.shape[0]
    cuts = [small[i * d : (i + 1) * d] for i in range(6)]
    at = 6 * d
    q_sum = lax.dynamic_slice_in_dim(small[at : at + n_t * width], t_me * width, width, 0)
    at += n_t * width
    v_sum = lax.dynamic_slice_in_dim(small[at : at + n_t * width], t_me * width, width, 0)
    at += n_t * width
    f_width = fc1_weight.shape[1]
    f_sum = lax.dynamic_slice_in_dim(small[at:], t_me * f_width, f_width, 0)
    return (
        encoded,
        patch_grad,
        cuts[0],
        cuts[1],
        jnp.stack([attn_grad[:, i * width : (i + 1) * width] for i in range(3)]),
        jnp.stack((q_sum, v_sum)),
        attn_grad[:, 3 * width :].T,
        cuts[2],
        cuts[3],
        cuts[4],
        fc1_grad,
        f_sum,
        fc2_grad.T,
        cuts[5],
    )


def solution(mesh):
    return jax.shard_map(
        partial(on_device, mesh.shape["dp"], mesh.shape["tensor"]),
        mesh=mesh,
        in_specs=(
            P("dp", None, None),
            P(),
            P(),
            P(None, "dp", "tensor"),
            P(None, "tensor"),
            P("tensor", "dp"),
            P(),
            P(),
            P(),
            P("dp", "tensor"),
            P("tensor"),
            P("tensor", "dp"),
            P(),
            P("dp", None, None),
        ),
        out_specs=(
            P("dp", None, None),
            P("dp", None, None),
            P(),
            P(),
            P(None, "dp", "tensor"),
            P(None, "tensor"),
            P("tensor", "dp"),
            P(),
            P(),
            P(),
            P("dp", "tensor"),
            P("tensor"),
            P("tensor", "dp"),
            P(),
        ),
        check_vma=False,
    )
```

```python
from functools import partial

import jax
import jax.numpy as jnp
from jax import lax
from jax.experimental import pallas as pl
from jax.experimental.pallas import tpu as pltpu
from jax.sharding import PartitionSpec as P

HEAD_DIM = 64
EPS = 1e-06
AXES = ("dp", "tensor")
bf16 = jnp.bfloat16
f32 = jnp.float32


def layer_norm(values, gain, shift):
    centre = values - jnp.mean(values, -1, keepdims=True)
    inverse = lax.rsqrt(jnp.mean(centre * centre, -1, keepdims=True) + EPS)
    normed = centre * inverse
    return (normed * gain + shift, normed, inverse)


def row_total(values):
    return jnp.sum(values.reshape(-1, values.shape[-1]), 0)


def norm_back(upstream, normed, inverse, gain):
    scaled = upstream * gain
    inner = (
        scaled
        - jnp.mean(scaled, -1, keepdims=True)
        - normed * jnp.mean(scaled * normed, -1, keepdims=True)
    )
    return (inverse * inner, row_total(upstream * normed), row_total(upstream))


def dot(spec, left, right):
    return jnp.einsum(spec, left, right, preferred_element_type=f32)


PARTS = 3
TILE = 16


class Cube:
    def __init__(self, n_dp, n_t, rows):
        self.n_dp, self.n_t, self.rows = n_dp, n_t, rows
        self.n = n_dp * n_t
        bits = [1 << i for i in range(self.n.bit_length() - 1)]
        self.fast = (1 << len(bits)) == self.n and len(bits) >= 4 and rows % (PARTS * TILE) == 0
        spin = bits[1:4]
        self.far = bits[4:]
        self.orders = [spin[p:] + spin[:p] for p in range(PARTS)]
        self.step = rows // PARTS

    def swap(self, value, mask):
        return lax.ppermute(value, AXES, [(i, i ^ mask) for i in range(self.n)])

    def place(self, part, index):
        masks = [1 << i for i in range(1, self.n.bit_length() - 1) if (1 << i) >= 16]
        masks = masks + self.orders[part][::-1]
        out = index * 0
        for k, mask in enumerate(masks):
            out = out | (((index // mask) % 2) << k)
        return out


def copy_call(body, inputs, out_shapes, n_copies, index):
    def kernel(index_ref, *refs):
        sems = refs[-1]
        copies = []
        for src, dst in body(index_ref, refs[: len(inputs)], refs[len(inputs) : -1]):
            copies.append(pltpu.make_async_copy(src, dst, sems.at[len(copies)]))
        for copy in copies:
            copy.start()
        for copy in copies:
            copy.wait()

    moved = sum(x.size * x.dtype.itemsize for x in inputs)
    return pl.pallas_call(
        kernel,
        out_shape=out_shapes,
        in_specs=[pl.BlockSpec(memory_space=pltpu.SMEM)]
        + [pl.BlockSpec(memory_space=pl.ANY)] * len(inputs),
        out_specs=jax.tree.map(lambda _: pl.BlockSpec(memory_space=pl.ANY), out_shapes),
        scratch_shapes=[pltpu.SemaphoreType.DMA((n_copies,))],
        cost_estimate=pl.CostEstimate(flops=0, bytes_accessed=2 * moved, transcendentals=0),
    )(index, *inputs)


def gather_weight(cube, piece):
    rows, cols = piece.shape
    n_dp, n_t = cube.n_dp, cube.n_t
    if not cube.fast:
        whole = lax.all_gather(piece, AXES, axis=0, tiled=False)
        whole = whole.reshape(n_dp, n_t, rows, cols).transpose(1, 0, 2, 3)
        whole = whole.reshape(n_t, n_dp * rows, cols)
        return jnp.take(whole, lax.axis_index("tensor") ^ jnp.arange(n_t), axis=0)
    have = piece[None]
    for mask in cube.far:
        have = jnp.concatenate((have, cube.swap(have, mask)))
    step = cube.step
    held = [have[:, p * step : (p + 1) * step] for p in range(PARTS)]
    for k in range(3):
        came = [cube.swap(held[p], cube.orders[p][::-1][k]) for p in range(PARTS)]
        held = [jnp.concatenate((held[p], came[p])) for p in range(PARTS)]
    other = [cube.swap(held[p], 1) for p in range(PARTS)]
    dp = lax.axis_index("dp")
    offsets = jnp.stack([cube.place(p, dp * n_t) for p in range(PARTS)]).astype(jnp.int32)

    def body(index_ref, ins, outs):
        for t in range(n_t):
            for d in range(n_dp):
                for p in range(PARTS):
                    at = index_ref[p] ^ cube.place(p, d * n_t + t)
                    src = ins[p + PARTS * (t % 2)].at[at]
                    yield src, outs[0].at[t, pl.ds(d * rows + p * step, step)]

    out = jax.ShapeDtypeStruct((n_t, n_dp * rows, cols), piece.dtype)
    return copy_call(body, held + other, [out], n_dp * n_t * PARTS, offsets)[0]


def scatter_grad(cube, part):
    n_dp, n_t, rows = cube.n_dp, cube.n_t, cube.rows
    cols = part.shape[2]
    part = part.astype(bf16)
    if not cube.fast:
        part = jnp.take(part, lax.axis_index("tensor") ^ jnp.arange(n_t), axis=0)
        part = part.reshape(n_t, n_dp, rows, cols).transpose(1, 0, 2, 3)
        part = part.reshape(n_dp * n_t * rows, cols)
        return lax.psum_scatter(part, AXES, scatter_dimension=0, tiled=True).astype(f32)
    step = cube.step
    dp = lax.axis_index("dp")
    offsets = jnp.stack([cube.place(p, dp * n_t) for p in range(PARTS)]).astype(jnp.int32)

    def body(index_ref, ins, outs):
        for t in range(n_t):
            for d in range(n_dp):
                for p in range(PARTS):
                    at = index_ref[p] ^ cube.place(p, d * n_t + t)
                    dst = outs[p + PARTS * (t % 2)].at[at]
                    yield ins[0].at[t, pl.ds(d * rows + p * step, step)], dst

    half = n_dp * n_t // 2
    out = jax.ShapeDtypeStruct((half, step, cols), bf16)
    blocks = copy_call(body, [part], [out] * (2 * PARTS), n_dp * n_t * PARTS, offsets)
    terms = [[blocks[p], cube.swap(blocks[p + PARTS], 1)] for p in range(PARTS)]

    def total(values):
        value = values[0].astype(f32)
        for more in values[1:]:
            value = value + more.astype(f32)
        return value

    size = half
    for k in range(3):
        size //= 2
        came = [
            cube.swap(total([v[size : 2 * size] for v in terms[p]]).astype(bf16), cube.orders[p][k])
            for p in range(PARTS)
        ]
        terms = [[v[:size] for v in terms[p]] + [came[p]] for p in range(PARTS)]
    joined = [jnp.concatenate(vs, axis=1) for vs in zip(*terms)]
    for mask in cube.far[::-1]:
        size //= 2
        came = cube.swap(total([v[size : 2 * size] for v in joined]).astype(bf16), mask)
        joined = [v[:size] for v in joined] + [came]
    return total(joined)[0]


def sum_all(cube, value):
    if not cube.fast:
        return lax.psum(value, AXES)
    for mask in [1] + cube.orders[0] + cube.far:
        value = value + cube.swap(value, mask)
    return value


def gather_images(cube, mine):
    if not cube.fast or cube.n_t != 4:
        return lax.all_gather(mine, "tensor", axis=0, tiled=True)
    count = mine.shape[0]
    there = cube.swap(mine, 2)
    pieces = [mine, cube.swap(mine, 1), there, cube.swap(there, 1)]
    index = lax.axis_index("tensor").astype(jnp.int32).reshape(1)

    def body(index_ref, ins, outs):
        for r in range(4):
            yield ins[r], outs[0].at[pl.ds((index_ref[0] ^ r) * count, count)]

    out = jax.ShapeDtypeStruct((4 * count,) + mine.shape[1:], mine.dtype)
    return copy_call(body, pieces, [out], 4, index)[0]


def on_device(
    n_dp,
    n_t,
    patches,
    attn_gain,
    attn_shift,
    qkv_weight,
    qv_bias,
    out_weight,
    out_bias,
    mlp_gain,
    mlp_shift,
    fc1_weight,
    fc1_bias,
    fc2_weight,
    fc2_bias,
    cotangent,
):
    factor = HEAD_DIM ** (-0.5)
    t_me = lax.axis_index("tensor")
    cube = Cube(n_dp, n_t, qkv_weight.shape[1])
    order = t_me ^ jnp.arange(n_t)
    width = qkv_weight.shape[2]
    heads = width // HEAD_DIM
    attn_piece = jnp.concatenate(
        (qkv_weight[0], qkv_weight[1], qkv_weight[2], out_weight.T), axis=1
    )
    w_attn = gather_weight(cube, attn_piece)
    f_width = fc1_weight.shape[1]
    w_mlp = gather_weight(cube, jnp.concatenate((fc1_weight, fc2_weight.T), axis=1))
    w_fc1, w_fc2 = (w_mlp[..., :f_width], w_mlp[..., f_width:])
    biases = jnp.concatenate((qv_bias.reshape(-1), fc1_bias))[None]
    if cube.fast and n_t == 4:
        biases = jnp.concatenate((biases, cube.swap(biases, 1)))
        biases = jnp.concatenate((biases, cube.swap(biases, 2)))
    else:
        biases = jnp.take(lax.all_gather(biases[0], "tensor", axis=0, tiled=False), order, axis=0)
    biases = biases.astype(f32)
    q_bias = biases[:, :width]
    v_bias = biases[:, width : 2 * width]
    f_bias = biases[:, 2 * width :]

    count = patches.shape[0] // n_t
    length = patches.shape[1]
    mine = lax.dynamic_slice_in_dim(patches, t_me * count, count, 0)
    cot = lax.dynamic_slice_in_dim(cotangent, t_me * count, count, 0)
    inputs = mine.astype(f32)
    gain_one = attn_gain.astype(f32)
    gain_two = mlp_gain.astype(f32)
    norm_one, normed_one, inverse_one = layer_norm(inputs, gain_one, attn_shift.astype(f32))
    norm_one_low = norm_one.astype(bf16)
    projected = dot("bsd,tde->tbse", norm_one_low, w_attn[:, :, : 3 * width])

    def heads_of(values):
        return values.reshape(n_t, count, length, heads, HEAD_DIM)

    query = heads_of((projected[..., :width] + q_bias[:, None, None, :]).astype(bf16))
    key = heads_of(projected[..., width : 2 * width].astype(bf16))
    value = heads_of((projected[..., 2 * width :] + v_bias[:, None, None, :]).astype(bf16))
    scores = dot("tbqhe,tbkhe->tbhqk", query, key) * factor
    lse = jax.nn.logsumexp(scores, -1, keepdims=True)
    probs = jnp.exp(scores - lse)
    mixed = dot("tbhqk,tbkhe->tbqhe", probs.astype(bf16), value)
    attended = mixed.reshape(n_t, count, length, width).astype(bf16)
    attn_full = dot("tbse,tde->bsd", attended, w_attn[:, :, 3 * width :])
    hidden_state = inputs + attn_full + out_bias.astype(f32)
    norm_two, normed_two, inverse_two = layer_norm(hidden_state, gain_two, mlp_shift.astype(f32))
    norm_two_low = norm_two.astype(bf16)
    pre_act = dot("bsd,tdf->tbsf", norm_two_low, w_fc1) + f_bias[:, None, None, :]
    activated, gelu_pull = jax.vjp(partial(jax.nn.gelu, approximate=False), pre_act)
    act_low = activated.astype(bf16)
    upstream = cot.astype(f32)
    fc2_grad_part = dot("bsd,tbsf->tdf", cot, act_low)
    dact = dot("bsd,tdf->tbsf", cot, w_fc2)
    dpre_low = gelu_pull(dact)[0].astype(bf16)
    fc1_grad_part = dot("bsd,tbsf->tdf", norm_two_low, dpre_low)
    mlp_grad = scatter_grad(
        cube, jnp.concatenate((fc1_grad_part.astype(bf16), fc2_grad_part.astype(bf16)), -1)
    )
    dnorm_two = dot("tbsf,tdf->bsd", dpre_low, w_fc1)
    mlp_full = dot("tbsf,tdf->bsd", act_low, w_fc2)
    encoded_mine = (hidden_state + mlp_full + fc2_bias.astype(f32)).astype(bf16)
    encoded = gather_images(cube, encoded_mine)
    dhidden_norm, gain_two_part, shift_two_part = norm_back(
        dnorm_two, normed_two, inverse_two, gain_two
    )
    dhidden = upstream + dhidden_norm
    dhidden_low = dhidden.astype(bf16)
    out_grad_part = dot("bsd,tbse->tde", dhidden_low, attended)
    dattended = heads_of(dot("bsd,tde->tbse", dhidden_low, w_attn[:, :, 3 * width :]).astype(bf16))
    dvalue = dot("tbhqk,tbqhe->tbkhe", probs.astype(bf16), dattended)
    dprobs = dot("tbqhe,tbkhe->tbhqk", dattended, value)
    dscores = (probs * (dprobs - jnp.sum(dprobs * probs, -1, keepdims=True))).astype(bf16)
    dquery = dot("tbhqk,tbkhe->tbqhe", dscores, key) * factor
    dkey = dot("tbhqk,tbqhe->tbkhe", dscores, query) * factor
    shape = (n_t, count, length, width)
    dqkv = jnp.concatenate(
        (dquery.reshape(shape), dkey.reshape(shape), dvalue.reshape(shape)), -1
    ).astype(bf16)
    qkv_grad_part = dot("bsd,tbse->tde", norm_one_low, dqkv)
    attn_grad = scatter_grad(cube, jnp.concatenate((qkv_grad_part, out_grad_part), -1))
    dnorm_one = dot("tbse,tde->bsd", dqkv, w_attn[:, :, : 3 * width])
    dinput_norm, gain_one_part, shift_one_part = norm_back(
        dnorm_one, normed_one, inverse_one, gain_one
    )
    patch_mine = (dhidden + dinput_norm).astype(bf16)
    patch_grad = gather_images(cube, patch_mine)
    d_sums = jnp.sum(dqkv.astype(f32), (1, 2))
    d_sums = jnp.take(d_sums, order, axis=0)
    f_sums = jnp.take(jnp.sum(dpre_low.astype(f32), (1, 2)), order, axis=0)
    small = jnp.concatenate(
        (
            gain_one_part,
            shift_one_part,
            row_total(dhidden),
            gain_two_part,
            shift_two_part,
            row_total(upstream),
            d_sums[:, :width].reshape(-1),
            d_sums[:, 2 * width :].reshape(-1),
            f_sums.reshape(-1),
        )
    )
    small = sum_all(cube, small)
    d = gain_one.shape[0]
    cuts = [small[i * d : (i + 1) * d] for i in range(6)]
    at = 6 * d
    q_sum = lax.dynamic_slice_in_dim(small[at : at + n_t * width], t_me * width, width, 0)
    at += n_t * width
    v_sum = lax.dynamic_slice_in_dim(small[at : at + n_t * width], t_me * width, width, 0)
    at += n_t * width
    f_sum = lax.dynamic_slice_in_dim(small[at:], t_me * f_width, f_width, 0)
    return (
        encoded,
        patch_grad,
        cuts[0],
        cuts[1],
        jnp.stack([attn_grad[:, i * width : (i + 1) * width] for i in range(3)]),
        jnp.stack((q_sum, v_sum)),
        attn_grad[:, 3 * width :].T,
        cuts[2],
        cuts[3],
        cuts[4],
        mlp_grad[:, :f_width],
        f_sum,
        mlp_grad[:, f_width:].T,
        cuts[5],
    )


def solution(mesh):
    return jax.shard_map(
        partial(on_device, mesh.shape["dp"], mesh.shape["tensor"]),
        mesh=mesh,
        in_specs=(
            P("dp", None, None),
            P(),
            P(),
            P(None, "dp", "tensor"),
            P(None, "tensor"),
            P("tensor", "dp"),
            P(),
            P(),
            P(),
            P("dp", "tensor"),
            P("tensor"),
            P("tensor", "dp"),
            P(),
            P("dp", None, None),
        ),
        out_specs=(
            P("dp", None, None),
            P("dp", None, None),
            P(),
            P(),
            P(None, "dp", "tensor"),
            P(None, "tensor"),
            P("tensor", "dp"),
            P(),
            P(),
            P(),
            P("dp", "tensor"),
            P("tensor"),
            P("tensor", "dp"),
            P(),
        ),
        check_vma=False,
    )
```

```python
from functools import partial

import jax
import jax.numpy as jnp
from jax import lax
from jax.experimental import pallas as pl
from jax.experimental.pallas import tpu as pltpu
from jax.sharding import PartitionSpec as P

HEAD_DIM = 64
EPS = 1e-06
AXES = ("dp", "tensor")
bf16 = jnp.bfloat16
f32 = jnp.float32


def layer_norm(values, gain, shift):
    centre = values - jnp.mean(values, -1, keepdims=True)
    inverse = lax.rsqrt(jnp.mean(centre * centre, -1, keepdims=True) + EPS)
    normed = centre * inverse
    return (normed * gain + shift, normed, inverse)


def row_total(values):
    return jnp.sum(values.reshape(-1, values.shape[-1]), 0)


def norm_back(upstream, normed, inverse, gain):
    scaled = upstream * gain
    inner = (
        scaled
        - jnp.mean(scaled, -1, keepdims=True)
        - normed * jnp.mean(scaled * normed, -1, keepdims=True)
    )
    return (inverse * inner, row_total(upstream * normed), row_total(upstream))


def dot(spec, left, right):
    return jnp.einsum(spec, left, right, preferred_element_type=f32)


PARTS = 3
TILE = 16


class Cube:
    def __init__(self, n_dp, n_t, rows):
        self.n_dp, self.n_t, self.rows = n_dp, n_t, rows
        self.n = n_dp * n_t
        bits = [1 << i for i in range(self.n.bit_length() - 1)]
        self.fast = (1 << len(bits)) == self.n and len(bits) >= 4 and rows % (PARTS * TILE) == 0
        spin = bits[1:4]
        self.far = bits[4:]
        self.orders = [spin[p:] + spin[:p] for p in range(PARTS)]
        self.step = rows // PARTS

    def swap(self, value, mask):
        return lax.ppermute(value, AXES, [(i, i ^ mask) for i in range(self.n)])

    def place(self, part, index):
        masks = [1 << i for i in range(1, self.n.bit_length() - 1) if (1 << i) >= 16]
        masks = masks + self.orders[part][::-1]
        out = index * 0
        for k, mask in enumerate(masks):
            out = out | (((index // mask) % 2) << k)
        return out


def copy_call(body, inputs, out_shapes, index):
    def kernel(index_ref, *refs):
        for src, dst, at in body(index_ref, refs[: len(inputs)], refs[len(inputs) :]):
            dst[at] = src

    moved = sum(x.size * x.dtype.itemsize for x in inputs)
    return pl.pallas_call(
        kernel,
        out_shape=out_shapes,
        in_specs=[pl.BlockSpec(memory_space=pltpu.SMEM)]
        + [pl.BlockSpec(memory_space=pltpu.VMEM)] * len(inputs),
        out_specs=jax.tree.map(lambda _: pl.BlockSpec(memory_space=pltpu.VMEM), out_shapes),
        compiler_params=pltpu.CompilerParams(vmem_limit_bytes=48 * 1024 * 1024),
        cost_estimate=pl.CostEstimate(flops=0, bytes_accessed=2 * moved, transcendentals=0),
    )(index, *inputs)


def gather_weight(cube, piece):
    rows, cols = piece.shape
    n_dp, n_t = cube.n_dp, cube.n_t
    if not cube.fast:
        whole = lax.all_gather(piece, AXES, axis=0, tiled=False)
        whole = whole.reshape(n_dp, n_t, rows, cols).transpose(1, 0, 2, 3)
        whole = whole.reshape(n_t, n_dp * rows, cols)
        return jnp.take(whole, lax.axis_index("tensor") ^ jnp.arange(n_t), axis=0)
    have = piece[None]
    for mask in cube.far:
        have = jnp.concatenate((have, cube.swap(have, mask)))
    step = cube.step
    held = [have[:, p * step : (p + 1) * step] for p in range(PARTS)]
    for k in range(3):
        came = [cube.swap(held[p], cube.orders[p][::-1][k]) for p in range(PARTS)]
        held = [jnp.concatenate((held[p], came[p])) for p in range(PARTS)]
    other = [cube.swap(held[p], 1) for p in range(PARTS)]
    dp = lax.axis_index("dp")
    offsets = jnp.stack([cube.place(p, dp * n_t) for p in range(PARTS)]).astype(jnp.int32)

    def body(index_ref, ins, outs):
        for t in range(n_t):
            for d in range(n_dp):
                for p in range(PARTS):
                    at = index_ref[p] ^ cube.place(p, d * n_t + t)
                    src = ins[p + PARTS * (t % 2)][at]
                    yield src, outs[0], (t, pl.ds(d * rows + p * step, step))

    out = jax.ShapeDtypeStruct((n_t, n_dp * rows, cols), piece.dtype)
    return copy_call(body, held + other, [out], offsets)[0]


def scatter_grad(cube, part):
    n_dp, n_t, rows = cube.n_dp, cube.n_t, cube.rows
    cols = part.shape[2]
    part = part.astype(bf16)
    if not cube.fast:
        part = jnp.take(part, lax.axis_index("tensor") ^ jnp.arange(n_t), axis=0)
        part = part.reshape(n_t, n_dp, rows, cols).transpose(1, 0, 2, 3)
        part = part.reshape(n_dp * n_t * rows, cols)
        return lax.psum_scatter(part, AXES, scatter_dimension=0, tiled=True).astype(f32)
    step = cube.step
    dp = lax.axis_index("dp")
    offsets = jnp.stack([cube.place(p, dp * n_t) for p in range(PARTS)]).astype(jnp.int32)

    def body(index_ref, ins, outs):
        for t in range(n_t):
            for d in range(n_dp):
                for p in range(PARTS):
                    at = index_ref[p] ^ cube.place(p, d * n_t + t)
                    src = ins[0][t, pl.ds(d * rows + p * step, step)]
                    yield src, outs[p + PARTS * (t % 2)], (at,)

    half = n_dp * n_t // 2
    out = jax.ShapeDtypeStruct((half, step, cols), bf16)
    blocks = copy_call(body, [part], [out] * (2 * PARTS), offsets)
    terms = [[blocks[p], cube.swap(blocks[p + PARTS], 1)] for p in range(PARTS)]

    def total(values):
        value = values[0].astype(f32)
        for more in values[1:]:
            value = value + more.astype(f32)
        return value

    size = half
    for k in range(3):
        size //= 2
        came = [
            cube.swap(total([v[size : 2 * size] for v in terms[p]]).astype(bf16), cube.orders[p][k])
            for p in range(PARTS)
        ]
        terms = [[v[:size] for v in terms[p]] + [came[p]] for p in range(PARTS)]
    joined = [jnp.concatenate(vs, axis=1) for vs in zip(*terms)]
    for mask in cube.far[::-1]:
        size //= 2
        came = cube.swap(total([v[size : 2 * size] for v in joined]).astype(bf16), mask)
        joined = [v[:size] for v in joined] + [came]
    return total(joined)[0]


def sum_all(cube, value):
    if not cube.fast:
        return lax.psum(value, AXES)
    for mask in [1] + cube.orders[0] + cube.far:
        value = value + cube.swap(value, mask)
    return value


def gather_images(cube, mine):
    if not cube.fast or cube.n_t != 4:
        return lax.all_gather(mine, "tensor", axis=0, tiled=True)
    count = mine.shape[0]
    there = cube.swap(mine, 2)
    pieces = [mine, cube.swap(mine, 1), there, cube.swap(there, 1)]
    index = lax.axis_index("tensor").astype(jnp.int32).reshape(1)

    def body(index_ref, ins, outs):
        for r in range(4):
            for i in range(count):
                yield ins[r][i], outs[0], ((index_ref[0] ^ r) * count + i,)

    out = jax.ShapeDtypeStruct((4 * count,) + mine.shape[1:], mine.dtype)
    return copy_call(body, pieces, [out], index)[0]


def on_device(
    n_dp,
    n_t,
    patches,
    attn_gain,
    attn_shift,
    qkv_weight,
    qv_bias,
    out_weight,
    out_bias,
    mlp_gain,
    mlp_shift,
    fc1_weight,
    fc1_bias,
    fc2_weight,
    fc2_bias,
    cotangent,
):
    factor = HEAD_DIM ** (-0.5)
    t_me = lax.axis_index("tensor")
    cube = Cube(n_dp, n_t, qkv_weight.shape[1])
    order = t_me ^ jnp.arange(n_t)
    width = qkv_weight.shape[2]
    heads = width // HEAD_DIM
    attn_piece = jnp.concatenate(
        (qkv_weight[0], qkv_weight[1], qkv_weight[2], out_weight.T), axis=1
    )
    w_attn = gather_weight(cube, attn_piece)
    f_width = fc1_weight.shape[1]
    w_mlp = gather_weight(cube, jnp.concatenate((fc1_weight, fc2_weight.T), axis=1))
    w_fc1, w_fc2 = (w_mlp[..., :f_width], w_mlp[..., f_width:])
    biases = jnp.concatenate((qv_bias.reshape(-1), fc1_bias))[None]
    if cube.fast and n_t == 4:
        biases = jnp.concatenate((biases, cube.swap(biases, 1)))
        biases = jnp.concatenate((biases, cube.swap(biases, 2)))
    else:
        biases = jnp.take(lax.all_gather(biases[0], "tensor", axis=0, tiled=False), order, axis=0)
    biases = biases.astype(f32)
    q_bias = biases[:, :width]
    v_bias = biases[:, width : 2 * width]
    f_bias = biases[:, 2 * width :]

    count = patches.shape[0] // n_t
    length = patches.shape[1]
    mine = lax.dynamic_slice_in_dim(patches, t_me * count, count, 0)
    cot = lax.dynamic_slice_in_dim(cotangent, t_me * count, count, 0)
    inputs = mine.astype(f32)
    gain_one = attn_gain.astype(f32)
    gain_two = mlp_gain.astype(f32)
    norm_one, normed_one, inverse_one = layer_norm(inputs, gain_one, attn_shift.astype(f32))
    norm_one_low = norm_one.astype(bf16)
    projected = dot("bsd,tde->tbse", norm_one_low, w_attn[:, :, : 3 * width])

    def heads_of(values):
        return values.reshape(n_t, count, length, heads, HEAD_DIM)

    query = heads_of((projected[..., :width] + q_bias[:, None, None, :]).astype(bf16))
    key = heads_of(projected[..., width : 2 * width].astype(bf16))
    value = heads_of((projected[..., 2 * width :] + v_bias[:, None, None, :]).astype(bf16))
    scores = dot("tbqhe,tbkhe->tbhqk", query, key) * factor
    lse = jax.nn.logsumexp(scores, -1, keepdims=True)
    probs = jnp.exp(scores - lse)
    mixed = dot("tbhqk,tbkhe->tbqhe", probs.astype(bf16), value)
    attended = mixed.reshape(n_t, count, length, width).astype(bf16)
    attn_full = dot("tbse,tde->bsd", attended, w_attn[:, :, 3 * width :])
    hidden_state = inputs + attn_full + out_bias.astype(f32)
    norm_two, normed_two, inverse_two = layer_norm(hidden_state, gain_two, mlp_shift.astype(f32))
    norm_two_low = norm_two.astype(bf16)
    pre_act = dot("bsd,tdf->tbsf", norm_two_low, w_fc1) + f_bias[:, None, None, :]
    activated, gelu_pull = jax.vjp(partial(jax.nn.gelu, approximate=False), pre_act)
    act_low = activated.astype(bf16)
    upstream = cot.astype(f32)
    fc2_grad_part = dot("bsd,tbsf->tdf", cot, act_low)
    dact = dot("bsd,tdf->tbsf", cot, w_fc2)
    dpre_low = gelu_pull(dact)[0].astype(bf16)
    fc1_grad_part = dot("bsd,tbsf->tdf", norm_two_low, dpre_low)
    mlp_grad = scatter_grad(
        cube, jnp.concatenate((fc1_grad_part.astype(bf16), fc2_grad_part.astype(bf16)), -1)
    )
    dnorm_two = dot("tbsf,tdf->bsd", dpre_low, w_fc1)
    mlp_full = dot("tbsf,tdf->bsd", act_low, w_fc2)
    encoded_mine = (hidden_state + mlp_full + fc2_bias.astype(f32)).astype(bf16)
    encoded = gather_images(cube, encoded_mine)
    dhidden_norm, gain_two_part, shift_two_part = norm_back(
        dnorm_two, normed_two, inverse_two, gain_two
    )
    dhidden = upstream + dhidden_norm
    dhidden_low = dhidden.astype(bf16)
    out_grad_part = dot("bsd,tbse->tde", dhidden_low, attended)
    dattended = heads_of(dot("bsd,tde->tbse", dhidden_low, w_attn[:, :, 3 * width :]).astype(bf16))
    dvalue = dot("tbhqk,tbqhe->tbkhe", probs.astype(bf16), dattended)
    dprobs = dot("tbqhe,tbkhe->tbhqk", dattended, value)
    dscores = (probs * (dprobs - jnp.sum(dprobs * probs, -1, keepdims=True))).astype(bf16)
    dquery = dot("tbhqk,tbkhe->tbqhe", dscores, key) * factor
    dkey = dot("tbhqk,tbqhe->tbkhe", dscores, query) * factor
    shape = (n_t, count, length, width)
    dqkv = jnp.concatenate(
        (dquery.reshape(shape), dkey.reshape(shape), dvalue.reshape(shape)), -1
    ).astype(bf16)
    qkv_grad_part = dot("bsd,tbse->tde", norm_one_low, dqkv)
    attn_grad = scatter_grad(cube, jnp.concatenate((qkv_grad_part, out_grad_part), -1))
    dnorm_one = dot("tbse,tde->bsd", dqkv, w_attn[:, :, : 3 * width])
    dinput_norm, gain_one_part, shift_one_part = norm_back(
        dnorm_one, normed_one, inverse_one, gain_one
    )
    patch_mine = (dhidden + dinput_norm).astype(bf16)
    patch_grad = gather_images(cube, patch_mine)
    d_sums = jnp.sum(dqkv.astype(f32), (1, 2))
    d_sums = jnp.take(d_sums, order, axis=0)
    f_sums = jnp.take(jnp.sum(dpre_low.astype(f32), (1, 2)), order, axis=0)
    small = jnp.concatenate(
        (
            gain_one_part,
            shift_one_part,
            row_total(dhidden),
            gain_two_part,
            shift_two_part,
            row_total(upstream),
            d_sums[:, :width].reshape(-1),
            d_sums[:, 2 * width :].reshape(-1),
            f_sums.reshape(-1),
        )
    )
    small = sum_all(cube, small)
    d = gain_one.shape[0]
    cuts = [small[i * d : (i + 1) * d] for i in range(6)]
    at = 6 * d
    q_sum = lax.dynamic_slice_in_dim(small[at : at + n_t * width], t_me * width, width, 0)
    at += n_t * width
    v_sum = lax.dynamic_slice_in_dim(small[at : at + n_t * width], t_me * width, width, 0)
    at += n_t * width
    f_sum = lax.dynamic_slice_in_dim(small[at:], t_me * f_width, f_width, 0)
    return (
        encoded,
        patch_grad,
        cuts[0],
        cuts[1],
        jnp.stack([attn_grad[:, i * width : (i + 1) * width] for i in range(3)]),
        jnp.stack((q_sum, v_sum)),
        attn_grad[:, 3 * width :].T,
        cuts[2],
        cuts[3],
        cuts[4],
        mlp_grad[:, :f_width],
        f_sum,
        mlp_grad[:, f_width:].T,
        cuts[5],
    )


def solution(mesh):
    return jax.shard_map(
        partial(on_device, mesh.shape["dp"], mesh.shape["tensor"]),
        mesh=mesh,
        in_specs=(
            P("dp", None, None),
            P(),
            P(),
            P(None, "dp", "tensor"),
            P(None, "tensor"),
            P("tensor", "dp"),
            P(),
            P(),
            P(),
            P("dp", "tensor"),
            P("tensor"),
            P("tensor", "dp"),
            P(),
            P("dp", None, None),
        ),
        out_specs=(
            P("dp", None, None),
            P("dp", None, None),
            P(),
            P(),
            P(None, "dp", "tensor"),
            P(None, "tensor"),
            P("tensor", "dp"),
            P(),
            P(),
            P(),
            P("dp", "tensor"),
            P("tensor"),
            P("tensor", "dp"),
            P(),
        ),
        check_vma=False,
    )
```

```python
from functools import partial

import jax
import jax.numpy as jnp
from jax import lax
from jax.experimental import pallas as pl
from jax.experimental.pallas import tpu as pltpu
from jax.sharding import PartitionSpec as P

HEAD_DIM = 64
EPS = 1e-06
AXES = ("dp", "tensor")
PARTS = 3
TILE = 16
FACTOR = HEAD_DIM ** (-0.5)
bf16 = jnp.bfloat16
f32 = jnp.float32


class Cube:
    def __init__(self, n_dp, n_t, rows):
        self.n_dp, self.n_t, self.rows = n_dp, n_t, rows
        self.n = n_dp * n_t
        n_bits = self.n.bit_length() - 1
        bits = list(range(n_bits))
        self.fast = (1 << n_bits) == self.n and n_t == 4 and n_bits >= 4
        self.fast = self.fast and rows % (PARTS * TILE) == 0
        spin = bits[1:4]
        self.far = bits[4:]
        self.orders = [spin[p:] + spin[:p] for p in range(PARTS)]
        self.step = rows // PARTS

    def swap(self, value, bit):
        return lax.ppermute(value, AXES, [(i, i ^ (1 << bit)) for i in range(self.n)])

    def place(self, part, index):
        out = index * 0
        for k, bit in enumerate(self.far + self.orders[part][::-1]):
            out = out | (((index >> bit) & 1) << k)
        return out

    def offsets(self):
        own = lax.axis_index("dp") * self.n_t
        return jnp.stack([self.place(p, own) for p in range(PARTS)]).astype(jnp.int32)

    def load(self, offset_ref, refs, t, out_ref):
        if not self.fast:
            out_ref[...] = refs[0][t]
            return
        for core in range(2):

            @pl.when((t & 1) == core)
            def _():
                for p in range(PARTS):
                    base = offset_ref[p] ^ self.place(p, t)
                    for d in range(self.n_dp):
                        at = base ^ self.place(p, d * self.n_t)
                        rows = pl.ds(d * self.rows + p * self.step, self.step)
                        out_ref[rows, :] = refs[core * PARTS + p][at]

    def store(self, offset_ref, refs, t, from_ref):
        if not self.fast:
            refs[0][t] = from_ref[...]
            return
        for core in range(2):

            @pl.when((t & 1) == core)
            def _():
                for p in range(PARTS):
                    base = offset_ref[p] ^ self.place(p, t)
                    for d in range(self.n_dp):
                        at = base ^ self.place(p, d * self.n_t)
                        rows = pl.ds(d * self.rows + p * self.step, self.step)
                        refs[core * PARTS + p][at] = from_ref[rows, :]

    def grad_shapes(self, cols):
        if not self.fast:
            return [jax.ShapeDtypeStruct((self.n_t, self.n_dp * self.rows, cols), bf16)]
        return [jax.ShapeDtypeStruct((self.n // 2, self.step, cols), bf16)] * (2 * PARTS)


def tie(*values):
    return lax.optimization_barrier(values)


def total(values):
    value = values[0].astype(f32)
    for more in values[1:]:
        value = value + more.astype(f32)
    return value


def gather_far(cube, piece):
    have = piece[None]
    for bit in cube.far:
        have = jnp.concatenate((have, cube.swap(have, bit)))
    return tuple(have[:, p * cube.step : (p + 1) * cube.step] for p in range(PARTS))


def gather_step(cube, held, k):
    came = [cube.swap(held[p], cube.orders[p][::-1][k]) for p in range(PARTS)]
    return tuple(jnp.concatenate((held[p], came[p])) for p in range(PARTS))


def gather_core(cube, held):
    return list(held) + [cube.swap(h, 0) for h in held]


def gather_plain(cube, piece):
    rows, cols = piece.shape
    whole = lax.all_gather(piece, AXES, axis=0, tiled=False)
    whole = whole.reshape(cube.n_dp, cube.n_t, rows, cols).transpose(1, 0, 2, 3)
    whole = whole.reshape(cube.n_t, cube.n_dp * rows, cols)
    return [jnp.take(whole, lax.axis_index("tensor") ^ jnp.arange(cube.n_t), axis=0)]


def scatter_plain(cube, part):
    n_t, n_dp, rows, cols = cube.n_t, cube.n_dp, cube.rows, part.shape[2]
    part = jnp.take(part, lax.axis_index("tensor") ^ jnp.arange(n_t), axis=0)
    part = part.reshape(n_t, n_dp, rows, cols).transpose(1, 0, 2, 3)
    part = part.reshape(n_dp * n_t * rows, cols)
    return lax.psum_scatter(part, AXES, scatter_dimension=0, tiled=True).astype(f32)


def scatter_core(cube, blocks):
    return [[blocks[p], cube.swap(blocks[p + PARTS], 0)] for p in range(PARTS)]


def scatter_sends(cube, terms):
    size = terms[0][0].shape[0] // 2
    return tuple(total([v[size : 2 * size] for v in ts]).astype(bf16) for ts in terms)


def scatter_step(cube, terms, sends, k):
    came = [cube.swap(sends[p], cube.orders[p][k]) for p in range(PARTS)]
    return [
        [v[: v.shape[0] // 2] for v in (ts if k == 0 else ts)] + [c] for ts, c in zip(terms, came)
    ]


def scatter_far(cube, terms):
    joined = [jnp.concatenate(vs, axis=1) for vs in zip(*terms)]
    for bit in cube.far[::-1]:
        size = joined[0].shape[0] // 2
        came = cube.swap(total([v[size:] for v in joined]).astype(bf16), bit)
        joined = [v[:size] for v in joined] + [came]
    return total(joined)[0]


def sum_all(cube, value):
    if not cube.fast:
        return lax.psum(value, AXES)
    for bit in [0] + cube.orders[0] + cube.far:
        value = value + cube.swap(value, bit)
    return value


def gather_images(cube, mine, length):
    if not cube.fast:
        return lax.all_gather(mine[:, :length], "tensor", axis=0, tiled=True)
    count = mine.shape[0]
    there = cube.swap(mine, 1)
    pieces = [mine, cube.swap(mine, 0), there, cube.swap(there, 0)]
    index = lax.axis_index("tensor").astype(jnp.int32).reshape(1)

    def kernel(index_ref, *refs):
        for r in range(4):
            for i in range(count):
                refs[4][(index_ref[0] ^ r) * count + i] = refs[r][i, :length, :]

    return call(
        kernel,
        jax.ShapeDtypeStruct((4 * count, length, mine.shape[2]), mine.dtype),
        index,
        pieces,
        [],
        0,
    )


def call(kernel, out_shapes, index, inputs, scratch, flops):
    moved = sum(x.size * x.dtype.itemsize for x in inputs)
    moved += sum(x.size * x.dtype.itemsize for x in jax.tree.leaves(out_shapes))
    return pl.pallas_call(
        kernel,
        out_shape=out_shapes,
        in_specs=[pl.BlockSpec(memory_space=pltpu.SMEM)]
        + [pl.BlockSpec(memory_space=pltpu.VMEM)] * len(inputs),
        out_specs=jax.tree.map(lambda _: pl.BlockSpec(memory_space=pltpu.VMEM), out_shapes),
        scratch_shapes=scratch,
        compiler_params=pltpu.CompilerParams(vmem_limit_bytes=56 * 1024 * 1024),
        cost_estimate=pl.CostEstimate(flops=flops, bytes_accessed=moved, transcendentals=0),
    )(index, *inputs)


def nn(left, right):
    return lax.dot_general(left, right, (((1,), (0,)), ((), ())), preferred_element_type=f32)


def nt(left, right):
    return lax.dot_general(left, right, (((1,), (1,)), ((), ())), preferred_element_type=f32)


def tn(left, right):
    return lax.dot_general(left, right, (((0,), (0,)), ((), ())), preferred_element_type=f32)


def normed_of(values):
    centre = values - jnp.mean(values, -1, keepdims=True)
    inverse = lax.rsqrt(jnp.mean(centre * centre, -1, keepdims=True) + EPS)
    return (centre * inverse, inverse)


def norm_back(upstream, normed, inverse, gain):
    scaled = upstream * gain
    inner = (
        scaled
        - jnp.mean(scaled, -1, keepdims=True)
        - normed * jnp.mean(scaled * normed, -1, keepdims=True)
    )
    return inverse * inner


def column_sum(values):
    return jnp.sum(values, 0, keepdims=True)


def attend_kernel(cube, count, length, width, n_w, index_ref, *refs):
    x_ref, vec_ref, bias_ref = refs[:3]
    w_refs = refs[3 : 3 + n_w]
    n1_ref, qkv_ref, att_ref, hidden_ref, n2_ref, w_ref, sum_ref = refs[3 + n_w :]
    x = x_ref[...].astype(f32)
    normed, _ = normed_of(x)
    n1_ref[...] = (normed * vec_ref[0:1] + vec_ref[1:2]).astype(bf16)
    sum_ref[...] = x + vec_ref[2:3]
    tokens = x.shape[0] // count
    heads = width // HEAD_DIM
    keep = lax.broadcasted_iota(jnp.int32, (tokens, tokens), 1) < length

    def step(t, carry):
        cube.load(index_ref, w_refs, t, w_ref)
        qkv = nn(n1_ref[...], w_ref[:, : 3 * width]) + bias_ref[t]
        qkv_ref[t] = qkv.astype(bf16)
        for b in range(count):
            rows = slice(b * tokens, (b + 1) * tokens)
            found = []
            for h in range(heads):
                q = qkv_ref[t, rows, h * HEAD_DIM : (h + 1) * HEAD_DIM]
                k = qkv_ref[t, rows, width + h * HEAD_DIM : width + (h + 1) * HEAD_DIM]
                v = qkv_ref[t, rows, 2 * width + h * HEAD_DIM : 2 * width + (h + 1) * HEAD_DIM]
                scores = jnp.where(keep, nt(q, k) * FACTOR, -1e30)
                weights = jnp.exp(scores - jnp.max(scores, -1, keepdims=True))
                probs = weights * (1.0 / jnp.sum(weights, -1, keepdims=True))
                found.append(nn(probs.astype(bf16), v).astype(bf16))
            att_ref[t, rows, :] = jnp.concatenate(found, axis=1)
        sum_ref[...] += nt(att_ref[t], w_ref[:, 3 * width :])
        return carry

    lax.fori_loop(0, cube.n_t, step, 0)
    hidden = sum_ref[...]
    hidden_ref[...] = hidden
    normed, _ = normed_of(hidden)
    n2_ref[...] = (normed * vec_ref[3:4] + vec_ref[4:5]).astype(bf16)


def mlp_kernel(cube, width, n_w, index_ref, *refs):
    n2_ref, cot_ref, hidden_ref, vec_ref, bias_ref = refs[:5]
    w_refs = refs[5 : 5 + n_w]
    enc_ref, dhidden_ref, small_ref = refs[5 + n_w : 8 + n_w]
    g_refs = refs[8 + n_w : 8 + 2 * n_w]
    w_ref, grad_ref, mlp_ref, dnorm_ref = refs[8 + 2 * n_w :]
    mlp_ref[...] = hidden_ref[...] + vec_ref[5:6]
    dnorm_ref[...] = jnp.zeros_like(dnorm_ref)

    def step(t, carry):
        cube.load(index_ref, w_refs, t, w_ref)
        pre = nn(n2_ref[...], w_ref[:, :width]) + bias_ref[t]
        cdf = 0.5 * (1.0 + lax.erf(pre * (0.5**0.5)))
        slope = cdf + pre * (jnp.exp(-0.5 * pre * pre) * 0.3989422804014327)
        act = (pre * cdf).astype(bf16)
        mlp_ref[...] += nt(act, w_ref[:, width:])
        dpre = (slope * nn(cot_ref[...], w_ref[:, width:])).astype(bf16)
        small_ref[pl.ds(t, 1)] = column_sum(dpre.astype(f32))[None]
        dnorm_ref[...] += nt(dpre, w_ref[:, :width])
        grad_ref[:, :width] = tn(n2_ref[...], dpre).astype(bf16)
        grad_ref[:, width:] = tn(cot_ref[...], act).astype(bf16)
        cube.store(index_ref, g_refs, t, grad_ref)
        return carry

    lax.fori_loop(0, cube.n_t, step, 0)
    enc_ref[...] = mlp_ref[...].astype(bf16)
    normed, inverse = normed_of(hidden_ref[...])
    dnorm = dnorm_ref[...]
    cot = cot_ref[...].astype(f32)
    dhidden = cot + norm_back(dnorm, normed, inverse, vec_ref[3:4])
    dhidden_ref[...] = dhidden
    small_ref[cube.n_t] = column_sum(dnorm * normed)
    small_ref[cube.n_t + 1] = column_sum(dnorm)
    small_ref[cube.n_t + 2] = column_sum(cot)
    small_ref[cube.n_t + 3] = column_sum(dhidden)


def attend_back_kernel(cube, count, length, width, n_w, index_ref, *refs):
    x_ref, n1_ref, qkv_ref, att_ref, dhidden_ref, vec_ref = refs[:6]
    w_refs = refs[6 : 6 + n_w]
    patch_ref, small_ref, dbias_ref = refs[6 + n_w : 9 + n_w]
    g_refs = refs[9 + n_w : 9 + 2 * n_w]
    w_ref, grad_ref, dnorm_ref, low_ref, dqkv_ref = refs[9 + 2 * n_w :]
    low_ref[...] = dhidden_ref[...].astype(bf16)
    dnorm_ref[...] = jnp.zeros_like(dnorm_ref)
    tokens = x_ref.shape[0] // count
    heads = width // HEAD_DIM
    keep = lax.broadcasted_iota(jnp.int32, (tokens, tokens), 0) < length

    def step(t, carry):
        cube.load(index_ref, w_refs, t, w_ref)
        datt = nn(low_ref[...], w_ref[:, 3 * width :]).astype(bf16)
        grad_ref[:, 3 * width :] = tn(low_ref[...], att_ref[t]).astype(bf16)
        for b in range(count):
            rows = slice(b * tokens, (b + 1) * tokens)
            dqs, dks, dvs = [], [], []
            for h in range(heads):
                q = qkv_ref[t, rows, h * HEAD_DIM : (h + 1) * HEAD_DIM]
                k = qkv_ref[t, rows, width + h * HEAD_DIM : width + (h + 1) * HEAD_DIM]
                v = qkv_ref[t, rows, 2 * width + h * HEAD_DIM : 2 * width + (h + 1) * HEAD_DIM]
                do = datt[rows, h * HEAD_DIM : (h + 1) * HEAD_DIM]
                scores = jnp.where(keep, nt(k, q) * FACTOR, -1e30)
                weights = jnp.exp(scores - jnp.max(scores, 0, keepdims=True))
                probs = weights * (1.0 / jnp.sum(weights, 0, keepdims=True))
                dvs.append(nn(probs.astype(bf16), do))
                dprobs = nt(v, do)
                inner = jnp.sum(dprobs * probs, 0, keepdims=True)
                dscores = (probs * (dprobs - inner)).astype(bf16)
                dks.append(nn(dscores, q) * FACTOR)
                dqs.append(tn(dscores, k) * FACTOR)
            dqkv_ref[rows, :] = jnp.concatenate(dqs + dks + dvs, axis=1).astype(bf16)
        dqkv = dqkv_ref[...]
        dbias_ref[pl.ds(t, 1)] = column_sum(dqkv.astype(f32))[None]
        dnorm_ref[...] += nt(dqkv, w_ref[:, : 3 * width])
        grad_ref[:, : 3 * width] = tn(n1_ref[...], dqkv).astype(bf16)
        cube.store(index_ref, g_refs, t, grad_ref)
        return carry

    lax.fori_loop(0, cube.n_t, step, 0)
    normed, inverse = normed_of(x_ref[...].astype(f32))
    dnorm = dnorm_ref[...]
    patch = dhidden_ref[...] + norm_back(dnorm, normed, inverse, vec_ref[0:1])
    patch_ref[...] = patch.astype(bf16)
    small_ref[0] = column_sum(dnorm * normed)
    small_ref[1] = column_sum(dnorm)


def on_device(
    n_dp,
    n_t,
    patches,
    attn_gain,
    attn_shift,
    qkv_weight,
    qv_bias,
    out_weight,
    out_bias,
    mlp_gain,
    mlp_shift,
    fc1_weight,
    fc1_bias,
    fc2_weight,
    fc2_bias,
    cotangent,
):
    t_me = lax.axis_index("tensor")
    cube = Cube(n_dp, n_t, qkv_weight.shape[1])
    order = t_me ^ jnp.arange(n_t)
    width = qkv_weight.shape[2]
    f_width = fc1_weight.shape[1]
    d = patches.shape[2]
    attn_piece = jnp.concatenate(
        (qkv_weight[0], qkv_weight[1], qkv_weight[2], out_weight.T), axis=1
    )
    mlp_piece = jnp.concatenate((fc1_weight, fc2_weight.T), axis=1)
    index = cube.offsets()
    biases = jnp.concatenate((qv_bias.reshape(-1), fc1_bias))[None]
    if cube.fast:
        held = gather_far(cube, attn_piece)
        held_mlp = gather_far(cube, mlp_piece)
        biases = jnp.concatenate((biases, cube.swap(biases, 0)))
        biases = jnp.concatenate((biases, cube.swap(biases, 1)))
        held = gather_step(cube, held, 0)
        held, held_mlp = tie(held, held_mlp)
        held = gather_step(cube, held, 1)
        held_mlp = gather_step(cube, held_mlp, 0)
        held, held_mlp = tie(held, held_mlp)
        held = gather_step(cube, held, 2)
        held_mlp = gather_step(cube, held_mlp, 1)
        w_attn = gather_core(cube, held)
        w_attn, held_mlp = tie(tuple(w_attn), held_mlp)
        held_mlp = gather_step(cube, held_mlp, 2)
        w_mlp = gather_core(cube, held_mlp)
    else:
        w_attn = gather_plain(cube, attn_piece)
        w_mlp = gather_plain(cube, mlp_piece)
        biases = jnp.take(lax.all_gather(biases[0], "tensor", axis=0, tiled=False), order, axis=0)
    n_w = len(w_attn)
    biases = biases.astype(f32)
    qkv_bias = jnp.concatenate(
        (biases[:, :width], jnp.zeros((n_t, width), f32), biases[:, width : 2 * width]), axis=1
    )[:, None]
    f_bias = biases[:, None, 2 * width :]
    vecs = jnp.stack((attn_gain, attn_shift, out_bias, mlp_gain, mlp_shift, fc2_bias)).astype(f32)

    count = patches.shape[0] // n_t
    length = patches.shape[1]
    padded = -(-length // TILE) * TILE
    tokens = count * padded

    def own_images(values):
        mine = lax.dynamic_slice_in_dim(values, t_me * count, count, 0)
        return jnp.pad(mine, ((0, 0), (0, padded - length), (0, 0))).reshape(tokens, d)

    x = own_images(patches)
    cot = own_images(cotangent)
    spots = 2 * tokens * d * n_t
    attn_macs = spots * 4 * width // 2 + 4 * count * n_t * padded * padded * width

    def shape(*dims, dtype=bf16):
        return jax.ShapeDtypeStruct(dims, dtype)

    n1, qkv, att, hidden, n2 = call(
        partial(attend_kernel, cube, count, length, width, n_w),
        [
            shape(tokens, d),
            shape(n_t, tokens, 3 * width),
            shape(n_t, tokens, width),
            shape(tokens, d, dtype=f32),
            shape(tokens, d),
        ],
        index,
        [x, vecs, qkv_bias, *w_attn],
        [pltpu.VMEM((d, 4 * width), bf16), pltpu.VMEM((tokens, d), f32)],
        2 * attn_macs,
    )
    enc, dhidden, mlp_small, *mlp_grads = call(
        partial(mlp_kernel, cube, f_width, n_w),
        [
            shape(tokens, d),
            shape(tokens, d, dtype=f32),
            shape(n_t + 4, 1, d, dtype=f32),
            *cube.grad_shapes(2 * f_width),
        ],
        index,
        [n2, cot, hidden, vecs, f_bias, *w_mlp],
        [pltpu.VMEM((d, 2 * f_width), bf16)] * 2 + [pltpu.VMEM((tokens, d), f32)] * 2,
        6 * spots * f_width,
    )
    if cube.fast:
        mlp_terms = scatter_core(cube, mlp_grads)
        sends = scatter_sends(cube, mlp_terms)
        sends, dhidden, att = tie(sends, dhidden, att)
        mlp_terms = scatter_step(cube, mlp_terms, sends, 0)
    patch, attn_small, dbias, *attn_grads = call(
        partial(attend_back_kernel, cube, count, length, width, n_w),
        [
            shape(tokens, d),
            shape(2, 1, d, dtype=f32),
            shape(n_t, 1, 3 * width, dtype=f32),
            *cube.grad_shapes(4 * width),
        ],
        index,
        [x, n1, qkv, att, dhidden, vecs, *w_attn],
        [
            pltpu.VMEM((d, 4 * width), bf16),
            pltpu.VMEM((d, 4 * width), bf16),
            pltpu.VMEM((tokens, d), f32),
            pltpu.VMEM((tokens, d), bf16),
            pltpu.VMEM((tokens, 3 * width), bf16),
        ],
        4 * attn_macs,
    )
    encoded = gather_images(cube, enc.reshape(count, padded, d), length)
    patch_grad = gather_images(cube, patch.reshape(count, padded, d), length)
    if cube.fast:
        attn_terms = scatter_core(cube, attn_grads)
        for k in range(3):
            sends = scatter_sends(cube, attn_terms)
            attn_terms = scatter_step(cube, attn_terms, sends, k)
            if k > 0:
                sends = scatter_sends(cube, mlp_terms)
                mlp_terms = scatter_step(cube, mlp_terms, sends, k)
        mlp_grad = scatter_far(cube, mlp_terms)
        attn_grad = scatter_far(cube, attn_terms)
    else:
        mlp_grad = scatter_plain(cube, mlp_grads[0])
        attn_grad = scatter_plain(cube, attn_grads[0])
    dbias = jnp.take(dbias[:, 0], order, axis=0)
    f_sums = jnp.take(mlp_small[:n_t, 0], order, axis=0)
    small = jnp.concatenate(
        (
            attn_small.reshape(-1),
            mlp_small[n_t:].reshape(-1),
            dbias[:, :width].reshape(-1),
            dbias[:, 2 * width :].reshape(-1),
            f_sums.reshape(-1),
        )
    )
    small = sum_all(cube, small)
    cuts = [small[i * d : (i + 1) * d] for i in range(6)]
    at = 6 * d
    q_sum = lax.dynamic_slice_in_dim(small[at : at + n_t * width], t_me * width, width, 0)
    at += n_t * width
    v_sum = lax.dynamic_slice_in_dim(small[at : at + n_t * width], t_me * width, width, 0)
    at += n_t * width
    f_sum = lax.dynamic_slice_in_dim(small[at:], t_me * f_width, f_width, 0)
    return (
        encoded,
        patch_grad,
        cuts[0],
        cuts[1],
        jnp.stack([attn_grad[:, i * width : (i + 1) * width] for i in range(3)]),
        jnp.stack((q_sum, v_sum)),
        attn_grad[:, 3 * width :].T,
        cuts[5],
        cuts[2],
        cuts[3],
        mlp_grad[:, :f_width],
        f_sum,
        mlp_grad[:, f_width:].T,
        cuts[4],
    )


def solution(mesh):
    return jax.shard_map(
        partial(on_device, mesh.shape["dp"], mesh.shape["tensor"]),
        mesh=mesh,
        in_specs=(
            P("dp", None, None),
            P(),
            P(),
            P(None, "dp", "tensor"),
            P(None, "tensor"),
            P("tensor", "dp"),
            P(),
            P(),
            P(),
            P("dp", "tensor"),
            P("tensor"),
            P("tensor", "dp"),
            P(),
            P("dp", None, None),
        ),
        out_specs=(
            P("dp", None, None),
            P("dp", None, None),
            P(),
            P(),
            P(None, "dp", "tensor"),
            P(None, "tensor"),
            P("tensor", "dp"),
            P(),
            P(),
            P(),
            P("dp", "tensor"),
            P("tensor"),
            P("tensor", "dp"),
            P(),
        ),
        check_vma=False,
    )
```

```python
from functools import partial

import jax
import jax.numpy as jnp
from jax import lax
from jax.experimental import pallas as pl
from jax.experimental.pallas import tpu as pltpu
from jax.sharding import PartitionSpec as P

HEAD_DIM = 64
EPS = 1e-06
AXES = ("dp", "tensor")
TILE = 16
FACTOR = HEAD_DIM ** (-0.5)
bf16 = jnp.bfloat16
f32 = jnp.float32


class Cube:
    def __init__(self, n_dp, n_t, rows):
        self.n_dp, self.n_t, self.rows = n_dp, n_t, rows
        self.n = n_dp * n_t
        n_bits = self.n.bit_length() - 1
        self.fast = (1 << n_bits) == self.n and n_bits >= 4 and rows % TILE == 0
        far = list(range(n_bits - 1, 3, -1))
        self.orders = ([2, 1, 3] + far, [1, 3, 2] + far)
        self.steps = len(self.orders[0])
        self.half = self.n // 2

    def swap(self, value, k):
        return lax.ppermute(
            value, AXES, [(i, i ^ (1 << self.orders[i & 1][k])) for i in range(self.n)]
        )

    def flip(self, value, bit):
        return lax.ppermute(value, AXES, [(i, i ^ (1 << bit)) for i in range(self.n)])

    def table(self):
        if not self.fast:
            return jnp.zeros((1,), jnp.int32)
        rows = lax.axis_index("dp") ^ jnp.arange(self.n_dp)
        core = lax.axis_index("tensor") & 1
        relative = (rows[None, :] << 2) | (jnp.arange(2)[:, None] << 1)
        found = []
        for order in self.orders:
            place = relative * 0
            for k, bit in enumerate(order[::-1]):
                place = place | (((relative >> bit) & 1) << k)
            found.append(place)
        both = jnp.where(core == 0, jnp.stack(found), jnp.stack(found[::-1]))
        return both.reshape(-1).astype(jnp.int32)

    def at(self, table_ref, core, y, block):
        return table_ref[(core * 2 + y) * self.n_dp + block]

    def buffers(self, cols):
        blocks = (self.half, self.rows, cols) if self.fast else (1, 8, 128)
        shard = pltpu.VMEM((self.n_dp * self.rows, cols), bf16)
        return [pltpu.VMEM(blocks, bf16), shard, pltpu.SemaphoreType.DMA((2,))]

    def fetch(self, refs, scratch):
        if not self.fast:
            return lambda: None
        held, _, sems = scratch
        part = self.half // 2
        copies = [
            pltpu.make_async_copy(refs[i], held.at[pl.ds(i * part, part)], sems.at[i])
            for i in range(2)
        ]
        for copy in copies:
            copy.start()

        def wait():
            for copy in copies:
                copy.wait()

        return wait

    def load(self, table_ref, refs, scratch, core, y):
        held, shard, sems = scratch
        if not self.fast:
            copy = pltpu.make_async_copy(refs[0].at[2 * y + core], shard, sems.at[0])
            copy.start()
            copy.wait()
            return
        for d in range(self.n_dp):
            shard[d * self.rows : (d + 1) * self.rows, :] = held[self.at(table_ref, core, y, d)]

    def store(self, table_ref, ref, core, y, value):
        if not self.fast:
            ref[y] = value
            return
        for d in range(self.n_dp):
            rows = value[d * self.rows : (d + 1) * self.rows]
            ref[self.at(table_ref, core, y, d)] = rows

    def grad_shape(self, cols):
        if not self.fast:
            return jax.ShapeDtypeStruct((2, self.n_dp * self.rows, cols), bf16)
        return jax.ShapeDtypeStruct((self.half, self.rows, cols), bf16)

    def of_core(self, buffers, core):
        return buffers[2 * core : 2 * core + 2] if self.fast else buffers


def gather_plain(cube, piece):
    rows, cols = piece.shape
    whole = lax.all_gather(piece, AXES, axis=0, tiled=False)
    whole = whole.reshape(cube.n_dp, cube.n_t, rows, cols).transpose(1, 0, 2, 3)
    whole = whole.reshape(cube.n_t, cube.n_dp * rows, cols)
    return [jnp.take(whole, lax.axis_index("tensor") ^ jnp.arange(cube.n_t), axis=0)]


def scatter_plain(cube, own, other):
    n_t, n_dp, rows, cols = cube.n_t, cube.n_dp, cube.rows, own.shape[2]
    part = jnp.stack((own, other), axis=1).reshape(n_t, n_dp * rows, cols)
    part = jnp.take(part, lax.axis_index("tensor") ^ jnp.arange(n_t), axis=0)
    part = part.reshape(n_t, n_dp, rows, cols).transpose(1, 0, 2, 3)
    part = part.reshape(n_dp * n_t * rows, cols)
    return lax.psum_scatter(part, AXES, scatter_dimension=0, tiled=True).astype(f32)


def join(pairs, after=()):
    def kernel(*refs):
        outs = refs[2 * len(pairs) + len(after) :]
        for i, out in enumerate(outs):
            size = pairs[i][0].shape[0]
            out[:size] = refs[2 * i][...]
            out[size:] = refs[2 * i + 1][...]

    shapes = [
        jax.ShapeDtypeStruct((2 * p[0].shape[0],) + p[0].shape[1:], p[0].dtype) for p in pairs
    ]
    return plain_call(kernel, shapes, [x for p in pairs for x in p], None, after)


def sends(groups, after=()):
    sizes = [min(v.shape[0] for v in g) // 2 for g in groups]
    specs, shapes = [], []
    for g, size in zip(groups, sizes):
        block = (size,) + g[0].shape[1:]
        specs += [pl.BlockSpec(block, lambda i: (1, 0, 0)) for _ in g]
        shapes.append(jax.ShapeDtypeStruct(block, bf16))

    def kernel(*refs):
        outs = refs[-len(groups) :]
        start = 0
        for g, out in zip(groups, outs):
            value = refs[start][...].astype(f32)
            for ref in refs[start + 1 : start + len(g)]:
                value = value + ref[...].astype(f32)
            out[...] = value.astype(bf16)
            start += len(g)

    return plain_call(kernel, shapes, [v for g in groups for v in g], specs, after)


def finish(group, after=()):
    block = (1,) + group[0].shape[1:]

    def kernel(*refs):
        value = refs[0][0].astype(f32)
        for ref in refs[1 : len(group)]:
            value = value + ref[0].astype(f32)
        refs[-1][...] = value

    specs = [pl.BlockSpec(block, lambda i: (0, 0, 0)) for _ in group]
    return plain_call(kernel, [jax.ShapeDtypeStruct(block[1:], f32)], group, specs, after)[0]


def plain_call(kernel, shapes, inputs, specs, after):
    moved = 2 * sum(x.size * x.dtype.itemsize for x in shapes)
    if specs is None:
        specs = [pl.BlockSpec(x.shape, lambda i: (0, 0, 0)) for x in inputs]
    return pl.pallas_call(
        kernel,
        grid=(1,),
        out_shape=shapes,
        in_specs=specs + [pl.BlockSpec(memory_space=pl.ANY)] * len(after),
        out_specs=[pl.BlockSpec(x.shape, lambda i, n=len(x.shape): (0,) * n) for x in shapes],
        compiler_params=pltpu.CompilerParams(vmem_limit_bytes=48 * 1024 * 1024),
        cost_estimate=pl.CostEstimate(flops=0, bytes_accessed=2 * moved, transcendentals=0),
    )(*inputs, *after)


def sum_all(cube, value):
    if not cube.fast:
        return lax.psum(value, AXES)
    value = value + cube.flip(value, 0)
    for k in range(cube.steps):
        value = value + cube.flip(value, cube.orders[0][k])
    return value


def place_images(cube, pieces, length, after=()):
    if not cube.fast:
        return lax.all_gather(pieces[0][:, :length], "tensor", axis=0, tiled=True)
    count = pieces[0].shape[0]
    index = lax.axis_index("tensor").astype(jnp.int32).reshape(1)

    def kernel(index_ref, *refs):
        for r in range(4):
            for i in range(count):
                refs[-1][(index_ref[0] ^ r) * count + i] = refs[r][i, :length, :]

    shape = (4 * count, length, pieces[0].shape[2])
    return call(kernel, [jax.ShapeDtypeStruct(shape, bf16)], index, pieces, [], [], 0, after)[0]


def call(kernel, out_shapes, index, inputs, weights, scratch, flops, after=()):
    inputs_all = [*inputs, *weights]
    moved = sum(x.size * x.dtype.itemsize for x in inputs_all)
    moved += sum(x.size * x.dtype.itemsize for x in out_shapes)
    n_in, n_w, n_out = len(inputs), len(weights), len(out_shapes)

    def body(index_ref, *refs):
        rest = refs[n_in + n_w + len(after) :]
        kernel(index_ref, *refs[: n_in + n_w], *rest)

    return pl.pallas_call(
        body,
        out_shape=out_shapes,
        in_specs=[pl.BlockSpec(memory_space=pltpu.SMEM)]
        + [pl.BlockSpec(memory_space=pltpu.VMEM)] * n_in
        + [pl.BlockSpec(memory_space=pl.ANY)] * (n_w + len(after)),
        out_specs=[pl.BlockSpec(memory_space=pltpu.VMEM)] * n_out,
        scratch_shapes=scratch,
        compiler_params=pltpu.CompilerParams(vmem_limit_bytes=56 * 1024 * 1024),
        cost_estimate=pl.CostEstimate(flops=flops, bytes_accessed=moved, transcendentals=0),
    )(index, *inputs, *weights, *after)


def nn(left, right):
    return lax.dot_general(left, right, (((1,), (0,)), ((), ())), preferred_element_type=f32)


def nt(left, right):
    return lax.dot_general(left, right, (((1,), (1,)), ((), ())), preferred_element_type=f32)


def tn(left, right):
    return lax.dot_general(left, right, (((0,), (0,)), ((), ())), preferred_element_type=f32)


def normed_of(values):
    centre = values - jnp.mean(values, -1, keepdims=True)
    inverse = lax.rsqrt(jnp.mean(centre * centre, -1, keepdims=True) + EPS)
    return (centre * inverse, inverse)


def norm_back(upstream, normed, inverse, gain):
    scaled = upstream * gain
    inner = (
        scaled
        - jnp.mean(scaled, -1, keepdims=True)
        - normed * jnp.mean(scaled * normed, -1, keepdims=True)
    )
    return inverse * inner


def column_sum(values):
    return jnp.sum(values, 0, keepdims=True)


def attend_kernel(cube, count, length, width, n_w, table_ref, *refs):
    x_ref, vec_ref, bias_ref = refs[:3]
    w_refs = refs[3 : 3 + n_w]
    n1_ref, qkv_ref, att_ref, hidden_ref, n2_ref = refs[3 + n_w : 8 + n_w]
    scratch, sum_ref = (refs[8 + n_w : 11 + n_w], refs[11 + n_w : 14 + n_w]), refs[14 + n_w]
    waits = [cube.fetch(cube.of_core(w_refs, core), scratch[core]) for core in range(2)]
    x = x_ref[...].astype(f32)
    normed, _ = normed_of(x)
    n1_ref[...] = (normed * vec_ref[0:1] + vec_ref[1:2]).astype(bf16)
    sum_ref[...] = x + vec_ref[2:3]
    tokens = x.shape[0] // count
    heads = width // HEAD_DIM
    keep = lax.broadcasted_iota(jnp.int32, (tokens, tokens), 1) < length

    for core in range(2):
        waits[core]()
        w_ref = scratch[core][1]

        def step(y, carry):
            t = 2 * y + core
            cube.load(table_ref, cube.of_core(w_refs, core), scratch[core], core, y)
            qkv = nn(n1_ref[...], w_ref[:, : 3 * width]) + bias_ref[t]
            qkv_ref[t] = qkv.astype(bf16)
            for b in range(count):
                rows = slice(b * tokens, (b + 1) * tokens)
                found = []
                for h in range(heads):
                    q = qkv_ref[t, rows, h * HEAD_DIM : (h + 1) * HEAD_DIM]
                    k = qkv_ref[t, rows, width + h * HEAD_DIM : width + (h + 1) * HEAD_DIM]
                    v = qkv_ref[t, rows, 2 * width + h * HEAD_DIM : 2 * width + (h + 1) * HEAD_DIM]
                    scores = jnp.where(keep, nt(q, k) * FACTOR, -1e30)
                    weights = jnp.exp(scores - jnp.max(scores, -1, keepdims=True))
                    probs = weights * (1.0 / jnp.sum(weights, -1, keepdims=True))
                    found.append(nn(probs.astype(bf16), v).astype(bf16))
                att_ref[t, rows, :] = jnp.concatenate(found, axis=1)
            sum_ref[...] += nt(att_ref[t], w_ref[:, 3 * width :])
            return carry

        lax.fori_loop(0, cube.n_t // 2, step, 0)
    hidden = sum_ref[...]
    hidden_ref[...] = hidden
    normed, _ = normed_of(hidden)
    n2_ref[...] = (normed * vec_ref[3:4] + vec_ref[4:5]).astype(bf16)


def gelu_kernel(cube, core, n_w, table_ref, *refs):
    n2_ref, cot_ref, bias_ref = refs[:3]
    w_refs = refs[3 : 3 + n_w]
    act_ref, slope_ref, grad_ref = refs[3 + n_w : 6 + n_w]
    scratch = refs[6 + n_w :]
    cube.fetch(w_refs, scratch)()

    def step(y, carry):
        cube.load(table_ref, w_refs, scratch, core, y)
        pre = nn(n2_ref[...], scratch[1][...]) + bias_ref[2 * y + core]
        cdf = 0.5 * (1.0 + lax.erf(pre * (0.5**0.5)))
        slope = cdf + pre * (jnp.exp(-0.5 * pre * pre) * 0.3989422804014327)
        act_ref[y] = (pre * cdf).astype(bf16)
        slope_ref[y] = slope.astype(bf16)
        cube.store(table_ref, grad_ref, core, y, tn(cot_ref[...], act_ref[y]).astype(bf16))
        return carry

    lax.fori_loop(0, cube.n_t // 2, step, 0)


def mlp_kernel(cube, core, first, n_w, table_ref, *refs):
    n2_ref, cot_ref, act_ref, slope_ref, mlp_in, dnorm_in, hidden_ref, vec_ref = refs[:8]
    one_refs, two_refs = refs[8 : 8 + n_w], refs[8 + n_w : 8 + 2 * n_w]
    outs = refs[8 + 2 * n_w :]
    grad_ref, sums_ref = outs[:2]
    if first:
        mlp_ref, dnorm_ref = outs[2:4]
        rest = outs[4:]
    else:
        enc_ref, dhidden_ref, small_ref = outs[2:5]
        rest = outs[5:]
    one, two = rest[:3], rest[3:6]
    if not first:
        mlp_ref, dnorm_ref = rest[6:8]
    waits = [cube.fetch(one_refs, one), cube.fetch(two_refs, two)]
    for wait in waits:
        wait()

    def step(y, carry):
        cube.load(table_ref, one_refs, one, core, y)
        cube.load(table_ref, two_refs, two, core, y)
        dact = nn(cot_ref[...], two[1][...])
        dpre = (slope_ref[y].astype(f32) * dact).astype(bf16)
        sums_ref[pl.ds(y, 1)] = column_sum(dpre.astype(f32))[None]
        cube.store(table_ref, grad_ref, core, y, tn(n2_ref[...], dpre).astype(bf16))
        dnorm_ref[...] += nt(dpre, one[1][...])
        mlp_ref[...] += nt(act_ref[y], two[1][...])
        return carry

    if first:
        mlp_ref[...] = mlp_in[...] + vec_ref[5:6]
        dnorm_ref[...] = jnp.zeros_like(dnorm_ref)
        lax.fori_loop(0, cube.n_t // 2, step, 0)
        return
    mlp_ref[...] = mlp_in[...]
    dnorm_ref[...] = dnorm_in[...]
    lax.fori_loop(0, cube.n_t // 2, step, 0)
    enc_ref[...] = mlp_ref[...].astype(bf16)
    normed, inverse = normed_of(hidden_ref[...])
    dnorm = dnorm_ref[...]
    cot = cot_ref[...].astype(f32)
    dhidden = cot + norm_back(dnorm, normed, inverse, vec_ref[3:4])
    dhidden_ref[...] = dhidden
    small_ref[0] = column_sum(dnorm * normed)
    small_ref[1] = column_sum(dnorm)
    small_ref[2] = column_sum(cot)
    small_ref[3] = column_sum(dhidden)


def attend_back_kernel(cube, core, first, count, length, width, n_w, table_ref, *refs):
    x_ref, n1_ref, qkv_ref, att_ref, dhidden_ref, dnorm_in, vec_ref = refs[:7]
    w_refs = refs[7 : 7 + n_w]
    outs = refs[7 + n_w :]
    grad_ref, dbias_ref = outs[:2]
    if first:
        dnorm_ref = outs[2]
        rest = outs[3:]
    else:
        patch_ref, small_ref = outs[2:4]
        rest = outs[4:]
    scratch = rest[:3]
    low_ref, dqkv_ref = rest[3:5]
    if not first:
        dnorm_ref = rest[5]
    wait = cube.fetch(w_refs, scratch)
    low_ref[...] = dhidden_ref[...].astype(bf16)
    dnorm_ref[...] = jnp.zeros_like(dnorm_ref) if first else dnorm_in[...]
    tokens = x_ref.shape[0] // count
    heads = width // HEAD_DIM
    keep = lax.broadcasted_iota(jnp.int32, (tokens, tokens), 0) < length
    wait()
    w_ref = scratch[1]

    def step(y, carry):
        t = 2 * y + core
        cube.load(table_ref, w_refs, scratch, core, y)
        datt = nn(low_ref[...], w_ref[:, 3 * width :]).astype(bf16)
        for b in range(count):
            rows = slice(b * tokens, (b + 1) * tokens)
            dqs, dks, dvs = [], [], []
            for h in range(heads):
                q = qkv_ref[t, rows, h * HEAD_DIM : (h + 1) * HEAD_DIM]
                k = qkv_ref[t, rows, width + h * HEAD_DIM : width + (h + 1) * HEAD_DIM]
                v = qkv_ref[t, rows, 2 * width + h * HEAD_DIM : 2 * width + (h + 1) * HEAD_DIM]
                do = datt[rows, h * HEAD_DIM : (h + 1) * HEAD_DIM]
                scores = jnp.where(keep, nt(k, q) * FACTOR, -1e30)
                weights = jnp.exp(scores - jnp.max(scores, 0, keepdims=True))
                probs = weights * (1.0 / jnp.sum(weights, 0, keepdims=True))
                dvs.append(nn(probs.astype(bf16), do))
                dprobs = nt(v, do)
                inner = jnp.sum(dprobs * probs, 0, keepdims=True)
                dscores = (probs * (dprobs - inner)).astype(bf16)
                dks.append(nn(dscores, q) * FACTOR)
                dqs.append(tn(dscores, k) * FACTOR)
            dqkv_ref[rows, :] = jnp.concatenate(dqs + dks + dvs, axis=1).astype(bf16)
        dqkv = dqkv_ref[...]
        dbias_ref[pl.ds(y, 1)] = column_sum(dqkv.astype(f32))[None]
        dnorm_ref[...] += nt(dqkv, w_ref[:, : 3 * width])
        grad = jnp.concatenate((tn(n1_ref[...], dqkv), tn(low_ref[...], att_ref[t])), axis=1)
        cube.store(table_ref, grad_ref, core, y, grad.astype(bf16))
        return carry

    lax.fori_loop(0, cube.n_t // 2, step, 0)
    if first:
        return
    normed, inverse = normed_of(x_ref[...].astype(f32))
    dnorm = dnorm_ref[...]
    patch = dhidden_ref[...] + norm_back(dnorm, normed, inverse, vec_ref[0:1])
    patch_ref[...] = patch.astype(bf16)
    small_ref[0] = column_sum(dnorm * normed)
    small_ref[1] = column_sum(dnorm)


def on_device(
    n_dp,
    n_t,
    patches,
    attn_gain,
    attn_shift,
    qkv_weight,
    qv_bias,
    out_weight,
    out_bias,
    mlp_gain,
    mlp_shift,
    fc1_weight,
    fc1_bias,
    fc2_weight,
    fc2_bias,
    cotangent,
):
    t_me = lax.axis_index("tensor")
    cube = Cube(n_dp, n_t, qkv_weight.shape[1])
    order = t_me ^ jnp.arange(n_t)
    width = qkv_weight.shape[2]
    f_width = fc1_weight.shape[1]
    d = patches.shape[2]
    table = cube.table()
    count = patches.shape[0] // n_t
    length = patches.shape[1]
    padded = -(-length // TILE) * TILE
    tokens = count * padded

    def own_images(values):
        mine = lax.dynamic_slice_in_dim(values, t_me * count, count, 0)
        return jnp.pad(mine, ((0, 0), (0, padded - length), (0, 0))).reshape(tokens, d)

    def shape(*dims, dtype=bf16):
        return jax.ShapeDtypeStruct(dims, dtype)

    attn_piece = jnp.concatenate(
        (qkv_weight[0], qkv_weight[1], qkv_weight[2], out_weight.T), axis=1
    )
    two_piece = fc2_weight.T
    biases = jnp.concatenate((qv_bias.reshape(-1), fc1_bias))[None]
    x = own_images(patches)
    cot = own_images(cotangent)
    vecs = jnp.stack((attn_gain, attn_shift, out_bias, mlp_gain, mlp_shift, fc2_bias)).astype(f32)

    def bias_parts(biases):
        biases = biases.astype(f32)
        zeros = jnp.zeros((n_t, width), f32)
        qkv = (biases[:, :width], zeros, biases[:, width : 2 * width])
        return (jnp.concatenate(qkv, axis=1)[:, None], biases[:, None, 2 * width :])

    last = cube.steps - 1
    if cube.fast:
        held = attn_piece[None]
        one = fc1_weight[None]
        two = two_piece[None]
        biases = jnp.concatenate((biases, cube.flip(biases, 0)))
        biases = jnp.concatenate((biases, cube.flip(biases, 1)))
        qkv_bias, f_bias = bias_parts(biases)
        for k in range(last, 0, -1):
            pairs = [(held, cube.swap(held, k))]
            if k < last:
                pairs.append((one, cube.swap(one, k + 1)))
            if k < last - 1:
                pairs.append((two, cube.swap(two, k + 2)))
            found = join(pairs, (x, cot) if k == last else ())
            if k == last:
                one, two = lax.optimization_barrier((one, two))
            held = found[0]
            one = found[1] if k < last else one
            two = found[2] if k < last - 1 else two
        came = cube.swap(held, 0)
        pairs = [(one, cube.swap(one, 1)), (two, cube.swap(two, 2))]
        w_attn = [held, came, cube.flip(held, 0), cube.flip(came, 0)]
        one, two = join(pairs, (came,))
        slot = (one, two)
    else:
        w_attn = gather_plain(cube, attn_piece)
        w_one = gather_plain(cube, fc1_weight)
        w_two = gather_plain(cube, two_piece)
        biases = jnp.take(lax.all_gather(biases[0], "tensor", axis=0, tiled=False), order, axis=0)
        qkv_bias, f_bias = bias_parts(biases)
        slot = ()
    n_w = len(w_attn)
    n_c = len(cube.of_core(w_attn, 0))
    spots = 2 * tokens * d * n_t
    attn_macs = spots * 2 * width + 4 * count * n_t * padded * padded * width
    buffers = cube.buffers(d)

    n1, qkv, att, hidden, n2 = call(
        partial(attend_kernel, cube, count, length, width, n_w),
        [
            shape(tokens, d),
            shape(n_t, tokens, 3 * width),
            shape(n_t, tokens, width),
            shape(tokens, d, dtype=f32),
            shape(tokens, d),
        ],
        table,
        [x, vecs, qkv_bias],
        w_attn,
        buffers * 2 + [pltpu.VMEM((tokens, d), f32)],
        2 * attn_macs,
        slot,
    )
    if cube.fast:
        came = cube.swap(one, 0)
        w_one = [one, came, cube.flip(one, 0), cube.flip(came, 0)]
        two = join([(two, cube.swap(two, 1))], (n2,))[0]
        slot = (two,)

    def gelu(core, after):
        return call(
            partial(gelu_kernel, cube, core, n_c),
            [shape(n_t // 2, tokens, f_width)] * 2 + [cube.grad_shape(f_width)],
            table,
            [n2, cot, f_bias],
            cube.of_core(w_one, core),
            buffers,
            spots * f_width,
            after,
        )

    act_other, slope_other, two_other = gelu(1, slot)
    act_own, slope_own, two_own = gelu(0, (two_other,))
    if cube.fast:
        came = cube.swap(two, 0)
        w_two = [two, came, cube.flip(two, 0), cube.flip(came, 0)]
        two_terms = [two_own, cube.flip(two_other, 0)]
        (s_two,) = sends([two_terms], ())
        slot = (s_two,)
    else:
        slot = ()

    def mlp(core, first, act, slope, mlp_in, dnorm_in, after):
        if first:
            outs = [shape(tokens, d, dtype=f32)] * 2
            scratch = []
        else:
            outs = [shape(tokens, d), shape(tokens, d, dtype=f32), shape(4, 1, d, dtype=f32)]
            scratch = [pltpu.VMEM((tokens, d), f32)] * 2
        return call(
            partial(mlp_kernel, cube, core, first, n_c),
            [cube.grad_shape(f_width), shape(n_t // 2, 1, f_width, dtype=f32)] + outs,
            table,
            [n2, cot, act, slope, mlp_in, dnorm_in, hidden, vecs],
            [*cube.of_core(w_one, core), *cube.of_core(w_two, core)],
            buffers * 2 + scratch,
            2 * spots * f_width,
            after,
        )

    one_other, f_other, mlp_sum, dnorm = mlp(1, True, act_other, slope_other, hidden, vecs, slot)
    one_own, f_own, enc, dhidden, mlp_small = mlp(
        0, False, act_own, slope_own, mlp_sum, dnorm, (one_other,)
    )
    images = enc.reshape(count, padded, d)
    if cube.fast:
        two_terms.append(cube.swap(s_two, 0))
        one_terms = [one_own, cube.flip(one_other, 0)]
        s_two, s_one = sends([two_terms, one_terms], (dhidden,))
        slot = (s_two, s_one)
        there = cube.flip(images, 1)
        enc_pieces = [images, cube.flip(images, 0), there, cube.flip(there, 0)]
    else:
        enc_pieces = [images]

    def attend_back(core, first, dnorm_in, after):
        if first:
            outs = [shape(tokens, d, dtype=f32)]
            scratch = []
        else:
            outs = [shape(tokens, d), shape(2, 1, d, dtype=f32)]
            scratch = [pltpu.VMEM((tokens, d), f32)]
        return call(
            partial(attend_back_kernel, cube, core, first, count, length, width, n_c),
            [cube.grad_shape(4 * width), shape(n_t // 2, 1, 3 * width, dtype=f32)] + outs,
            table,
            [x, n1, qkv, att, dhidden, dnorm_in, vecs],
            cube.of_core(w_attn, core),
            buffers
            + [pltpu.VMEM((tokens, d), bf16), pltpu.VMEM((tokens, 3 * width), bf16)]
            + scratch,
            2 * attn_macs,
            after,
        )

    attn_other, dbias_other, dnorm = attend_back(1, True, vecs, slot)
    if cube.fast:
        two_terms.append(cube.swap(s_two, 1))
        (s_two,) = sends([two_terms], (dnorm,))
        slot = (s_two,)
    attn_own, dbias_own, patch, attn_small = attend_back(0, False, dnorm, slot)
    images = patch.reshape(count, padded, d)
    if cube.fast:
        there = cube.flip(images, 1)
        patch_pieces = [images, cube.flip(images, 0), there, cube.flip(there, 0)]
        two_terms.append(cube.swap(s_two, 2))
        one_terms.append(cube.swap(s_one, 0))
        attn_terms = [attn_own, cube.flip(attn_other, 0)]
        s_attn, s_one, s_two = sends([attn_terms, one_terms, two_terms])
        k_attn, k_one, k_two = 0, 1, 3
        while True:
            attn_terms.append(cube.swap(s_attn, k_attn))
            if k_one <= last:
                one_terms.append(cube.swap(s_one, k_one))
            if k_two <= last:
                two_terms.append(cube.swap(s_two, k_two))
            k_attn, k_one, k_two = (k_attn + 1, k_one + 1, k_two + 1)
            if k_attn > last:
                break
            groups = [attn_terms]
            groups += [one_terms] if k_one <= last else []
            groups += [two_terms] if k_two <= last else []
            found = sends(groups)
            s_attn = found[0]
            s_one = found[1] if k_one <= last else None
            s_two = found[2] if k_two <= last else None
        two_grad = finish(two_terms)
        one_grad = finish(one_terms)
        attn_grad = finish(attn_terms)
    else:
        patch_pieces = [images]
        two_grad = scatter_plain(cube, two_own, two_other)
        one_grad = scatter_plain(cube, one_own, one_other)
        attn_grad = scatter_plain(cube, attn_own, attn_other)
    encoded = place_images(cube, enc_pieces, length)
    patch_grad = place_images(cube, patch_pieces, length)

    def in_order(own, other):
        both = jnp.stack((own[:, 0], other[:, 0]), axis=1)
        return jnp.take(both.reshape((n_t,) + own.shape[2:]), order, axis=0)

    dbias = in_order(dbias_own, dbias_other)
    f_sums = in_order(f_own, f_other)
    small = jnp.concatenate(
        (
            attn_small.reshape(-1),
            mlp_small.reshape(-1),
            dbias[:, :width].reshape(-1),
            dbias[:, 2 * width :].reshape(-1),
            f_sums.reshape(-1),
        )
    )
    small = sum_all(cube, small)
    cuts = [small[i * d : (i + 1) * d] for i in range(6)]
    at = 6 * d
    q_sum = lax.dynamic_slice_in_dim(small[at : at + n_t * width], t_me * width, width, 0)
    at += n_t * width
    v_sum = lax.dynamic_slice_in_dim(small[at : at + n_t * width], t_me * width, width, 0)
    at += n_t * width
    f_sum = lax.dynamic_slice_in_dim(small[at:], t_me * f_width, f_width, 0)
    return (
        encoded,
        patch_grad,
        cuts[0],
        cuts[1],
        jnp.stack([attn_grad[:, i * width : (i + 1) * width] for i in range(3)]),
        jnp.stack((q_sum, v_sum)),
        attn_grad[:, 3 * width :].T,
        cuts[5],
        cuts[2],
        cuts[3],
        one_grad,
        f_sum,
        two_grad.T,
        cuts[4],
    )


def solution(mesh):
    return jax.shard_map(
        partial(on_device, mesh.shape["dp"], mesh.shape["tensor"]),
        mesh=mesh,
        in_specs=(
            P("dp", None, None),
            P(),
            P(),
            P(None, "dp", "tensor"),
            P(None, "tensor"),
            P("tensor", "dp"),
            P(),
            P(),
            P(),
            P("dp", "tensor"),
            P("tensor"),
            P("tensor", "dp"),
            P(),
            P("dp", None, None),
        ),
        out_specs=(
            P("dp", None, None),
            P("dp", None, None),
            P(),
            P(),
            P(None, "dp", "tensor"),
            P(None, "tensor"),
            P("tensor", "dp"),
            P(),
            P(),
            P(),
            P("dp", "tensor"),
            P("tensor"),
            P("tensor", "dp"),
            P(),
        ),
        check_vma=False,
    )
```

```python
from functools import partial

import jax
import jax.numpy as jnp
from jax import lax
from jax.experimental import pallas as pl
from jax.experimental.pallas import tpu as pltpu
from jax.sharding import PartitionSpec as P

HEAD_DIM = 64
EPS = 1e-06
AXES = ("dp", "tensor")
TILE = 16
ROWS = 32
FACTOR = HEAD_DIM ** (-0.5)
bf16 = jnp.bfloat16
f32 = jnp.float32


class Cube:
    def __init__(self, n_dp, n_t, rows):
        self.n_dp, self.n_t, self.rows = n_dp, n_t, rows
        self.n = n_dp * n_t
        n_bits = self.n.bit_length() - 1
        self.fast = (1 << n_bits) == self.n and n_bits >= 4 and rows % TILE == 0
        far = list(range(n_bits - 1, 3, -1))
        self.orders = ([2, 1, 3] + far, [1, 3, 2] + far)
        self.steps = len(self.orders[0])
        self.half = self.n // 2

    def swap(self, value, k):
        return lax.ppermute(
            value, AXES, [(i, i ^ (1 << self.orders[i & 1][k])) for i in range(self.n)]
        )

    def flip(self, value, bit):
        return lax.ppermute(value, AXES, [(i, i ^ (1 << bit)) for i in range(self.n)])

    def at(self, ids_ref, core, y, block):
        relative = ((ids_ref[0] ^ block) << 2) | (y << 1)
        found = []
        for order in self.orders:
            place = 0
            for k, bit in enumerate(order[::-1]):
                place = place | (((relative >> bit) & 1) << k)
            found.append(place)
        return jnp.where((ids_ref[1] & 1) == core, found[0], found[1])

    def buffers(self, cols):
        blocks = (self.half, self.rows, cols) if self.fast else (1, 8, 128)
        shard = pltpu.VMEM((self.n_dp * self.rows, cols), bf16)
        return [pltpu.VMEM(blocks, bf16), shard, pltpu.SemaphoreType.DMA((2,))]

    def fetch(self, refs, scratch):
        if not self.fast:
            return lambda: None
        held, _, sems = scratch
        part = self.half // 2
        copies = [
            pltpu.make_async_copy(refs[i], held.at[pl.ds(i * part, part)], sems.at[i])
            for i in range(2)
        ]
        for copy in copies:
            copy.start()

        def wait():
            for copy in copies:
                copy.wait()

        return wait

    def load(self, ids_ref, refs, scratch, core, y):
        held, shard, sems = scratch
        if not self.fast:
            copy = pltpu.make_async_copy(refs[0].at[2 * y + core], shard, sems.at[0])
            copy.start()
            copy.wait()
            return
        for d in range(self.n_dp):
            shard[d * self.rows : (d + 1) * self.rows, :] = held[self.at(ids_ref, core, y, d)]

    def store(self, ids_ref, ref, core, y, value):
        if not self.fast:
            ref[y] = value
            return
        for d in range(self.n_dp):
            rows = value[d * self.rows : (d + 1) * self.rows]
            ref[self.at(ids_ref, core, y, d)] = rows

    def grad_shape(self, cols):
        if not self.fast:
            return jax.ShapeDtypeStruct((2, self.n_dp * self.rows, cols), bf16)
        return jax.ShapeDtypeStruct((self.half, self.rows, cols), bf16)

    def of_core(self, buffers, core):
        return buffers[2 * core : 2 * core + 2] if self.fast else buffers


def gather_plain(cube, piece):
    rows, cols = piece.shape
    whole = lax.all_gather(piece, AXES, axis=0, tiled=False)
    whole = whole.reshape(cube.n_dp, cube.n_t, rows, cols).transpose(1, 0, 2, 3)
    whole = whole.reshape(cube.n_t, cube.n_dp * rows, cols)
    return [jnp.take(whole, lax.axis_index("tensor") ^ jnp.arange(cube.n_t), axis=0)]


def scatter_plain(cube, own, other):
    n_t, n_dp, rows, cols = cube.n_t, cube.n_dp, cube.rows, own.shape[2]
    part = jnp.stack((own, other), axis=1).reshape(n_t, n_dp * rows, cols)
    part = jnp.take(part, lax.axis_index("tensor") ^ jnp.arange(n_t), axis=0)
    part = part.reshape(n_t, n_dp, rows, cols).transpose(1, 0, 2, 3)
    part = part.reshape(n_dp * n_t * rows, cols)
    return lax.psum_scatter(part, AXES, scatter_dimension=0, tiled=True).astype(f32)


def join(pairs, after=()):
    def kernel(*refs):
        outs = refs[2 * len(pairs) + len(after) :]
        for i, out in enumerate(outs):
            size = pairs[i][0].shape[0]
            out[:size] = refs[2 * i][...]
            out[size:] = refs[2 * i + 1][...]

    shapes = [
        jax.ShapeDtypeStruct((2 * p[0].shape[0],) + p[0].shape[1:], p[0].dtype) for p in pairs
    ]
    return plain_call(kernel, shapes, [x for p in pairs for x in p], None, after)


def sends(groups, after=()):
    sizes = [min(v.shape[0] for v in g) // 2 for g in groups]
    specs, shapes = [], []
    for g, size in zip(groups, sizes):
        block = (size,) + g[0].shape[1:]
        specs += [pl.BlockSpec(block, lambda i: (1, 0, 0)) for _ in g]
        shapes.append(jax.ShapeDtypeStruct(block, bf16))

    def kernel(*refs):
        outs = refs[-len(groups) :]
        start = 0
        for g, out in zip(groups, outs):
            value = refs[start][...].astype(f32)
            for ref in refs[start + 1 : start + len(g)]:
                value = value + ref[...].astype(f32)
            out[...] = value.astype(bf16)
            start += len(g)

    return plain_call(kernel, shapes, [v for g in groups for v in g], specs, after)


def finish(group, after=()):
    block = (1,) + group[0].shape[1:]

    def kernel(*refs):
        value = refs[0][0].astype(f32)
        for ref in refs[1 : len(group)]:
            value = value + ref[0].astype(f32)
        refs[-1][...] = value

    specs = [pl.BlockSpec(block, lambda i: (0, 0, 0)) for _ in group]
    return plain_call(kernel, [jax.ShapeDtypeStruct(block[1:], f32)], group, specs, after)[0]


def plain_call(kernel, shapes, inputs, specs, after, ids=None, scratch=()):
    if specs is None:
        specs = [pl.BlockSpec(x.shape, lambda i: (0, 0, 0)) for x in inputs]
    if ids is not None:
        specs = [pl.BlockSpec(memory_space=pltpu.SMEM)] + specs
        inputs = [ids, *inputs]
    return pl.pallas_call(
        kernel,
        grid=(1,),
        out_shape=shapes,
        in_specs=specs + [pl.BlockSpec(memory_space=pl.ANY)] * len(after),
        out_specs=[pl.BlockSpec(x.shape, lambda i, n=len(x.shape): (0,) * n) for x in shapes],
        scratch_shapes=list(scratch),
        compiler_params=pltpu.CompilerParams(vmem_limit_bytes=48 * 1024 * 1024),
        cost_estimate=pl.CostEstimate(flops=0, bytes_accessed=1024, transcendentals=0),
    )(*inputs, *after)


def sends_with_small(cube, group, groups, small, ids, after=()):
    rows = cube.rows
    kept = [v.shape[0] // rows * rows for v in group]
    size = min(kept) // 2
    d = group[0].shape[1]
    first = len(small) > 1
    specs, inputs = [], list(group)
    for v in group:
        if v.shape[0] % size == 0:
            specs.append(pl.BlockSpec((size, d), lambda i: (1, 0)))
        else:
            specs.append(pl.BlockSpec(v.shape, lambda i: (0, 0)))
    exact = [v.shape[0] % size == 0 for v in group]
    for v in small:
        specs.append(pl.BlockSpec(v.shape, lambda i, n=len(v.shape): (0,) * n))
        inputs.append(v)
    sizes = [min(v.shape[0] for v in g) // 2 for g in groups]
    shapes = [
        jax.ShapeDtypeStruct((size + ROWS, d), bf16),
        jax.ShapeDtypeStruct((ROWS, d), bf16),
    ]
    for g, half in zip(groups, sizes):
        block = (half,) + g[0].shape[1:]
        specs += [pl.BlockSpec(block, lambda i: (1, 0, 0)) for _ in g]
        shapes.append(jax.ShapeDtypeStruct(block, bf16))
        inputs += g
    n_out = len(shapes)

    def kernel(ids_ref, *refs):
        outs = refs[len(inputs) + len(after) :]
        total_ref = outs[n_out]
        terms = refs[: len(group)]
        value = None
        for ref, whole in zip(terms, exact):
            part = (ref[...] if whole else ref[size : 2 * size, :]).astype(f32)
            value = part if value is None else value + part
        outs[0][:size, :] = value.astype(bf16)
        extra = refs[len(group) : len(group) + len(small)]
        if first:
            gather_small(cube, ids_ref, extra, total_ref)
        else:
            last = terms[-1]
            total_ref[...] = extra[0][...].astype(f32) + last[kept[-1] :, :].astype(f32)
        low = total_ref[...].astype(bf16)
        outs[0][size:, :] = low
        outs[1][...] = low
        start = len(group) + len(small)
        for g, out in zip(groups, outs[2:n_out]):
            value = refs[start][...].astype(f32)
            for ref in refs[start + 1 : start + len(g)]:
                value = value + ref[...].astype(f32)
            out[...] = value.astype(bf16)
            start += len(g)

    return plain_call(kernel, shapes, inputs, specs, after, ids, [pltpu.VMEM((ROWS, d), f32)])


def gather_small(cube, ids_ref, refs, out_ref):
    attn_ref, mlp_ref = refs[:2]
    out_ref[...] = jnp.zeros_like(out_ref)
    for i in range(2):
        out_ref[i : i + 1, :] = attn_ref[i]
    for i in range(4):
        out_ref[2 + i : 3 + i, :] = mlp_ref[i]
    n_t = cube.n_t
    for core in range(2):
        for y in range(n_t // 2):
            t = (2 * y + core) ^ ids_ref[1]
            dbias = refs[2 + core][y]
            width = dbias.shape[1] // 3
            out_ref[pl.ds(6 + t, 1), :] = refs[4 + core][y]
            out_ref[pl.ds(6 + n_t + t, 1), :width] = dbias[:, :width]
            out_ref[pl.ds(6 + 2 * n_t + t, 1), :width] = dbias[:, 2 * width :]


def finish_with_small(cube, group, small):
    rows = cube.rows
    d = group[0].shape[1]
    tail = group[-1].shape[0] - rows
    specs = [
        pl.BlockSpec((rows, d), lambda i: (0, 0))
        if v.shape[0] % rows == 0
        else pl.BlockSpec(v.shape, lambda i: (0, 0))
        for v in group
    ]
    specs.append(pl.BlockSpec(small.shape, lambda i: (0, 0)))

    def kernel(*refs):
        value = None
        for ref in refs[: len(group)]:
            part = ref[:rows, :].astype(f32)
            value = part if value is None else value + part
        refs[-2][...] = value
        extra = refs[len(group) - 1][rows : rows + tail, :].astype(f32)
        refs[-1][...] = (refs[len(group)][...].astype(f32) + extra).astype(bf16)

    shapes = [jax.ShapeDtypeStruct((rows, d), f32), jax.ShapeDtypeStruct(small.shape, bf16)]
    return plain_call(kernel, shapes, [*group, small], specs, ())


def place_images(cube, pieces, length, after=()):
    if not cube.fast:
        return lax.all_gather(pieces[0][:, :length], "tensor", axis=0, tiled=True)
    count = pieces[0].shape[0]
    index = lax.axis_index("tensor").astype(jnp.int32).reshape(1)

    def kernel(index_ref, *refs):
        for r in range(4):
            for i in range(count):
                refs[-1][(index_ref[0] ^ r) * count + i] = refs[r][i, :length, :]

    shape = (4 * count, length, pieces[0].shape[2])
    return call(kernel, [jax.ShapeDtypeStruct(shape, bf16)], index, pieces, [], [], after)[0]


def call(kernel, out_shapes, index, inputs, weights, scratch, after=()):
    n_in, n_w, n_out = len(inputs), len(weights), len(out_shapes)

    def body(index_ref, *refs):
        rest = refs[n_in + n_w + len(after) :]
        kernel(index_ref, *refs[: n_in + n_w], *rest)

    return pl.pallas_call(
        body,
        out_shape=out_shapes,
        in_specs=[pl.BlockSpec(memory_space=pltpu.SMEM)]
        + [pl.BlockSpec(memory_space=pltpu.VMEM)] * n_in
        + [pl.BlockSpec(memory_space=pl.ANY)] * (n_w + len(after)),
        out_specs=[pl.BlockSpec(memory_space=pltpu.VMEM)] * n_out,
        scratch_shapes=scratch,
        compiler_params=pltpu.CompilerParams(vmem_limit_bytes=56 * 1024 * 1024),
        cost_estimate=pl.CostEstimate(flops=0, bytes_accessed=1024, transcendentals=0),
    )(index, *inputs, *weights, *after)


def nn(left, right):
    return lax.dot_general(left, right, (((1,), (0,)), ((), ())), preferred_element_type=f32)


def nt(left, right):
    return lax.dot_general(left, right, (((1,), (1,)), ((), ())), preferred_element_type=f32)


def tn(left, right):
    return lax.dot_general(left, right, (((0,), (0,)), ((), ())), preferred_element_type=f32)


def normed_of(values):
    centre = values - jnp.mean(values, -1, keepdims=True)
    inverse = lax.rsqrt(jnp.mean(centre * centre, -1, keepdims=True) + EPS)
    return (centre * inverse, inverse)


def norm_back(upstream, normed, inverse, gain):
    scaled = upstream * gain
    inner = (
        scaled
        - jnp.mean(scaled, -1, keepdims=True)
        - normed * jnp.mean(scaled * normed, -1, keepdims=True)
    )
    return inverse * inner


def column_sum(values):
    return jnp.sum(values, 0, keepdims=True)


def attend_kernel(cube, core, first, count, length, width, n_w, ids_ref, *refs):
    x_ref, n1_in, sum_in, vec_ref, bias_ref = refs[:5]
    w_refs = refs[5 : 5 + n_w]
    qkv_ref, att_ref = refs[5 + n_w : 7 + n_w]
    scratch = refs[9 + n_w : 12 + n_w]
    wait = cube.fetch(w_refs, scratch)
    if first:
        n1_ref, sum_ref = refs[7 + n_w : 9 + n_w]
        x = x_ref[...].astype(f32)
        normed, _ = normed_of(x)
        n1_ref[...] = (normed * vec_ref[0:1] + vec_ref[1:2]).astype(bf16)
        sum_ref[...] = x + vec_ref[2:3]
    else:
        hidden_ref, n2_ref = refs[7 + n_w : 9 + n_w]
        n1_ref, sum_ref = n1_in, hidden_ref
        sum_ref[...] = sum_in[...]
    tokens = x_ref.shape[0] // count
    heads = width // HEAD_DIM
    keep = lax.broadcasted_iota(jnp.int32, (tokens, tokens), 1) < length

    wait()
    w_ref = scratch[1]

    def step(y, carry):
        cube.load(ids_ref, w_refs, scratch, core, y)
        qkv = nn(n1_ref[...], w_ref[:, : 3 * width]) + bias_ref[2 * y + core]
        qkv_ref[y] = qkv.astype(bf16)
        for b in range(count):
            rows = slice(b * tokens, (b + 1) * tokens)
            found = []
            for h in range(heads):
                q = qkv_ref[y, rows, h * HEAD_DIM : (h + 1) * HEAD_DIM]
                k = qkv_ref[y, rows, width + h * HEAD_DIM : width + (h + 1) * HEAD_DIM]
                v = qkv_ref[y, rows, 2 * width + h * HEAD_DIM : 2 * width + (h + 1) * HEAD_DIM]
                scores = jnp.where(keep, nt(q, k) * FACTOR, -1e30)
                weights = jnp.exp(scores - jnp.max(scores, -1, keepdims=True))
                probs = weights * (1.0 / jnp.sum(weights, -1, keepdims=True))
                found.append(nn(probs.astype(bf16), v).astype(bf16))
            att_ref[y, rows, :] = jnp.concatenate(found, axis=1)
        sum_ref[...] += nt(att_ref[y], w_ref[:, 3 * width :])
        return carry

    lax.fori_loop(0, cube.n_t // 2, step, 0)
    if first:
        return
    normed, _ = normed_of(hidden_ref[...])
    n2_ref[...] = (normed * vec_ref[3:4] + vec_ref[4:5]).astype(bf16)


def gelu_kernel(cube, core, n_w, ids_ref, *refs):
    n2_ref, cot_ref, bias_ref = refs[:3]
    w_refs = refs[3 : 3 + n_w]
    act_ref, slope_ref, grad_ref = refs[3 + n_w : 6 + n_w]
    scratch = refs[6 + n_w :]
    cube.fetch(w_refs, scratch)()

    def step(y, carry):
        cube.load(ids_ref, w_refs, scratch, core, y)
        pre = nn(n2_ref[...], scratch[1][...]) + bias_ref[2 * y + core]
        cdf = 0.5 * (1.0 + lax.erf(pre * (0.5**0.5)))
        slope = cdf + pre * (jnp.exp(-0.5 * pre * pre) * 0.3989422804014327)
        act_ref[y] = (pre * cdf).astype(bf16)
        slope_ref[y] = slope.astype(bf16)
        cube.store(ids_ref, grad_ref, core, y, tn(cot_ref[...], act_ref[y]).astype(bf16))
        return carry

    lax.fori_loop(0, cube.n_t // 2, step, 0)


def mlp_kernel(cube, core, first, n_w, ids_ref, *refs):
    n2_ref, cot_ref, act_ref, slope_ref, mlp_in, dnorm_in, hidden_ref, vec_ref = refs[:8]
    one_refs, two_refs = refs[8 : 8 + n_w], refs[8 + n_w : 8 + 2 * n_w]
    outs = refs[8 + 2 * n_w :]
    grad_ref, sums_ref = outs[:2]
    if first:
        mlp_ref, dnorm_ref = outs[2:4]
        rest = outs[4:]
    else:
        enc_ref, dhidden_ref, small_ref = outs[2:5]
        rest = outs[5:]
    one, two = rest[:3], rest[3:6]
    if not first:
        mlp_ref, dnorm_ref = rest[6:8]
    waits = [cube.fetch(one_refs, one), cube.fetch(two_refs, two)]
    for wait in waits:
        wait()

    def step(y, carry):
        cube.load(ids_ref, one_refs, one, core, y)
        cube.load(ids_ref, two_refs, two, core, y)
        dact = nn(cot_ref[...], two[1][...])
        dpre = (slope_ref[y].astype(f32) * dact).astype(bf16)
        sums_ref[pl.ds(y, 1)] = column_sum(dpre.astype(f32))[None]
        cube.store(ids_ref, grad_ref, core, y, tn(n2_ref[...], dpre).astype(bf16))
        dnorm_ref[...] += nt(dpre, one[1][...])
        mlp_ref[...] += nt(act_ref[y], two[1][...])
        return carry

    if first:
        mlp_ref[...] = mlp_in[...] + vec_ref[5:6]
        dnorm_ref[...] = jnp.zeros_like(dnorm_ref)
        lax.fori_loop(0, cube.n_t // 2, step, 0)
        return
    mlp_ref[...] = mlp_in[...]
    dnorm_ref[...] = dnorm_in[...]
    lax.fori_loop(0, cube.n_t // 2, step, 0)
    enc_ref[...] = mlp_ref[...].astype(bf16)
    normed, inverse = normed_of(hidden_ref[...])
    dnorm = dnorm_ref[...]
    cot = cot_ref[...].astype(f32)
    dhidden = cot + norm_back(dnorm, normed, inverse, vec_ref[3:4])
    dhidden_ref[...] = dhidden
    small_ref[0] = column_sum(dnorm * normed)
    small_ref[1] = column_sum(dnorm)
    small_ref[2] = column_sum(cot)
    small_ref[3] = column_sum(dhidden)


def attend_back_kernel(cube, core, first, count, length, width, n_w, ids_ref, *refs):
    x_ref, n1_ref, qkv_ref, att_ref, dhidden_ref, dnorm_in, vec_ref = refs[:7]
    w_refs = refs[7 : 7 + n_w]
    outs = refs[7 + n_w :]
    grad_ref, dbias_ref = outs[:2]
    if first:
        dnorm_ref = outs[2]
        rest = outs[3:]
    else:
        dnorm_ref, small_ref = outs[2:4]
        rest = outs[4:]
    scratch = rest[:3]
    low_ref, dqkv_ref = rest[3:5]
    wait = cube.fetch(w_refs, scratch)
    low_ref[...] = dhidden_ref[...].astype(bf16)
    dnorm_ref[...] = jnp.zeros_like(dnorm_ref) if first else dnorm_in[...]
    tokens = x_ref.shape[0] // count
    heads = width // HEAD_DIM
    keep = lax.broadcasted_iota(jnp.int32, (tokens, tokens), 0) < length
    wait()
    w_ref = scratch[1]

    def step(y, carry):
        cube.load(ids_ref, w_refs, scratch, core, y)
        datt = nn(low_ref[...], w_ref[:, 3 * width :]).astype(bf16)
        for b in range(count):
            rows = slice(b * tokens, (b + 1) * tokens)
            dqs, dks, dvs = [], [], []
            for h in range(heads):
                q = qkv_ref[y, rows, h * HEAD_DIM : (h + 1) * HEAD_DIM]
                k = qkv_ref[y, rows, width + h * HEAD_DIM : width + (h + 1) * HEAD_DIM]
                v = qkv_ref[y, rows, 2 * width + h * HEAD_DIM : 2 * width + (h + 1) * HEAD_DIM]
                do = datt[rows, h * HEAD_DIM : (h + 1) * HEAD_DIM]
                scores = jnp.where(keep, nt(k, q) * FACTOR, -1e30)
                weights = jnp.exp(scores - jnp.max(scores, 0, keepdims=True))
                probs = weights * (1.0 / jnp.sum(weights, 0, keepdims=True))
                dvs.append(nn(probs.astype(bf16), do))
                dprobs = nt(v, do)
                inner = jnp.sum(dprobs * probs, 0, keepdims=True)
                dscores = (probs * (dprobs - inner)).astype(bf16)
                dks.append(nn(dscores, q) * FACTOR)
                dqs.append(tn(dscores, k) * FACTOR)
            dqkv_ref[rows, :] = jnp.concatenate(dqs + dks + dvs, axis=1).astype(bf16)
        dqkv = dqkv_ref[...]
        dbias_ref[pl.ds(y, 1)] = column_sum(dqkv.astype(f32))[None]
        dnorm_ref[...] += nt(dqkv, w_ref[:, : 3 * width])
        grad = jnp.concatenate((tn(n1_ref[...], dqkv), tn(low_ref[...], att_ref[y])), axis=1)
        cube.store(ids_ref, grad_ref, core, y, grad.astype(bf16))
        return carry

    lax.fori_loop(0, cube.n_t // 2, step, 0)
    if first:
        return
    normed, _ = normed_of(x_ref[...].astype(f32))
    dnorm = dnorm_ref[...]
    small_ref[0] = column_sum(dnorm * normed)
    small_ref[1] = column_sum(dnorm)


def patch_kernel(ids_ref, x_ref, dhidden_ref, dnorm_ref, vec_ref, patch_ref):
    normed, inverse = normed_of(x_ref[...].astype(f32))
    patch = dhidden_ref[...] + norm_back(dnorm_ref[...], normed, inverse, vec_ref[0:1])
    patch_ref[...] = patch.astype(bf16)


def on_device(
    n_dp,
    n_t,
    patches,
    attn_gain,
    attn_shift,
    qkv_weight,
    qv_bias,
    out_weight,
    out_bias,
    mlp_gain,
    mlp_shift,
    fc1_weight,
    fc1_bias,
    fc2_weight,
    fc2_bias,
    cotangent,
):
    t_me = lax.axis_index("tensor")
    cube = Cube(n_dp, n_t, qkv_weight.shape[1])
    order = t_me ^ jnp.arange(n_t)
    width = qkv_weight.shape[2]
    f_width = fc1_weight.shape[1]
    d = patches.shape[2]
    ids = jnp.stack((lax.axis_index("dp"), t_me)).astype(jnp.int32)
    count = patches.shape[0] // n_t
    length = patches.shape[1]
    padded = -(-length // TILE) * TILE
    tokens = count * padded

    def own_images(values):
        mine = lax.dynamic_slice_in_dim(values, t_me * count, count, 0)
        return jnp.pad(mine, ((0, 0), (0, padded - length), (0, 0))).reshape(tokens, d)

    def shape(*dims, dtype=bf16):
        return jax.ShapeDtypeStruct(dims, dtype)

    attn_piece = jnp.concatenate(
        (qkv_weight[0], qkv_weight[1], qkv_weight[2], out_weight.T), axis=1
    )
    two_piece = fc2_weight.T
    biases = jnp.concatenate((qv_bias.reshape(-1), fc1_bias))[None]
    x = own_images(patches)
    cot = own_images(cotangent)
    vecs = jnp.stack((attn_gain, attn_shift, out_bias, mlp_gain, mlp_shift, fc2_bias)).astype(f32)

    def bias_parts(biases):
        biases = biases.astype(f32)
        zeros = jnp.zeros((n_t, width), f32)
        qkv = (biases[:, :width], zeros, biases[:, width : 2 * width])
        return (jnp.concatenate(qkv, axis=1)[:, None], biases[:, None, 2 * width :])

    last = cube.steps - 1
    if cube.fast:
        held = attn_piece[None]
        one = fc1_weight[None]
        two = two_piece[None]
        biases = jnp.concatenate((biases, cube.flip(biases, 0)))
        biases = jnp.concatenate((biases, cube.flip(biases, 1)))
        qkv_bias, f_bias = bias_parts(biases)
        for k in range(last, 0, -1):
            pairs = [(held, cube.swap(held, k))]
            if k < last:
                pairs.append((one, cube.swap(one, k + 1)))
            tokens_in = (x, cot) if k == last else (vecs, qkv_bias, f_bias) if k == 1 else ()
            found = join(pairs, tokens_in)
            held = found[0]
            one = found[1] if k < last else one
        came = cube.swap(held, 0)
        pairs = [(one, cube.swap(one, 1)), (two, cube.swap(two, last))]
        w_attn = [held, came, cube.flip(held, 0), cube.flip(came, 0)]
        one, two = join(pairs, (came,))
        slot = (one, two)
    else:
        w_attn = gather_plain(cube, attn_piece)
        w_one = gather_plain(cube, fc1_weight)
        w_two = gather_plain(cube, two_piece)
        biases = jnp.take(lax.all_gather(biases[0], "tensor", axis=0, tiled=False), order, axis=0)
        qkv_bias, f_bias = bias_parts(biases)
        slot = ()
    n_c = len(cube.of_core(w_attn, 0))
    buffers = cube.buffers(d)

    def attend(core, first, n1, sums, after):
        if first:
            outs = [shape(tokens, d), shape(tokens, d, dtype=f32)]
        else:
            outs = [shape(tokens, d, dtype=f32), shape(tokens, d)]
        return call(
            partial(attend_kernel, cube, core, first, count, length, width, n_c),
            [shape(n_t // 2, tokens, 3 * width), shape(n_t // 2, tokens, width)] + outs,
            ids,
            [x, n1, sums, vecs, qkv_bias],
            cube.of_core(w_attn, core),
            buffers,
            after,
        )

    qkv_own, att_own, n1, sums = attend(0, True, vecs, vecs, slot)
    if cube.fast:
        for k in range(last - 1, 1, -1):
            two = join([(two, cube.swap(two, k))], (n1,))[0]
        slot = (two,)
    qkv_other, att_other, hidden, n2 = attend(1, False, n1, sums, slot)
    qkvs, atts = (qkv_own, qkv_other), (att_own, att_other)
    if cube.fast:
        came = cube.swap(one, 0)
        w_one = [one, came, cube.flip(one, 0), cube.flip(came, 0)]
        two = join([(two, cube.swap(two, 1))], (n2,))[0]
        slot = (two,)

    def gelu(core, after):
        return call(
            partial(gelu_kernel, cube, core, n_c),
            [shape(n_t // 2, tokens, f_width)] * 2 + [cube.grad_shape(f_width)],
            ids,
            [n2, cot, f_bias],
            cube.of_core(w_one, core),
            buffers,
            after,
        )

    act_own, slope_own, two_own = gelu(0, slot)
    act_other, slope_other, two_other = gelu(1, (two_own,))
    if cube.fast:
        came = cube.swap(two, 0)
        w_two = [two, came, cube.flip(two, 0), cube.flip(came, 0)]
        two_terms = [two_own, cube.flip(two_other, 0)]

    def mlp(core, first, act, slope, mlp_in, dnorm_in, after):
        if first:
            outs = [shape(tokens, d, dtype=f32)] * 2
            scratch = []
        else:
            outs = [shape(tokens, d), shape(tokens, d, dtype=f32), shape(4, 1, d, dtype=f32)]
            scratch = [pltpu.VMEM((tokens, d), f32)] * 2
        return call(
            partial(mlp_kernel, cube, core, first, n_c),
            [cube.grad_shape(f_width), shape(n_t // 2, 1, f_width, dtype=f32)] + outs,
            ids,
            [n2, cot, act, slope, mlp_in, dnorm_in, hidden, vecs],
            [*cube.of_core(w_one, core), *cube.of_core(w_two, core)],
            buffers * 2 + scratch,
            after,
        )

    one_own, f_own, mlp_sum, dnorm = mlp(0, True, act_own, slope_own, hidden, vecs, (two_other,))
    slot = (one_own,)
    if cube.fast:
        (s_two,) = sends([two_terms], (dnorm,))
        slot = (s_two,)
    one_other, f_other, enc, dhidden, mlp_small = mlp(
        1, False, act_other, slope_other, mlp_sum, dnorm, slot
    )
    images = enc.reshape(count, padded, d)
    slot = ()
    if cube.fast:
        two_terms.append(cube.swap(s_two, 0))
        one_terms = [one_own, cube.flip(one_other, 0)]
        (s_two,) = sends([two_terms], (dhidden,))
        slot = (s_two,)
        there = cube.flip(images, 1)
        enc_pieces = [images, cube.flip(images, 0), there, cube.flip(there, 0)]
    else:
        enc_pieces = [images]

    def attend_back(core, first, dnorm_in, after):
        if first:
            outs = [shape(tokens, d, dtype=f32)]
            scratch = []
        else:
            outs = [shape(tokens, d, dtype=f32), shape(2, 1, d, dtype=f32)]
            scratch = []
        return call(
            partial(attend_back_kernel, cube, core, first, count, length, width, n_c),
            [cube.grad_shape(4 * width), shape(n_t // 2, 1, 3 * width, dtype=f32)] + outs,
            ids,
            [x, n1, qkvs[core], atts[core], dhidden, dnorm_in, vecs],
            cube.of_core(w_attn, core),
            buffers
            + [pltpu.VMEM((tokens, d), bf16), pltpu.VMEM((tokens, 3 * width), bf16)]
            + scratch,
            after,
        )

    attn_other, dbias_other, dnorm = attend_back(1, True, vecs, slot)
    if cube.fast:
        two_terms.append(cube.swap(s_two, 1))
        s_one, s_two = sends([one_terms, two_terms], (dnorm,))
        slot = (s_one, s_two)
    attn_own, dbias_own, dnorm, attn_small = attend_back(0, False, dnorm, slot)

    def patch_of(after):
        patch = call(
            patch_kernel, [shape(tokens, d)], ids, [x, dhidden, dnorm, vecs], [], [], after
        )[0]
        return patch.reshape(count, padded, d)

    if cube.fast:
        one_terms.append(cube.swap(s_one, 0))
        two_terms.append(cube.swap(s_two, 2))
        flat = (cube.half * cube.rows, d)
        attn_terms = [attn_own.reshape(flat), cube.flip(attn_other.reshape(flat), 0)]
        small = (attn_small, mlp_small, dbias_own, dbias_other, f_own, f_other)
        k_one, k_two = 1, 3
        for k in range(cube.steps):
            groups = [one_terms] if k_one <= last else []
            groups += [two_terms] if k_two <= last else []
            found = sends_with_small(cube, attn_terms, groups, small, ids)
            small = (found[1],)
            if k == 1:
                images = patch_of((found[1],))
            attn_terms.append(cube.swap(found[0], k))
            if k_one <= last:
                one_terms.append(cube.swap(found[2], k_one))
            if k_two <= last:
                two_terms.append(cube.swap(found[3], k_two))
            k_one, k_two = (k_one + 1, k_two + 1)
        there = cube.flip(images, 1)
        patch_pieces = [images, cube.flip(images, 0), there, cube.flip(there, 0)]
        two_grad = finish(two_terms)
        one_grad = finish(one_terms)
        attn_grad, small = finish_with_small(cube, attn_terms, small[0])
        small = small.astype(f32) + cube.flip(small, 0).astype(f32)
    else:
        patch_pieces = [patch_of(())]
        two_grad = scatter_plain(cube, two_own, two_other)
        one_grad = scatter_plain(cube, one_own, one_other)
        attn_grad = scatter_plain(cube, attn_own, attn_other)
    encoded = place_images(cube, enc_pieces, length)
    patch_grad = place_images(cube, patch_pieces, length)

    if not cube.fast:

        def collect(ids_ref, *refs):
            gather_small(cube, ids_ref, refs[:6], refs[6])

        small = call(
            collect,
            [shape(ROWS, d, dtype=f32)],
            ids,
            [attn_small, mlp_small, dbias_own, dbias_other, f_own, f_other],
            [],
            [],
        )[0]
        small = lax.psum(small, AXES)

    def shard_row(at):
        return lax.dynamic_slice_in_dim(small, at + t_me, 1, 0)

    return (
        encoded,
        patch_grad,
        small[0],
        small[1],
        jnp.stack([attn_grad[:, i * width : (i + 1) * width] for i in range(3)]),
        jnp.concatenate((shard_row(6 + n_t), shard_row(6 + 2 * n_t)))[:, :width],
        attn_grad[:, 3 * width :].T,
        small[5],
        small[2],
        small[3],
        one_grad,
        shard_row(6)[0],
        two_grad.T,
        small[4],
    )


def solution(mesh):
    return jax.shard_map(
        partial(on_device, mesh.shape["dp"], mesh.shape["tensor"]),
        mesh=mesh,
        in_specs=(
            P("dp", None, None),
            P(),
            P(),
            P(None, "dp", "tensor"),
            P(None, "tensor"),
            P("tensor", "dp"),
            P(),
            P(),
            P(),
            P("dp", "tensor"),
            P("tensor"),
            P("tensor", "dp"),
            P(),
            P("dp", None, None),
        ),
        out_specs=(
            P("dp", None, None),
            P("dp", None, None),
            P(),
            P(),
            P(None, "dp", "tensor"),
            P(None, "tensor"),
            P("tensor", "dp"),
            P(),
            P(),
            P(),
            P("dp", "tensor"),
            P("tensor"),
            P("tensor", "dp"),
            P(),
        ),
        check_vma=False,
    )
```

```python
from functools import partial

import jax
import jax.numpy as jnp
from jax import lax
from jax.experimental import pallas as pl
from jax.experimental.pallas import tpu as pltpu
from jax.sharding import PartitionSpec as P

HEAD_DIM = 64
EPS = 1e-06
AXES = ("dp", "tensor")
TILE = 16
ROWS = 32
FACTOR = HEAD_DIM ** (-0.5)
bf16 = jnp.bfloat16
f32 = jnp.float32


class Cube:
    def __init__(self, n_dp, n_t, rows):
        self.n_dp, self.n_t, self.rows = n_dp, n_t, rows
        self.n = n_dp * n_t
        n_bits = self.n.bit_length() - 1
        self.fast = (1 << n_bits) == self.n and n_bits >= 4 and rows % TILE == 0
        far = list(range(n_bits - 1, 3, -1))
        self.orders = [
            ([2, 1, 3] + far, [1, 3, 2] + far),
            ([2, 3, 1] + far, [1, 3, 2] + far),
            ([3, 1, 2] + far, [2, 3, 1] + far),
        ]
        self.steps = 3 + len(far)
        self.half = self.n // 2

    def swap(self, group, value, k):
        orders = self.orders[group]
        return lax.ppermute(value, AXES, [(i, i ^ (1 << orders[i & 1][k])) for i in range(self.n)])

    def flip(self, value, bits):
        return lax.ppermute(value, AXES, [(i, i ^ bits) for i in range(self.n)])

    def at(self, group, ids_ref, core, y, block):
        relative = ((ids_ref[0] ^ block) << 2) | (y << 1)
        found = []
        for order in self.orders[group]:
            place = 0
            for k, bit in enumerate(order[::-1]):
                place = place | (((relative >> bit) & 1) << k)
            found.append(place)
        return jnp.where((ids_ref[1] & 1) == core, found[0], found[1])

    def buffers(self, cols):
        blocks = (2, self.half, self.rows, cols) if self.fast else (1, 1, 8, 128)
        shard = pltpu.VMEM((self.n_dp * self.rows, cols), bf16)
        return [pltpu.VMEM(blocks, bf16), shard, pltpu.SemaphoreType.DMA((4,))]

    def fetch(self, refs, scratch):
        if not self.fast:
            return lambda core: None
        held, _, sems = scratch
        part = self.half // 2
        copies = [
            pltpu.make_async_copy(refs[i], held.at[i // 2, pl.ds(i % 2 * part, part)], sems.at[i])
            for i in range(4)
        ]
        for copy in copies:
            copy.start()

        def wait(core):
            copies[2 * core].wait()
            copies[2 * core + 1].wait()

        return wait

    def load(self, group, ids_ref, refs, scratch, core, y):
        held, shard, sems = scratch
        if not self.fast:
            copy = pltpu.make_async_copy(refs[0].at[2 * y + core], shard, sems.at[0])
            copy.start()
            copy.wait()
            return
        for d in range(self.n_dp):
            rows = slice(d * self.rows, (d + 1) * self.rows)
            shard[rows, :] = held[core, self.at(group, ids_ref, core, y, d)]

    def grad_buffers(self, cols):
        shape = self.grad_shape(cols).shape
        return [pltpu.VMEM((2,) + shape, bf16), pltpu.SemaphoreType.DMA((2,))]

    def store(self, group, ids_ref, scratch, core, y, value):
        if not self.fast:
            scratch[0][core, y] = value
            return
        for d in range(self.n_dp):
            rows = value[d * self.rows : (d + 1) * self.rows]
            scratch[0][core, self.at(group, ids_ref, core, y, d)] = rows

    def send_out(self, scratch, core, ref):
        copy = pltpu.make_async_copy(scratch[0].at[core], ref, scratch[1].at[core])
        copy.start()
        return copy

    def grad_shape(self, cols):
        if not self.fast:
            return jax.ShapeDtypeStruct((2, self.n_dp * self.rows, cols), bf16)
        return jax.ShapeDtypeStruct((self.half, self.rows, cols), bf16)


def gather_plain(cube, piece):
    rows, cols = piece.shape
    whole = lax.all_gather(piece, AXES, axis=0, tiled=False)
    whole = whole.reshape(cube.n_dp, cube.n_t, rows, cols).transpose(1, 0, 2, 3)
    whole = whole.reshape(cube.n_t, cube.n_dp * rows, cols)
    return [jnp.take(whole, lax.axis_index("tensor") ^ jnp.arange(cube.n_t), axis=0)]


def scatter_plain(cube, own, other):
    n_t, n_dp, rows, cols = cube.n_t, cube.n_dp, cube.rows, own.shape[2]
    part = jnp.stack((own, other), axis=1).reshape(n_t, n_dp * rows, cols)
    part = jnp.take(part, lax.axis_index("tensor") ^ jnp.arange(n_t), axis=0)
    part = part.reshape(n_t, n_dp, rows, cols).transpose(1, 0, 2, 3)
    part = part.reshape(n_dp * n_t * rows, cols)
    return lax.psum_scatter(part, AXES, scatter_dimension=0, tiled=True).astype(f32)


def join(pairs, after=()):
    def kernel(*refs):
        outs = refs[2 * len(pairs) + len(after) :]
        for i, out in enumerate(outs):
            size = pairs[i][0].shape[0]
            out[:size] = refs[2 * i][...]
            out[size:] = refs[2 * i + 1][...]

    shapes = [
        jax.ShapeDtypeStruct((2 * p[0].shape[0],) + p[0].shape[1:], p[0].dtype) for p in pairs
    ]
    return plain_call(kernel, shapes, [x for p in pairs for x in p], after)


def sends(groups, after=()):
    sizes = [min(v.shape[0] for v in g) // 2 for g in groups]
    inputs = [(v, size) for g, size in zip(groups, sizes) for v in g]
    shapes = [jax.ShapeDtypeStruct((n,) + g[0].shape[1:], bf16) for g, n in zip(groups, sizes)]

    def kernel(*refs):
        outs = refs[len(inputs) + len(after) :]
        parts = pull(refs, [(size, size) for _, size in inputs], outs[len(groups) :])
        for g, out in zip(groups, outs):
            out[...] = added(parts, len(g)).astype(bf16)

    return pull_call(kernel, shapes, [v for v, _ in inputs], [n for _, n in inputs], after)


def pull(refs, spots, scratch):
    sems = scratch[len(spots)]
    copies = [
        pltpu.make_async_copy(refs[i].at[pl.ds(start, size)], scratch[i], sems.at[i])
        for i, (start, size) in enumerate(spots)
    ]
    for copy in copies:
        copy.start()

    def each():
        for i, copy in enumerate(copies):
            copy.wait()
            yield scratch[i][...]

    return each()


def added(parts, n):
    value = next(parts).astype(f32)
    for _ in range(n - 1):
        value = value + next(parts).astype(f32)
    return value


def pull_call(kernel, shapes, inputs, sizes, after, ids=None, whole=(), scratch=()):
    specs = [pl.BlockSpec(memory_space=pltpu.HBM)] * len(inputs)
    specs += [pl.BlockSpec(memory_space=pl.ANY)] * len(after)
    values = [*inputs, *after]
    pulled = [pltpu.VMEM((n,) + v.shape[1:], bf16) for v, n in zip(inputs, sizes)]
    pulled += [pltpu.SemaphoreType.DMA((len(inputs),)), *scratch]
    if ids is not None:
        specs = [
            pl.BlockSpec(memory_space=pltpu.SMEM),
            *[pl.BlockSpec(memory_space=pltpu.VMEM)] * len(whole),
            *specs,
        ]
        values = [ids, *whole, *values]
    return pl.pallas_call(
        kernel,
        out_shape=shapes,
        in_specs=specs,
        out_specs=[pl.BlockSpec(memory_space=pltpu.VMEM)] * len(shapes),
        scratch_shapes=pulled,
        compiler_params=pltpu.CompilerParams(vmem_limit_bytes=48 * 1024 * 1024),
        cost_estimate=pl.CostEstimate(flops=0, bytes_accessed=1024, transcendentals=0),
    )(*values)


def plain_call(kernel, shapes, inputs, after):
    specs = [pl.BlockSpec(x.shape, lambda i: (0, 0, 0)) for x in inputs]
    return pl.pallas_call(
        kernel,
        grid=(1,),
        out_shape=shapes,
        in_specs=specs + [pl.BlockSpec(memory_space=pl.ANY)] * len(after),
        out_specs=[pl.BlockSpec(x.shape, lambda i, n=len(x.shape): (0,) * n) for x in shapes],
        compiler_params=pltpu.CompilerParams(vmem_limit_bytes=48 * 1024 * 1024),
        cost_estimate=pl.CostEstimate(flops=0, bytes_accessed=1024, transcendentals=0),
    )(*inputs, *after)


def sends_with_small(cube, group, groups, small, ids, after=(), final=False):
    rows = cube.rows
    kept = [v.shape[0] // rows * rows for v in group]
    size = min(kept) // 2
    d = group[0].shape[1]
    first = len(small) > 1
    sizes = [min(v.shape[0] for v in g) // 2 for g in groups]
    shapes = [
        jax.ShapeDtypeStruct((size + ROWS, d), bf16),
        jax.ShapeDtypeStruct((ROWS, d), bf16),
    ]
    if final:
        shapes += [jax.ShapeDtypeStruct(g[0].shape[1:], f32) for g in groups]
    else:
        shapes += [jax.ShapeDtypeStruct((n,) + g[0].shape[1:], bf16) for g, n in zip(groups, sizes)]
    inputs = list(group) + [v for g in groups for v in g]
    spots = [(size, size)] * len(group)
    spots += [(0, 1) if final else (n, n) for g, n in zip(groups, sizes) for _ in g]
    if not first:
        inputs.append(group[-1])
        spots.append((kept[-1], ROWS))

    def kernel(ids_ref, *refs):
        extra, refs = refs[: len(small)], refs[len(small) :]
        outs = refs[len(inputs) + len(after) :]
        total_ref = outs[-1]
        parts = pull(refs, spots, outs[len(shapes) :])
        outs[0][:size, :] = added(parts, len(group)).astype(bf16)
        for g, out in zip(groups, outs[2:]):
            value = added(parts, len(g))
            out[...] = value[0] if final else value.astype(bf16)
        if first:
            gather_small(cube, ids_ref, extra, total_ref)
        else:
            total_ref[...] = extra[0][...].astype(f32) + added(parts, 1)
        low = total_ref[...].astype(bf16)
        outs[0][size:, :] = low
        outs[1][...] = low

    return pull_call(
        kernel, shapes, inputs, [n for _, n in spots], after, ids, small, [pltpu.VMEM((ROWS, d), f32)]
    )


def gather_small(cube, ids_ref, refs, out_ref):
    attn_ref, mlp_ref = refs[:2]
    out_ref[...] = jnp.zeros_like(out_ref)
    for i in range(2):
        out_ref[i : i + 1, :] = attn_ref[i]
    for i in range(4):
        out_ref[2 + i : 3 + i, :] = mlp_ref[i]
    n_t = cube.n_t
    for relative in range(n_t):
        t = relative ^ ids_ref[1]
        dbias = refs[2][relative]
        width = dbias.shape[1] // 3
        out_ref[pl.ds(6 + t, 1), :] = refs[3][relative]
        out_ref[pl.ds(6 + n_t + t, 1), :width] = dbias[:, :width]
        out_ref[pl.ds(6 + 2 * n_t + t, 1), :width] = dbias[:, 2 * width :]


def finish_with_small(cube, group, small, ids, after=()):
    rows, d = cube.rows, group[0].shape[1]
    inputs = [*group, group[-1]]
    spots = [(0, rows)] * len(group) + [(group[-1].shape[0] - ROWS, ROWS)]

    def kernel(ids_ref, small_ref, *refs):
        outs = refs[len(inputs) + len(after) :]
        parts = pull(refs, spots, outs[2:])
        outs[0][...] = added(parts, len(group))
        outs[1][...] = (small_ref[...].astype(f32) + added(parts, 1)).astype(bf16)

    shapes = [jax.ShapeDtypeStruct((rows, d), f32), jax.ShapeDtypeStruct(small.shape, bf16)]
    return pull_call(kernel, shapes, inputs, [n for _, n in spots], after, ids, [small])


def hold(values, after):
    n = len(values)

    def kernel(*refs):
        pass

    return pl.pallas_call(
        kernel,
        out_shape=[jax.ShapeDtypeStruct(v.shape, v.dtype) for v in values],
        in_specs=[pl.BlockSpec(memory_space=pl.ANY)] * (n + len(after)),
        out_specs=[pl.BlockSpec(memory_space=pl.ANY)] * n,
        input_output_aliases={i: i for i in range(n)},
        cost_estimate=pl.CostEstimate(flops=0, bytes_accessed=1024, transcendentals=0),
    )(*values, *after)


def place_images(cube, pieces, length, after=()):
    if not cube.fast:
        return lax.all_gather(pieces[0][:, :length], "tensor", axis=0, tiled=True)
    count = pieces[0].shape[0]
    index = lax.axis_index("tensor").astype(jnp.int32).reshape(1)

    def kernel(index_ref, *refs):
        for r in range(4):
            for i in range(count):
                refs[-1][(index_ref[0] ^ r) * count + i] = refs[r][i, :length, :]

    shape = (4 * count, length, pieces[0].shape[2])
    return call(kernel, [jax.ShapeDtypeStruct(shape, bf16)], index, pieces, [], [], after)[0]


def call(kernel, out_shapes, index, inputs, weights, scratch, after=(), grads=()):
    out_shapes = [*out_shapes, jax.ShapeDtypeStruct((8, 128), f32)]
    n_in, n_w, n_out = len(inputs), len(weights), len(out_shapes)
    spots = [pl.BlockSpec(memory_space=pltpu.VMEM)] * n_out
    spots += [pl.BlockSpec(memory_space=pltpu.HBM)] * len(grads)

    def body(index_ref, *refs):
        rest = refs[n_in + n_w + len(after) :]
        rest[n_out - 1][...] = jnp.zeros((8, 128), f32)
        kernel(index_ref, *refs[: n_in + n_w], *rest[: n_out - 1], *rest[n_out:])

    return pl.pallas_call(
        body,
        out_shape=[*out_shapes, *grads],
        in_specs=[pl.BlockSpec(memory_space=pltpu.SMEM)]
        + [pl.BlockSpec(memory_space=pltpu.VMEM)] * n_in
        + [pl.BlockSpec(memory_space=pltpu.HBM)] * n_w
        + [pl.BlockSpec(memory_space=pl.ANY)] * len(after),
        out_specs=spots,
        scratch_shapes=scratch,
        compiler_params=pltpu.CompilerParams(vmem_limit_bytes=56 * 1024 * 1024),
        cost_estimate=pl.CostEstimate(flops=0, bytes_accessed=1024, transcendentals=0),
    )(index, *inputs, *weights, *after)


def nn(left, right):
    return lax.dot_general(left, right, (((1,), (0,)), ((), ())), preferred_element_type=f32)


def nt(left, right):
    return lax.dot_general(left, right, (((1,), (1,)), ((), ())), preferred_element_type=f32)


def tn(left, right):
    return lax.dot_general(left, right, (((0,), (0,)), ((), ())), preferred_element_type=f32)


def normed_of(values):
    centre = values - jnp.mean(values, -1, keepdims=True)
    inverse = lax.rsqrt(jnp.mean(centre * centre, -1, keepdims=True) + EPS)
    return (centre * inverse, inverse)


def norm_back(upstream, normed, inverse, gain):
    scaled = upstream * gain
    inner = (
        scaled
        - jnp.mean(scaled, -1, keepdims=True)
        - normed * jnp.mean(scaled * normed, -1, keepdims=True)
    )
    return inverse * inner


def column_sum(values):
    return jnp.sum(values, 0, keepdims=True)


def attend_kernel(cube, count, length, width, n_w, ids_ref, *refs):
    x_ref, vec_ref, bias_ref = refs[:3]
    w_refs = refs[3 : 3 + n_w]
    n1_ref, qkv_ref, att_ref, sum_ref, n2_ref = refs[3 + n_w : 8 + n_w]
    scratch = refs[8 + n_w :]
    wait = cube.fetch(w_refs, scratch)
    x = x_ref[...].astype(f32)
    normed, _ = normed_of(x)
    n1_ref[...] = (normed * vec_ref[0:1] + vec_ref[1:2]).astype(bf16)
    sum_ref[...] = x + vec_ref[2:3]
    tokens = x_ref.shape[0] // count
    heads = width // HEAD_DIM
    keep = lax.broadcasted_iota(jnp.int32, (tokens, tokens), 1) < length
    w_ref = scratch[1]

    for core in range(2):
        wait(core)

        def step(y, carry):
            t = 2 * y + core
            cube.load(0, ids_ref, w_refs, scratch, core, y)
            qkv = nn(n1_ref[...], w_ref[:, : 3 * width]) + bias_ref[t]
            qkv_ref[t] = qkv.astype(bf16)
            for b in range(count):
                rows = slice(b * tokens, (b + 1) * tokens)
                found = []
                for h in range(heads):
                    q = qkv_ref[t, rows, h * HEAD_DIM : (h + 1) * HEAD_DIM]
                    k = qkv_ref[t, rows, width + h * HEAD_DIM : width + (h + 1) * HEAD_DIM]
                    v = qkv_ref[t, rows, 2 * width + h * HEAD_DIM : 2 * width + (h + 1) * HEAD_DIM]
                    scores = jnp.where(keep, nt(q, k) * FACTOR, -1e30)
                    weights = jnp.exp(scores - jnp.max(scores, -1, keepdims=True))
                    probs = weights * (1.0 / jnp.sum(weights, -1, keepdims=True))
                    found.append(nn(probs.astype(bf16), v).astype(bf16))
                att_ref[t, rows, :] = jnp.concatenate(found, axis=1)
            sum_ref[...] += nt(att_ref[t], w_ref[:, 3 * width :])
            return carry

        lax.fori_loop(0, cube.n_t // 2, step, 0)
    normed, _ = normed_of(sum_ref[...])
    n2_ref[...] = (normed * vec_ref[3:4] + vec_ref[4:5]).astype(bf16)


def gelu_kernel(cube, n_w, ids_ref, *refs):
    n2_ref, cot_ref, bias_ref = refs[:3]
    w_refs = refs[3 : 3 + n_w]
    act_ref, slope_ref = refs[3 + n_w : 5 + n_w]
    grad_refs = refs[5 + n_w : 7 + n_w]
    scratch, grads = refs[7 + n_w : 10 + n_w], refs[10 + n_w :]
    wait = cube.fetch(w_refs, scratch)
    copies = []
    for core in range(2):
        wait(core)

        def step(y, carry):
            t = 2 * y + core
            cube.load(1, ids_ref, w_refs, scratch, core, y)
            pre = nn(n2_ref[...], scratch[1][...]) + bias_ref[t]
            cdf = 0.5 * (1.0 + lax.erf(pre * (0.5**0.5)))
            slope = cdf + pre * (jnp.exp(-0.5 * pre * pre) * 0.3989422804014327)
            act_ref[t] = (pre * cdf).astype(bf16)
            slope_ref[t] = slope.astype(bf16)
            cube.store(2, ids_ref, grads, core, y, tn(cot_ref[...], act_ref[t]).astype(bf16))
            return carry

        lax.fori_loop(0, cube.n_t // 2, step, 0)
        copies.append(cube.send_out(grads, core, grad_refs[core]))
    for copy in copies:
        copy.wait()


def mlp_kernel(cube, n_w, ids_ref, *refs):
    n2_ref, cot_ref, act_ref, slope_ref, hidden_ref, vec_ref = refs[:6]
    one_refs, two_refs = refs[6 : 6 + n_w], refs[6 + n_w : 6 + 2 * n_w]
    outs = refs[6 + 2 * n_w :]
    sums_ref, enc_ref, dhidden_ref, small_ref = outs[:4]
    grad_refs = outs[4:6]
    one, two, grads = outs[6:9], outs[9:12], outs[12:14]
    mlp_ref, dnorm_ref = outs[14:]
    waits = [cube.fetch(one_refs, one), cube.fetch(two_refs, two)]
    mlp_ref[...] = hidden_ref[...] + vec_ref[5:6]
    dnorm_ref[...] = jnp.zeros_like(dnorm_ref)
    copies = []
    for core in range(2):
        for wait in waits:
            wait(core)

        def step(y, carry):
            t = 2 * y + core
            cube.load(1, ids_ref, one_refs, one, core, y)
            cube.load(2, ids_ref, two_refs, two, core, y)
            dact = nn(cot_ref[...], two[1][...])
            dpre = (slope_ref[t].astype(f32) * dact).astype(bf16)
            sums_ref[pl.ds(t, 1)] = column_sum(dpre.astype(f32))[None]
            cube.store(1, ids_ref, grads, core, y, tn(n2_ref[...], dpre).astype(bf16))
            dnorm_ref[...] += nt(dpre, one[1][...])
            mlp_ref[...] += nt(act_ref[t], two[1][...])
            return carry

        lax.fori_loop(0, cube.n_t // 2, step, 0)
        copies.append(cube.send_out(grads, core, grad_refs[core]))
    enc_ref[...] = mlp_ref[...].astype(bf16)
    normed, inverse = normed_of(hidden_ref[...])
    dnorm = dnorm_ref[...]
    cot = cot_ref[...].astype(f32)
    dhidden = cot + norm_back(dnorm, normed, inverse, vec_ref[3:4])
    dhidden_ref[...] = dhidden
    small_ref[0] = column_sum(dnorm * normed)
    small_ref[1] = column_sum(dnorm)
    small_ref[2] = column_sum(cot)
    small_ref[3] = column_sum(dhidden)
    for copy in copies:
        copy.wait()


def attend_back_kernel(cube, count, length, width, n_w, ids_ref, *refs):
    x_ref, n1_ref, qkv_ref, att_ref, dhidden_ref, vec_ref = refs[:6]
    w_refs = refs[6 : 6 + n_w]
    outs = refs[6 + n_w :]
    dbias_ref, dnorm_ref, small_ref = outs[:3]
    grad_refs = outs[3:5]
    scratch, grads = outs[5:8], outs[8:10]
    low_ref, dqkv_ref = outs[10:]
    wait = cube.fetch(w_refs, scratch)
    low_ref[...] = dhidden_ref[...].astype(bf16)
    dnorm_ref[...] = jnp.zeros_like(dnorm_ref)
    tokens = x_ref.shape[0] // count
    heads = width // HEAD_DIM
    keep = lax.broadcasted_iota(jnp.int32, (tokens, tokens), 0) < length
    w_ref = scratch[1]
    copies = []
    for core in (1, 0):
        wait(core)

        def step(y, carry):
            t = 2 * y + core
            cube.load(0, ids_ref, w_refs, scratch, core, y)
            datt = nn(low_ref[...], w_ref[:, 3 * width :]).astype(bf16)
            for b in range(count):
                rows = slice(b * tokens, (b + 1) * tokens)
                dqs, dks, dvs = [], [], []
                for h in range(heads):
                    q = qkv_ref[t, rows, h * HEAD_DIM : (h + 1) * HEAD_DIM]
                    k = qkv_ref[t, rows, width + h * HEAD_DIM : width + (h + 1) * HEAD_DIM]
                    v = qkv_ref[t, rows, 2 * width + h * HEAD_DIM : 2 * width + (h + 1) * HEAD_DIM]
                    do = datt[rows, h * HEAD_DIM : (h + 1) * HEAD_DIM]
                    scores = jnp.where(keep, nt(k, q) * FACTOR, -1e30)
                    weights = jnp.exp(scores - jnp.max(scores, 0, keepdims=True))
                    probs = weights * (1.0 / jnp.sum(weights, 0, keepdims=True))
                    dvs.append(nn(probs.astype(bf16), do))
                    dprobs = nt(v, do)
                    inner = jnp.sum(dprobs * probs, 0, keepdims=True)
                    dscores = (probs * (dprobs - inner)).astype(bf16)
                    dks.append(nn(dscores, q) * FACTOR)
                    dqs.append(tn(dscores, k) * FACTOR)
                dqkv_ref[rows, :] = jnp.concatenate(dqs + dks + dvs, axis=1).astype(bf16)
            dqkv = dqkv_ref[...]
            dbias_ref[pl.ds(t, 1)] = column_sum(dqkv.astype(f32))[None]
            dnorm_ref[...] += nt(dqkv, w_ref[:, : 3 * width])
            grad = jnp.concatenate((tn(n1_ref[...], dqkv), tn(low_ref[...], att_ref[t])), axis=1)
            cube.store(0, ids_ref, grads, core, y, grad.astype(bf16))
            return carry

        lax.fori_loop(0, cube.n_t // 2, step, 0)
        copies.append(cube.send_out(grads, core, grad_refs[core]))
    normed, _ = normed_of(x_ref[...].astype(f32))
    dnorm = dnorm_ref[...]
    small_ref[0] = column_sum(dnorm * normed)
    small_ref[1] = column_sum(dnorm)
    for copy in copies:
        copy.wait()


def patch_kernel(ids_ref, x_ref, dhidden_ref, dnorm_ref, vec_ref, patch_ref):
    normed, inverse = normed_of(x_ref[...].astype(f32))
    patch = dhidden_ref[...] + norm_back(dnorm_ref[...], normed, inverse, vec_ref[0:1])
    patch_ref[...] = patch.astype(bf16)


def on_device(
    n_dp,
    n_t,
    patches,
    attn_gain,
    attn_shift,
    qkv_weight,
    qv_bias,
    out_weight,
    out_bias,
    mlp_gain,
    mlp_shift,
    fc1_weight,
    fc1_bias,
    fc2_weight,
    fc2_bias,
    cotangent,
):
    t_me = lax.axis_index("tensor")
    cube = Cube(n_dp, n_t, qkv_weight.shape[1])
    order = t_me ^ jnp.arange(n_t)
    width = qkv_weight.shape[2]
    f_width = fc1_weight.shape[1]
    d = patches.shape[2]
    ids = jnp.stack((lax.axis_index("dp"), t_me)).astype(jnp.int32)
    count = patches.shape[0] // n_t
    length = patches.shape[1]
    padded = -(-length // TILE) * TILE
    tokens = count * padded

    def own_images(values):
        mine = lax.dynamic_slice_in_dim(values, t_me * count, count, 0)
        return jnp.pad(mine, ((0, 0), (0, padded - length), (0, 0))).reshape(tokens, d)

    def shape(*dims, dtype=bf16):
        return jax.ShapeDtypeStruct(dims, dtype)

    attn_piece = jnp.concatenate(
        (qkv_weight[0], qkv_weight[1], qkv_weight[2], out_weight.T), axis=1
    )
    two_piece = fc2_weight.T
    biases = jnp.concatenate((qv_bias.reshape(-1), fc1_bias))[None]
    x = own_images(patches)
    cot = own_images(cotangent)
    vecs = jnp.stack((attn_gain, attn_shift, out_bias, mlp_gain, mlp_shift, fc2_bias)).astype(f32)

    def bias_parts(biases):
        biases = biases.astype(f32)
        zeros = jnp.zeros((n_t, width), f32)
        qkv = (biases[:, :width], zeros, biases[:, width : 2 * width])
        return (jnp.concatenate(qkv, axis=1)[:, None], biases[:, None, 2 * width :])

    last = cube.steps - 1
    if cube.fast:
        held = attn_piece[None]
        one = fc1_weight[None]
        two = two_piece[None]
        for k in range(last, 0, -1):
            pairs = [(held, cube.swap(0, held, k))]
            if k < last:
                pairs.append((one, cube.swap(1, one, k + 1)))
            if k < last - 1:
                pairs.append((two, cube.swap(2, two, k + 2)))
            tokens_in = (x, cot) if k == last else (vecs, qkv_bias, f_bias) if k == 1 else ()
            found = join(pairs, tokens_in)
            held = found[0]
            one = found[1] if k < last else one
            two = found[2] if k < last - 1 else two
            if k == last:
                (biases,) = hold([biases], (held,))
                biases = [biases] + [cube.flip(biases, r) for r in range(1, n_t)]
                qkv_bias, f_bias = bias_parts(jnp.concatenate(biases))
        came = cube.swap(0, held, 0)
        pairs = [(one, cube.swap(1, one, 1)), (two, cube.swap(2, two, 2))]
        w_attn = [held, came, cube.flip(held, 1), cube.flip(came, 1)]
        one, two = join(pairs, (came,))
        slot = (one, two)
    else:
        w_attn = gather_plain(cube, attn_piece)
        w_one = gather_plain(cube, fc1_weight)
        w_two = gather_plain(cube, two_piece)
        biases = jnp.take(lax.all_gather(biases[0], "tensor", axis=0, tiled=False), order, axis=0)
        qkv_bias, f_bias = bias_parts(biases)
        slot = ()
    n_w = len(w_attn)
    buffers = cube.buffers(d)
    grad_buffers = cube.grad_buffers(d)
    grad_shapes = [cube.grad_shape(d)] * 2

    n1, qkv, att, hidden, n2, done = call(
        partial(attend_kernel, cube, count, length, width, n_w),
        [
            shape(tokens, d),
            shape(n_t, tokens, 3 * width),
            shape(n_t, tokens, width),
            shape(tokens, d, dtype=f32),
            shape(tokens, d),
        ],
        ids,
        [x, vecs, qkv_bias],
        w_attn,
        buffers,
        slot,
    )
    if cube.fast:
        (came,) = hold([cube.swap(1, one, 0)], (done,))
        w_one = [one, came, cube.flip(one, 1), cube.flip(came, 1)]
        (two,) = join([(two, cube.swap(2, two, 1))], (done,))
        slot = (two,)
    act, slope, done, *two_grads = call(
        partial(gelu_kernel, cube, n_w),
        [shape(n_t, tokens, f_width)] * 2,
        ids,
        [n2, cot, f_bias],
        w_one,
        buffers + grad_buffers,
        slot,
        grad_shapes,
    )
    if cube.fast:
        (came,) = hold([cube.swap(2, two, 0)], (done,))
        w_two = [two, came, cube.flip(two, 1), cube.flip(came, 1)]
    f_sums, enc, dhidden, mlp_small, done, *one_grads = call(
        partial(mlp_kernel, cube, n_w),
        [
            shape(n_t, 1, f_width, dtype=f32),
            shape(tokens, d),
            shape(tokens, d, dtype=f32),
            shape(4, 1, d, dtype=f32),
        ],
        ids,
        [n2, cot, act, slope, hidden, vecs],
        [*w_one, *w_two],
        buffers * 2 + grad_buffers + [pltpu.VMEM((tokens, d), f32)] * 2,
        (),
        grad_shapes,
    )
    slot = ()
    if cube.fast:
        two_terms = [two_grads[0], cube.flip(two_grads[1], 1)]
        one_terms = [one_grads[0], cube.flip(one_grads[1], 1)]
        s_two, s_one = sends([two_terms, one_terms], (done,))
        slot = (s_two, s_one)
    dbias, dnorm, attn_small, done, *attn_grads = call(
        partial(attend_back_kernel, cube, count, length, width, n_w),
        [
            shape(n_t, 1, 3 * width, dtype=f32),
            shape(tokens, d, dtype=f32),
            shape(2, 1, d, dtype=f32),
        ],
        ids,
        [x, n1, qkv, att, dhidden, vecs],
        w_attn,
        buffers
        + grad_buffers
        + [pltpu.VMEM((tokens, d), bf16), pltpu.VMEM((tokens, 3 * width), bf16)],
        slot,
        grad_shapes,
    )

    def patch_of(after):
        patch = call(
            patch_kernel, [shape(tokens, d)], ids, [x, dhidden, dnorm, vecs], [], [], after
        )[0]
        return patch.reshape(count, padded, d)

    images = enc.reshape(count, padded, d)
    sums = (attn_small, mlp_small, dbias, f_sums)
    if cube.fast:

        def spread(images, there):
            return [images, cube.flip(images, 1), there, cube.flip(there, 1)]

        two_terms.append(cube.swap(2, s_two, 0))
        one_terms.append(cube.swap(1, s_one, 0))
        there = cube.flip(images, 2)
        came = (two_terms[-1], one_terms[-1], there)
        flat = (cube.half * cube.rows, d)
        other, images = hold([attn_grads[1].reshape(flat), images], came)
        s_two, s_one = sends([two_terms, one_terms], (done,))
        attn_terms = [attn_grads[0].reshape(flat), cube.flip(other, 1)]
        small = sums
        for k in range(cube.steps):
            if k == 0:
                found = sends_with_small(cube, attn_terms, [], small, ids, (s_one,))
            elif k < last:
                found = sends_with_small(cube, attn_terms, [two_terms, one_terms], small, ids, after)
                s_two, s_one = found[2:]
            else:
                found = sends_with_small(
                    cube, attn_terms, [two_terms, one_terms], small, ids, after, True
                )
                two_grad, one_grad = found[2:]
            small, after = (found[1],), ()
            attn_terms.append(cube.swap(0, found[0], k))
            if k < last:
                two_terms.append(cube.swap(2, s_two, k + 1))
                one_terms.append(cube.swap(1, s_one, k + 1))
            if k == 0:
                images, there = hold([images, there], small)
                encoded = place_images(cube, spread(images, there), length)
                after = (encoded,)
            if k == last - 1:
                images = patch_of(small)
                there = cube.flip(images, 2)
            if k == last:
                images, there = hold([images, there], small)
                patch_grad = place_images(cube, spread(images, there), length)
        attn_grad, small = finish_with_small(cube, attn_terms, small[0], ids, (patch_grad,))
        small = small.astype(f32) + cube.flip(small, 1).astype(f32)
    else:
        two_grad = scatter_plain(cube, *two_grads)
        one_grad = scatter_plain(cube, *one_grads)
        attn_grad = scatter_plain(cube, *attn_grads)
        encoded = place_images(cube, [images], length)
        patch_grad = place_images(cube, [patch_of(())], length)

        def collect(ids_ref, *refs):
            gather_small(cube, ids_ref, refs[:4], refs[4])

        small = call(collect, [shape(ROWS, d, dtype=f32)], ids, sums, [], [])[0]
        small = lax.psum(small, AXES)

    def shard_row(at):
        return lax.dynamic_slice_in_dim(small, at + t_me, 1, 0)

    return (
        encoded,
        patch_grad,
        small[0],
        small[1],
        jnp.stack([attn_grad[:, i * width : (i + 1) * width] for i in range(3)]),
        jnp.concatenate((shard_row(6 + n_t), shard_row(6 + 2 * n_t)))[:, :width],
        attn_grad[:, 3 * width :].T,
        small[5],
        small[2],
        small[3],
        one_grad,
        shard_row(6)[0],
        two_grad.T,
        small[4],
    )


def solution(mesh):
    return jax.shard_map(
        partial(on_device, mesh.shape["dp"], mesh.shape["tensor"]),
        mesh=mesh,
        in_specs=(
            P("dp", None, None),
            P(),
            P(),
            P(None, "dp", "tensor"),
            P(None, "tensor"),
            P("tensor", "dp"),
            P(),
            P(),
            P(),
            P("dp", "tensor"),
            P("tensor"),
            P("tensor", "dp"),
            P(),
            P("dp", None, None),
        ),
        out_specs=(
            P("dp", None, None),
            P("dp", None, None),
            P(),
            P(),
            P(None, "dp", "tensor"),
            P(None, "tensor"),
            P("tensor", "dp"),
            P(),
            P(),
            P(),
            P("dp", "tensor"),
            P("tensor"),
            P("tensor", "dp"),
            P(),
        ),
        check_vma=False,
    )
```

```python
from functools import partial

import jax
import jax.numpy as jnp
from jax import lax
from jax.experimental import pallas as pl
from jax.experimental.pallas import tpu as pltpu
from jax.sharding import PartitionSpec as P

HEAD_DIM = 64
EPS = 1e-06
AXES = ("dp", "tensor")
TILE = 16
ROWS = 32
MIB = 1024 * 1024
FACTOR = HEAD_DIM ** (-0.5)
bf16 = jnp.bfloat16
f32 = jnp.float32


class Cube:
    def __init__(self, n_dp, n_t, rows):
        self.n_dp, self.n_t, self.rows = n_dp, n_t, rows
        self.n = n_dp * n_t
        n_bits = self.n.bit_length() - 1
        self.fast = (1 << n_bits) == self.n and n_bits >= 4 and rows % TILE == 0
        far = list(range(n_bits - 1, 3, -1))
        self.gather = [
            ([2, 3, 1] + far, [1, 2, 3] + far),
            ([2, 3, 1] + far, [1, 3, 2] + far),
            ([2, 3, 1] + far, [1, 3, 2] + far),
        ]
        self.scatter = [
            ([2, 1, 3] + far, [1, 3, 2] + far),
            ([2, 3, 1] + far, [1, 3, 2] + far),
            ([2, 3, 1] + far, [1, 3, 2] + far),
        ]
        self.steps = 3 + len(far)
        self.half = self.n // 2

    def swap(self, orders, value, k):
        return lax.ppermute(value, AXES, [(i, i ^ (1 << orders[i & 1][k])) for i in range(self.n)])

    def flip(self, value, bits):
        return lax.ppermute(value, AXES, [(i, i ^ bits) for i in range(self.n)])

    def at(self, orders, ids_ref, core, y, block):
        relative = ((ids_ref[0] ^ block) << 2) | (y << 1)
        found = []
        for order in orders:
            place = 0
            for k, bit in enumerate(order[::-1]):
                place = place | (((relative >> bit) & 1) << k)
            found.append(place)
        return jnp.where((ids_ref[1] & 1) == core, found[0], found[1])

    def buffers(self, cols):
        blocks = (2, self.half, self.rows, cols) if self.fast else (1, 1, 8, 128)
        shard = pltpu.VMEM((self.n_dp * self.rows, cols), bf16)
        return [pltpu.VMEM(blocks, bf16), shard, pltpu.SemaphoreType.DMA((4,))]

    def fetch(self, refs, scratch):
        if not self.fast:
            return lambda core: None
        held, _, sems = scratch
        part = self.half // 2
        copies = [
            pltpu.make_async_copy(refs[i], held.at[i // 2, pl.ds(i % 2 * part, part)], sems.at[i])
            for i in range(4)
        ]
        for copy in copies:
            copy.start()

        def wait(core):
            copies[2 * core].wait()
            copies[2 * core + 1].wait()

        return wait

    def load(self, group, ids_ref, refs, scratch, core, y):
        held, shard, sems = scratch
        if not self.fast:
            copy = pltpu.make_async_copy(refs[0].at[2 * y + core], shard, sems.at[0])
            copy.start()
            copy.wait()
            return
        for d in range(self.n_dp):
            rows = slice(d * self.rows, (d + 1) * self.rows)
            shard[rows, :] = held[core, self.at(self.gather[group], ids_ref, core, y, d)]

    def grad_buffers(self, cols):
        shape = self.grad_shape(cols).shape
        return [pltpu.VMEM((2,) + shape, bf16), pltpu.SemaphoreType.DMA((2,))]

    def store(self, group, ids_ref, scratch, core, y, value):
        if not self.fast:
            scratch[0][core, y] = value
            return
        for d in range(self.n_dp):
            rows = value[d * self.rows : (d + 1) * self.rows]
            scratch[0][core, self.at(self.scatter[group], ids_ref, core, y, d)] = rows

    def send_out(self, scratch, core, ref):
        copy = pltpu.make_async_copy(scratch[0].at[core], ref, scratch[1].at[core])
        copy.start()
        return copy

    def grad_shape(self, cols):
        if not self.fast:
            return jax.ShapeDtypeStruct((2, self.n_dp * self.rows, cols), bf16)
        return jax.ShapeDtypeStruct((self.half, self.rows, cols), bf16)


def gather_plain(cube, piece):
    rows, cols = piece.shape
    whole = lax.all_gather(piece, AXES, axis=0, tiled=False)
    whole = whole.reshape(cube.n_dp, cube.n_t, rows, cols).transpose(1, 0, 2, 3)
    whole = whole.reshape(cube.n_t, cube.n_dp * rows, cols)
    return [jnp.take(whole, lax.axis_index("tensor") ^ jnp.arange(cube.n_t), axis=0)]


def scatter_plain(cube, own, other):
    n_t, n_dp, rows, cols = cube.n_t, cube.n_dp, cube.rows, own.shape[2]
    part = jnp.stack((own, other), axis=1).reshape(n_t, n_dp * rows, cols)
    part = jnp.take(part, lax.axis_index("tensor") ^ jnp.arange(n_t), axis=0)
    part = part.reshape(n_t, n_dp, rows, cols).transpose(1, 0, 2, 3)
    part = part.reshape(n_dp * n_t * rows, cols)
    return lax.psum_scatter(part, AXES, scatter_dimension=0, tiled=True).astype(f32)


def join(pairs, after=()):
    def kernel(*refs):
        outs = refs[2 * len(pairs) + len(after) :]
        for i, out in enumerate(outs):
            size = pairs[i][0].shape[0]
            out[:size] = refs[2 * i][...]
            out[size:] = refs[2 * i + 1][...]

    shapes = [
        jax.ShapeDtypeStruct((2 * p[0].shape[0],) + p[0].shape[1:], p[0].dtype) for p in pairs
    ]
    return plain_call(kernel, shapes, [x for p in pairs for x in p], after)


def fold(pairs, after=()):
    shapes = []
    for a, _ in pairs:
        shapes += [jax.ShapeDtypeStruct((a.shape[0] // 2,) + a.shape[1:], bf16)] * 2
    n_in = 2 * len(pairs)

    def kernel(*refs):
        outs = refs[n_in + len(after) :]
        for i in range(len(pairs)):
            size = shapes[2 * i].shape[0]
            for part in range(2):
                add_rows(outs[2 * i + part], refs[2 * i : 2 * i + 2], (1 - part) * size)

    found = vmem_call(kernel, shapes, [x for p in pairs for x in p], after)
    return [found[2 * i : 2 * i + 2] for i in range(len(pairs))]


def add_rows(out_ref, refs, start):
    size, rows, _ = out_ref.shape

    def step(i, carry):
        for c in range(0, rows, ROWS):
            at = (i, slice(c, c + ROWS), slice(None))
            source = (start + i, slice(c, c + ROWS), slice(None))
            value = refs[0][source].astype(f32)
            for ref in refs[1:]:
                value = value + ref[source].astype(f32)
            out_ref[at] = value.astype(out_ref.dtype)
        return carry

    lax.fori_loop(0, size, step, 0)


def vmem_call(kernel, shapes, inputs, after, ids=None, scratch=()):
    specs = [pl.BlockSpec(memory_space=pltpu.VMEM)] * len(inputs)
    specs += [pl.BlockSpec(memory_space=pl.ANY)] * len(after)
    values = [*inputs, *after]
    if ids is not None:
        specs = [pl.BlockSpec(memory_space=pltpu.SMEM), *specs]
        values = [ids, *values]
    return pl.pallas_call(
        kernel,
        out_shape=shapes,
        in_specs=specs,
        out_specs=[pl.BlockSpec(memory_space=pltpu.VMEM)] * len(shapes),
        scratch_shapes=list(scratch),
        compiler_params=pltpu.CompilerParams(vmem_limit_bytes=48 * MIB),
        cost_estimate=pl.CostEstimate(flops=0, bytes_accessed=1024, transcendentals=0),
    )(*values)


def plain_call(kernel, shapes, inputs, after):
    specs = [pl.BlockSpec(x.shape, lambda i: (0, 0, 0)) for x in inputs]
    return pl.pallas_call(
        kernel,
        grid=(1,),
        out_shape=shapes,
        in_specs=specs + [pl.BlockSpec(memory_space=pl.ANY)] * len(after),
        out_specs=[pl.BlockSpec(x.shape, lambda i, n=len(x.shape): (0,) * n) for x in shapes],
        compiler_params=pltpu.CompilerParams(vmem_limit_bytes=48 * MIB),
        cost_estimate=pl.CostEstimate(flops=0, bytes_accessed=1024, transcendentals=0),
    )(*inputs, *after)


def fold_with_small(cube, kept, came, small, pairs, finals, ids, after=()):
    first = len(small) > 1
    size, d = kept.shape[0] // 2, kept.shape[1]
    shapes = [
        jax.ShapeDtypeStruct((size + ROWS, d), bf16),
        jax.ShapeDtypeStruct((size, d), bf16),
        jax.ShapeDtypeStruct((ROWS, d), bf16),
    ]
    for a, _ in pairs:
        shapes += [jax.ShapeDtypeStruct((a.shape[0] // 2,) + a.shape[1:], bf16)] * 2
    shapes += [jax.ShapeDtypeStruct(a.shape[1:], f32) for a, _ in finals]
    others = [x for p in [*pairs, *finals] for x in p]

    def kernel(ids_ref, kept_ref, came_ref, *refs):
        extra, refs = refs[: len(small)], refs[len(small) :]
        ins, outs = refs[: len(others)], refs[len(others) + len(after) :]
        send_ref, keep_ref, low_ref = outs[:3]
        total_ref = outs[-1]
        for n in range(len(pairs)):
            for part in range(2):
                out_ref = outs[3 + 2 * n + part]
                add_rows(out_ref, ins[2 * n : 2 * n + 2], (1 - part) * out_ref.shape[0])
        for n in range(len(pairs), len(pairs) + len(finals)):
            total = ins[2 * n][0].astype(f32) + ins[2 * n + 1][0].astype(f32)
            outs[3 + len(pairs) + n][...] = total

        def step(i, carry):
            at = pl.ds(pl.multiple_of(i * ROWS, ROWS), ROWS)
            there = pl.ds(pl.multiple_of(size + i * ROWS, ROWS), ROWS)
            sent = kept_ref[there, :].astype(f32) + came_ref[there, :].astype(f32)
            send_ref[at, :] = sent.astype(bf16)
            keep_ref[at, :] = (kept_ref[at, :].astype(f32) + came_ref[at, :].astype(f32)).astype(bf16)
            return carry

        lax.fori_loop(0, size // ROWS, step, 0)
        if first:
            gather_small(cube, ids_ref, extra, total_ref)
        else:
            total_ref[...] = extra[0][...].astype(f32) + came_ref[2 * size :, :].astype(f32)
        low = total_ref[...].astype(bf16)
        send_ref[size:, :] = low
        low_ref[...] = low

    return vmem_call(
        kernel, shapes, [kept, came, *small, *others], after, ids, [pltpu.VMEM((ROWS, d), f32)]
    )


def gather_small(cube, ids_ref, refs, out_ref):
    attn_ref, mlp_ref = refs[:2]
    out_ref[...] = jnp.zeros_like(out_ref)
    for i in range(2):
        out_ref[i : i + 1, :] = attn_ref[i]
    for i in range(4):
        out_ref[2 + i : 3 + i, :] = mlp_ref[i]
    n_t = cube.n_t
    for relative in range(n_t):
        t = relative ^ ids_ref[1]
        dbias = refs[2][relative]
        width = dbias.shape[1] // 3
        out_ref[pl.ds(6 + t, 1), :] = refs[3][relative]
        out_ref[pl.ds(6 + n_t + t, 1), :width] = dbias[:, :width]
        out_ref[pl.ds(6 + 2 * n_t + t, 1), :width] = dbias[:, 2 * width :]


def finish_with_small(kept, came, small, after=()):
    rows, d = kept.shape

    def kernel(kept_ref, came_ref, small_ref, *refs):
        outs = refs[len(after) :]
        outs[0][...] = kept_ref[...].astype(f32) + came_ref[:rows, :].astype(f32)
        outs[1][...] = (small_ref[...].astype(f32) + came_ref[rows:, :].astype(f32)).astype(bf16)

    shapes = [jax.ShapeDtypeStruct((rows, d), f32), jax.ShapeDtypeStruct(small.shape, bf16)]
    return vmem_call(kernel, shapes, [kept, came, small], after)


def hold(values, after):
    n = len(values)

    def kernel(*refs):
        pass

    return pl.pallas_call(
        kernel,
        out_shape=[jax.ShapeDtypeStruct(v.shape, v.dtype) for v in values],
        in_specs=[pl.BlockSpec(memory_space=pl.ANY)] * (n + len(after)),
        out_specs=[pl.BlockSpec(memory_space=pl.ANY)] * n,
        input_output_aliases={i: i for i in range(n)},
        cost_estimate=pl.CostEstimate(flops=0, bytes_accessed=1024, transcendentals=0),
    )(*values, *after)


def place_images(cube, pieces, length, after=()):
    if not cube.fast:
        return lax.all_gather(pieces[0][:, :length], "tensor", axis=0, tiled=True)
    count = pieces[0].shape[0]
    index = lax.axis_index("tensor").astype(jnp.int32).reshape(1)

    def kernel(index_ref, *refs):
        out_ref, ordered = refs[4:]
        for r in range(4):
            for i in range(count):
                ordered[(index_ref[0] ^ r) * count + i] = refs[r][i]
        out_ref[...] = jnp.swapaxes(ordered[...], 0, 1)[:length]

    shape = (length, 4 * count, pieces[0].shape[2])
    ordered = pltpu.VMEM((4 * count,) + pieces[0].shape[1:], bf16)
    out = call(kernel, [jax.ShapeDtypeStruct(shape, bf16)], index, pieces, [], [ordered], after)[0]
    return out.transpose(1, 0, 2)


def call(kernel, out_shapes, index, inputs, weights, scratch, after=(), grads=()):
    out_shapes = [*out_shapes, jax.ShapeDtypeStruct((8, 128), f32)]
    n_in, n_w, n_out = len(inputs), len(weights), len(out_shapes)
    spots = [pl.BlockSpec(memory_space=pltpu.VMEM)] * n_out
    spots += [pl.BlockSpec(memory_space=pltpu.HBM)] * len(grads)

    def body(index_ref, *refs):
        rest = refs[n_in + n_w + len(after) :]
        rest[n_out - 1][...] = jnp.zeros((8, 128), f32)
        kernel(index_ref, *refs[: n_in + n_w], *rest[: n_out - 1], *rest[n_out:])

    return pl.pallas_call(
        body,
        out_shape=[*out_shapes, *grads],
        in_specs=[pl.BlockSpec(memory_space=pltpu.SMEM)]
        + [pl.BlockSpec(memory_space=pltpu.VMEM)] * n_in
        + [pl.BlockSpec(memory_space=pltpu.HBM)] * n_w
        + [pl.BlockSpec(memory_space=pl.ANY)] * len(after),
        out_specs=spots,
        scratch_shapes=scratch,
        compiler_params=pltpu.CompilerParams(vmem_limit_bytes=56 * MIB),
        cost_estimate=pl.CostEstimate(flops=0, bytes_accessed=1024, transcendentals=0),
    )(index, *inputs, *weights, *after)


def nn(left, right):
    return lax.dot_general(left, right, (((1,), (0,)), ((), ())), preferred_element_type=f32)


def nt(left, right):
    return lax.dot_general(left, right, (((1,), (1,)), ((), ())), preferred_element_type=f32)


def tn(left, right):
    return lax.dot_general(left, right, (((0,), (0,)), ((), ())), preferred_element_type=f32)


def normed_of(values):
    centre = values - jnp.mean(values, -1, keepdims=True)
    inverse = lax.rsqrt(jnp.mean(centre * centre, -1, keepdims=True) + EPS)
    return (centre * inverse, inverse)


def norm_back(upstream, normed, inverse, gain):
    scaled = upstream * gain
    inner = (
        scaled
        - jnp.mean(scaled, -1, keepdims=True)
        - normed * jnp.mean(scaled * normed, -1, keepdims=True)
    )
    return inverse * inner


def column_sum(values):
    return jnp.sum(values, 0, keepdims=True)


def attend_kernel(cube, count, length, width, n_w, ids_ref, *refs):
    x_ref, vec_ref, bias_ref = refs[:3]
    w_refs = refs[3 : 3 + n_w]
    n1_ref, qkv_ref, att_ref, sum_ref, n2_ref = refs[3 + n_w : 8 + n_w]
    scratch = refs[8 + n_w :]
    wait = cube.fetch(w_refs, scratch)
    x = x_ref[...].astype(f32)
    normed, _ = normed_of(x)
    n1_ref[...] = (normed * vec_ref[0:1] + vec_ref[1:2]).astype(bf16)
    sum_ref[...] = x + vec_ref[2:3]
    tokens = x_ref.shape[0] // count
    heads = width // HEAD_DIM
    keep = lax.broadcasted_iota(jnp.int32, (tokens, tokens), 1) < length
    w_ref = scratch[1]

    for core in range(2):
        wait(core)

        def step(y, carry):
            t = 2 * y + core
            cube.load(0, ids_ref, w_refs, scratch, core, y)
            qkv = nn(n1_ref[...], w_ref[:, : 3 * width]) + bias_ref[t]
            qkv_ref[t] = qkv.astype(bf16)
            for b in range(count):
                rows = slice(b * tokens, (b + 1) * tokens)
                found = []
                for h in range(heads):
                    q = qkv_ref[t, rows, h * HEAD_DIM : (h + 1) * HEAD_DIM]
                    k = qkv_ref[t, rows, width + h * HEAD_DIM : width + (h + 1) * HEAD_DIM]
                    v = qkv_ref[t, rows, 2 * width + h * HEAD_DIM : 2 * width + (h + 1) * HEAD_DIM]
                    scores = jnp.where(keep, nt(q, k) * FACTOR, -1e30)
                    weights = jnp.exp(scores - jnp.max(scores, -1, keepdims=True))
                    probs = weights * (1.0 / jnp.sum(weights, -1, keepdims=True))
                    found.append(nn(probs.astype(bf16), v).astype(bf16))
                att_ref[t, rows, :] = jnp.concatenate(found, axis=1)
            sum_ref[...] += nt(att_ref[t], w_ref[:, 3 * width :])
            return carry

        lax.fori_loop(0, cube.n_t // 2, step, 0)
    normed, _ = normed_of(sum_ref[...])
    n2_ref[...] = (normed * vec_ref[3:4] + vec_ref[4:5]).astype(bf16)


def gelu_kernel(cube, n_w, ids_ref, *refs):
    n2_ref, cot_ref, bias_ref = refs[:3]
    w_refs = refs[3 : 3 + n_w]
    act_ref, slope_ref = refs[3 + n_w : 5 + n_w]
    grad_refs = refs[5 + n_w : 7 + n_w]
    scratch, grads = refs[7 + n_w : 10 + n_w], refs[10 + n_w :]
    wait = cube.fetch(w_refs, scratch)
    copies = []
    for core in range(2):
        wait(core)

        def step(y, carry):
            t = 2 * y + core
            cube.load(1, ids_ref, w_refs, scratch, core, y)
            pre = nn(n2_ref[...], scratch[1][...]) + bias_ref[t]
            cdf = 0.5 * (1.0 + lax.erf(pre * (0.5**0.5)))
            slope = cdf + pre * (jnp.exp(-0.5 * pre * pre) * 0.3989422804014327)
            act_ref[t] = (pre * cdf).astype(bf16)
            slope_ref[t] = slope.astype(bf16)
            cube.store(2, ids_ref, grads, core, y, tn(cot_ref[...], act_ref[t]).astype(bf16))
            return carry

        lax.fori_loop(0, cube.n_t // 2, step, 0)
        copies.append(cube.send_out(grads, core, grad_refs[core]))
    for copy in copies:
        copy.wait()


def mlp_kernel(cube, n_w, ids_ref, *refs):
    n2_ref, cot_ref, act_ref, slope_ref, hidden_ref, vec_ref = refs[:6]
    one_refs, two_refs = refs[6 : 6 + n_w], refs[6 + n_w : 6 + 2 * n_w]
    outs = refs[6 + 2 * n_w :]
    sums_ref, enc_ref, dhidden_ref, small_ref = outs[:4]
    grad_refs = outs[4:6]
    one, two, grads = outs[6:9], outs[9:12], outs[12:14]
    mlp_ref, dnorm_ref = outs[14:]
    waits = [cube.fetch(one_refs, one), cube.fetch(two_refs, two)]
    mlp_ref[...] = hidden_ref[...] + vec_ref[5:6]
    dnorm_ref[...] = jnp.zeros_like(dnorm_ref)
    copies = []
    for core in range(2):
        for wait in waits:
            wait(core)

        def step(y, carry):
            t = 2 * y + core
            cube.load(1, ids_ref, one_refs, one, core, y)
            cube.load(2, ids_ref, two_refs, two, core, y)
            dact = nn(cot_ref[...], two[1][...])
            dpre = (slope_ref[t].astype(f32) * dact).astype(bf16)
            sums_ref[pl.ds(t, 1)] = column_sum(dpre.astype(f32))[None]
            cube.store(1, ids_ref, grads, core, y, tn(n2_ref[...], dpre).astype(bf16))
            dnorm_ref[...] += nt(dpre, one[1][...])
            mlp_ref[...] += nt(act_ref[t], two[1][...])
            return carry

        lax.fori_loop(0, cube.n_t // 2, step, 0)
        copies.append(cube.send_out(grads, core, grad_refs[core]))
    enc_ref[...] = mlp_ref[...].astype(bf16)
    normed, inverse = normed_of(hidden_ref[...])
    dnorm = dnorm_ref[...]
    cot = cot_ref[...].astype(f32)
    dhidden = cot + norm_back(dnorm, normed, inverse, vec_ref[3:4])
    dhidden_ref[...] = dhidden
    small_ref[0] = column_sum(dnorm * normed)
    small_ref[1] = column_sum(dnorm)
    small_ref[2] = column_sum(cot)
    small_ref[3] = column_sum(dhidden)
    for copy in copies:
        copy.wait()


def attend_back_kernel(cube, count, length, width, n_w, ids_ref, *refs):
    x_ref, n1_ref, qkv_ref, att_ref, dhidden_ref, vec_ref = refs[:6]
    w_refs = refs[6 : 6 + n_w]
    outs = refs[6 + n_w :]
    dbias_ref, dnorm_ref, small_ref = outs[:3]
    grad_refs = outs[3:5]
    scratch, grads = outs[5:8], outs[8:10]
    low_ref, dqkv_ref = outs[10:]
    wait = cube.fetch(w_refs, scratch)
    low_ref[...] = dhidden_ref[...].astype(bf16)
    dnorm_ref[...] = jnp.zeros_like(dnorm_ref)
    tokens = x_ref.shape[0] // count
    heads = width // HEAD_DIM
    keep = lax.broadcasted_iota(jnp.int32, (tokens, tokens), 0) < length
    w_ref = scratch[1]
    copies = []
    for core in (1, 0):
        wait(core)

        def step(y, carry):
            t = 2 * y + core
            cube.load(0, ids_ref, w_refs, scratch, core, y)
            datt = nn(low_ref[...], w_ref[:, 3 * width :]).astype(bf16)
            for b in range(count):
                rows = slice(b * tokens, (b + 1) * tokens)
                dqs, dks, dvs = [], [], []
                for h in range(heads):
                    q = qkv_ref[t, rows, h * HEAD_DIM : (h + 1) * HEAD_DIM]
                    k = qkv_ref[t, rows, width + h * HEAD_DIM : width + (h + 1) * HEAD_DIM]
                    v = qkv_ref[t, rows, 2 * width + h * HEAD_DIM : 2 * width + (h + 1) * HEAD_DIM]
                    do = datt[rows, h * HEAD_DIM : (h + 1) * HEAD_DIM]
                    scores = jnp.where(keep, nt(k, q) * FACTOR, -1e30)
                    weights = jnp.exp(scores - jnp.max(scores, 0, keepdims=True))
                    probs = weights * (1.0 / jnp.sum(weights, 0, keepdims=True))
                    dvs.append(nn(probs.astype(bf16), do))
                    dprobs = nt(v, do)
                    inner = jnp.sum(dprobs * probs, 0, keepdims=True)
                    dscores = (probs * (dprobs - inner)).astype(bf16)
                    dks.append(nn(dscores, q) * FACTOR)
                    dqs.append(tn(dscores, k) * FACTOR)
                dqkv_ref[rows, :] = jnp.concatenate(dqs + dks + dvs, axis=1).astype(bf16)
            dqkv = dqkv_ref[...]
            dbias_ref[pl.ds(t, 1)] = column_sum(dqkv.astype(f32))[None]
            dnorm_ref[...] += nt(dqkv, w_ref[:, : 3 * width])
            grad = jnp.concatenate((tn(n1_ref[...], dqkv), tn(low_ref[...], att_ref[t])), axis=1)
            cube.store(0, ids_ref, grads, core, y, grad.astype(bf16))
            return carry

        lax.fori_loop(0, cube.n_t // 2, step, 0)
        copies.append(cube.send_out(grads, core, grad_refs[core]))
    normed, _ = normed_of(x_ref[...].astype(f32))
    dnorm = dnorm_ref[...]
    small_ref[0] = column_sum(dnorm * normed)
    small_ref[1] = column_sum(dnorm)
    for copy in copies:
        copy.wait()


def patch_kernel(ids_ref, x_ref, dhidden_ref, dnorm_ref, vec_ref, patch_ref):
    normed, inverse = normed_of(x_ref[...].astype(f32))
    patch = dhidden_ref[...] + norm_back(dnorm_ref[...], normed, inverse, vec_ref[0:1])
    patch_ref[...] = patch.astype(bf16)


def on_device(
    n_dp,
    n_t,
    patches,
    attn_gain,
    attn_shift,
    qkv_weight,
    qv_bias,
    out_weight,
    out_bias,
    mlp_gain,
    mlp_shift,
    fc1_weight,
    fc1_bias,
    fc2_weight,
    fc2_bias,
    cotangent,
):
    t_me = lax.axis_index("tensor")
    cube = Cube(n_dp, n_t, qkv_weight.shape[1])
    order = t_me ^ jnp.arange(n_t)
    width = qkv_weight.shape[2]
    f_width = fc1_weight.shape[1]
    d = patches.shape[2]
    ids = jnp.stack((lax.axis_index("dp"), t_me)).astype(jnp.int32)
    count = patches.shape[0] // n_t
    length = patches.shape[1]
    padded = -(-length // TILE) * TILE
    tokens = count * padded

    def own_images(values):
        mine = lax.dynamic_slice_in_dim(values, t_me * count, count, 0)
        return jnp.pad(mine, ((0, 0), (0, padded - length), (0, 0))).reshape(tokens, d)

    def shape(*dims, dtype=bf16):
        return jax.ShapeDtypeStruct(dims, dtype)

    attn_piece = jnp.concatenate(
        (qkv_weight[0], qkv_weight[1], qkv_weight[2], out_weight.T), axis=1
    )
    two_piece = fc2_weight.T
    biases = jnp.concatenate((qv_bias.reshape(-1), fc1_bias))[None]
    x = own_images(patches)
    cot = own_images(cotangent)
    vecs = jnp.stack((attn_gain, attn_shift, out_bias, mlp_gain, mlp_shift, fc2_bias)).astype(f32)

    def bias_parts(biases):
        biases = biases.astype(f32)
        zeros = jnp.zeros((n_t, width), f32)
        qkv = (biases[:, :width], zeros, biases[:, width : 2 * width])
        return (jnp.concatenate(qkv, axis=1)[:, None], biases[:, None, 2 * width :])

    last = cube.steps - 1
    if cube.fast:
        held = attn_piece[None]
        one = fc1_weight[None]
        two = two_piece[None]
        (biases,) = hold([biases], (x,))
        biases = [biases] + [cube.flip(biases, r) for r in range(1, n_t)]
        qkv_bias, f_bias = bias_parts(jnp.concatenate(biases))
        for k in range(last, 0, -1):
            pairs = [(held, cube.swap(cube.gather[0], held, k))]
            if k < last:
                pairs.append((one, cube.swap(cube.gather[1], one, k + 1)))
            if k < last - 1:
                pairs.append((two, cube.swap(cube.gather[2], two, k + 2)))
            tokens_in = ((x, cot), (qkv_bias, f_bias), (vecs,))[min(last - k, 2)]
            found = join(pairs, tokens_in)
            held = found[0]
            one = found[1] if k < last else one
            two = found[2] if k < last - 1 else two
        came = cube.swap(cube.gather[0], held, 0)
        pairs = [(one, cube.swap(cube.gather[1], one, 1)), (two, cube.swap(cube.gather[2], two, 2))]
        w_attn = [held, came, cube.flip(held, 1), cube.flip(came, 1)]
        one, two = join(pairs, (came,))
        slot = (one, two)
    else:
        w_attn = gather_plain(cube, attn_piece)
        w_one = gather_plain(cube, fc1_weight)
        w_two = gather_plain(cube, two_piece)
        biases = jnp.take(lax.all_gather(biases[0], "tensor", axis=0, tiled=False), order, axis=0)
        qkv_bias, f_bias = bias_parts(biases)
        slot = ()
    n_w = len(w_attn)
    buffers = cube.buffers(d)
    grad_buffers = cube.grad_buffers(d)
    grad_shapes = [cube.grad_shape(d)] * 2

    n1, qkv, att, hidden, n2, done = call(
        partial(attend_kernel, cube, count, length, width, n_w),
        [
            shape(tokens, d),
            shape(n_t, tokens, 3 * width),
            shape(n_t, tokens, width),
            shape(tokens, d, dtype=f32),
            shape(tokens, d),
        ],
        ids,
        [x, vecs, qkv_bias],
        w_attn,
        buffers,
        slot,
    )
    if cube.fast:
        came, there = hold(
            [cube.swap(cube.gather[1], one, 0), cube.swap(cube.gather[2], two, 1)], (done,)
        )
        w_one = [one, came, cube.flip(one, 1), cube.flip(came, 1)]
        (two,) = join([(two, there)])
        slot = (two,)
    act, slope, done, *two_grads = call(
        partial(gelu_kernel, cube, n_w),
        [shape(n_t, tokens, f_width)] * 2,
        ids,
        [n2, cot, f_bias],
        w_one,
        buffers + grad_buffers,
        slot,
        grad_shapes,
    )
    if cube.fast:
        came, other = hold([cube.swap(cube.gather[2], two, 0), two_grads[1]], (done,))
        w_two = [two, came, cube.flip(two, 1), cube.flip(came, 1)]
        ((s_two, k_two),) = fold([(two_grads[0], cube.flip(other, 1))])
        c_two = cube.swap(cube.scatter[2], s_two, 0)
        slot = (s_two,)
    f_sums, enc, dhidden, mlp_small, done, *one_grads = call(
        partial(mlp_kernel, cube, n_w),
        [
            shape(n_t, 1, f_width, dtype=f32),
            shape(tokens, d),
            shape(tokens, d, dtype=f32),
            shape(4, 1, d, dtype=f32),
        ],
        ids,
        [n2, cot, act, slope, hidden, vecs],
        [*w_one, *w_two],
        buffers * 2 + grad_buffers + [pltpu.VMEM((tokens, d), f32)] * 2,
        slot,
        grad_shapes,
    )
    slot = ()
    if cube.fast:
        images = enc.reshape(count, padded, d)
        c_two, other, images = hold([c_two, one_grads[1], images], (done,))
        ((s_two, k_two),) = fold([(k_two, c_two)])
        c_two = cube.swap(cube.scatter[2], s_two, 1)
        ((s_one, k_one),) = fold([(one_grads[0], cube.flip(other, 1))], (s_two,))
        slot = (s_two, s_one)
    dbias, dnorm, attn_small, done, *attn_grads = call(
        partial(attend_back_kernel, cube, count, length, width, n_w),
        [
            shape(n_t, 1, 3 * width, dtype=f32),
            shape(tokens, d, dtype=f32),
            shape(2, 1, d, dtype=f32),
        ],
        ids,
        [x, n1, qkv, att, dhidden, vecs],
        w_attn,
        buffers
        + grad_buffers
        + [pltpu.VMEM((tokens, d), bf16), pltpu.VMEM((tokens, 3 * width), bf16)],
        slot,
        grad_shapes,
    )

    def patch_of(after):
        patch = call(
            patch_kernel, [shape(tokens, d)], ids, [x, dhidden, dnorm, vecs], [], [], after
        )[0]
        return patch.reshape(count, padded, d)

    sums = (attn_small, mlp_small, dbias, f_sums)
    if cube.fast:

        def spread(images, there):
            return [images, cube.flip(images, 1), there, cube.flip(there, 1)]

        c_one = cube.swap(cube.scatter[1], s_one, 0)
        there = cube.flip(images, 2)
        flat = (cube.half * cube.rows, d)
        other, images, there, c_two, c_one = hold(
            [attn_grads[1].reshape(flat), images, there, c_two, c_one], (done,)
        )
        k_attn, c_attn = attn_grads[0].reshape(flat), cube.flip(other, 1)
        waiting = {2: [2, k_two, c_two], 1: [1, k_one, c_one]}
        grads = {}
        found = fold([(k, c) for _, k, c in waiting.values()])
        for (group, state), (sent, kept) in zip(waiting.items(), found):
            state[1:] = [kept, cube.swap(cube.scatter[group], sent, state[0])]
            state[0] += 1
        small, after = sums, (found[0][0],)
        for k in range(cube.steps):
            more = [g for g in waiting if k > 0 and waiting[g][0] <= last]
            ended = [g for g in waiting if k > 0 and waiting[g][0] > last]
            pairs = [waiting[g][1:] for g in more]
            finals = [waiting.pop(g)[1:] for g in ended]
            s_attn, k_attn, small, *found = fold_with_small(
                cube, k_attn, c_attn, small, pairs, finals, ids, after
            )
            c_attn = cube.swap(cube.scatter[0], s_attn, k)
            for n, g in enumerate(more):
                came = cube.swap(cube.scatter[g], found[2 * n], waiting[g][0])
                waiting[g] = [waiting[g][0] + 1, found[2 * n + 1], came]
            grads.update(zip(ended, found[2 * len(more) :]))
            after = ()
            if k == 0:
                images, there = hold([images, there], (small,))
                encoded = place_images(cube, spread(images, there), length)
                after = (encoded,)
            if k == 1:
                images = patch_of((small,))
                after = (images,)
            if k == last - 1:
                (images,) = hold([images], (small,))
                there = cube.flip(images, 2)
            if k == last:
                images, there = hold([images, there], (small,))
                patch_grad = place_images(cube, spread(images, there), length)
            small = (small,)
        two_grad, one_grad = grads[2], grads[1]
        attn_grad, small = finish_with_small(k_attn, c_attn, small[0], (patch_grad,))
        small = small.astype(f32) + cube.flip(small, 1).astype(f32)
    else:
        two_grad = scatter_plain(cube, *two_grads)
        one_grad = scatter_plain(cube, *one_grads)
        attn_grad = scatter_plain(cube, *attn_grads)
        encoded = place_images(cube, [enc.reshape(count, padded, d)], length)
        patch_grad = place_images(cube, [patch_of(())], length)

        def collect(ids_ref, *refs):
            gather_small(cube, ids_ref, refs[:4], refs[4])

        small = call(collect, [shape(ROWS, d, dtype=f32)], ids, sums, [], [])[0]
        small = lax.psum(small, AXES)

    def shard_row(at):
        return lax.dynamic_slice_in_dim(small, at + t_me, 1, 0)

    return (
        encoded,
        patch_grad,
        small[0],
        small[1],
        jnp.stack([attn_grad[:, i * width : (i + 1) * width] for i in range(3)]),
        jnp.concatenate((shard_row(6 + n_t), shard_row(6 + 2 * n_t)))[:, :width],
        attn_grad[:, 3 * width :].T,
        small[5],
        small[2],
        small[3],
        one_grad,
        shard_row(6)[0],
        two_grad.T,
        small[4],
    )


def solution(mesh):
    return jax.shard_map(
        partial(on_device, mesh.shape["dp"], mesh.shape["tensor"]),
        mesh=mesh,
        in_specs=(
            P("dp", None, None),
            P(),
            P(),
            P(None, "dp", "tensor"),
            P(None, "tensor"),
            P("tensor", "dp"),
            P(),
            P(),
            P(),
            P("dp", "tensor"),
            P("tensor"),
            P("tensor", "dp"),
            P(),
            P("dp", None, None),
        ),
        out_specs=(
            P("dp", None, None),
            P("dp", None, None),
            P(),
            P(),
            P(None, "dp", "tensor"),
            P(None, "tensor"),
            P("tensor", "dp"),
            P(),
            P(),
            P(),
            P("dp", "tensor"),
            P("tensor"),
            P("tensor", "dp"),
            P(),
        ),
        check_vma=False,
    )
```

```python
from functools import partial

import jax
import jax.numpy as jnp
from jax import lax
from jax.experimental import pallas as pl
from jax.experimental.pallas import tpu as pltpu
from jax.sharding import PartitionSpec as P

HEAD_DIM = 64
EPS = 1e-06
AXES = ("dp", "tensor")
TILE = 16
ROWS = 32
MIB = 1024 * 1024
FACTOR = HEAD_DIM ** (-0.5)
bf16 = jnp.bfloat16
f32 = jnp.float32


class Cube:
    def __init__(self, n_dp, n_t, rows):
        self.n_dp, self.n_t, self.rows = n_dp, n_t, rows
        self.n = n_dp * n_t
        n_bits = self.n.bit_length() - 1
        self.fast = (1 << n_bits) == self.n and n_bits >= 4 and rows % TILE == 0
        far = list(range(n_bits - 1, 3, -1))
        self.gather = [
            ([2, 3, 1] + far, [1, 2, 3] + far),
            ([2, 3, 1] + far, [1, 3, 2] + far),
            ([2, 3, 1] + far, [1, 3, 2] + far),
        ]
        self.scatter = [
            ([2, 1, 3] + far, [1, 3, 2] + far),
            ([2, 3, 1] + far, [1, 3, 2] + far),
            ([2, 3, 1] + far, [1, 3, 2] + far),
        ]
        self.steps = 3 + len(far)
        self.half = self.n // 2

    def swap(self, orders, value, k):
        return lax.ppermute(value, AXES, [(i, i ^ (1 << orders[i & 1][k])) for i in range(self.n)])

    def flip(self, value, bits):
        return lax.ppermute(value, AXES, [(i, i ^ bits) for i in range(self.n)])

    def at(self, orders, ids_ref, core, y, block):
        relative = ((ids_ref[0] ^ block) << 2) | (y << 1)
        found = []
        for order in orders:
            place = 0
            for k, bit in enumerate(order[::-1]):
                place = place | (((relative >> bit) & 1) << k)
            found.append(place)
        return jnp.where((ids_ref[1] & 1) == core, found[0], found[1])

    def buffers(self, cols):
        blocks = (2, self.half, self.rows, cols) if self.fast else (1, 1, 8, 128)
        shard = pltpu.VMEM((self.n_dp * self.rows, cols), bf16)
        return [pltpu.VMEM(blocks, bf16), shard, pltpu.SemaphoreType.DMA((4,))]

    def fetch(self, refs, scratch):
        if not self.fast:
            return lambda core: None
        held, _, sems = scratch
        part = self.half // 2
        copies = [
            pltpu.make_async_copy(refs[i], held.at[i // 2, pl.ds(i % 2 * part, part)], sems.at[i])
            for i in range(4)
        ]
        for copy in copies:
            copy.start()

        def wait(core):
            copies[2 * core].wait()
            copies[2 * core + 1].wait()

        return wait

    def load(self, group, ids_ref, refs, scratch, core, y):
        held, shard, sems = scratch
        if not self.fast:
            copy = pltpu.make_async_copy(refs[0].at[2 * y + core], shard, sems.at[0])
            copy.start()
            copy.wait()
            return
        for d in range(self.n_dp):
            rows = slice(d * self.rows, (d + 1) * self.rows)
            shard[rows, :] = held[core, self.at(self.gather[group], ids_ref, core, y, d)]

    def grad_buffers(self, cols):
        shape = self.grad_shape(cols).shape
        return [pltpu.VMEM((2,) + shape, bf16), pltpu.SemaphoreType.DMA((2,))]

    def store(self, group, ids_ref, scratch, core, y, value):
        if not self.fast:
            scratch[0][core, y] = value
            return
        for d in range(self.n_dp):
            rows = value[d * self.rows : (d + 1) * self.rows]
            scratch[0][core, self.at(self.scatter[group], ids_ref, core, y, d)] = rows

    def send_out(self, scratch, core, ref):
        copy = pltpu.make_async_copy(scratch[0].at[core], ref, scratch[1].at[core])
        copy.start()
        return copy

    def grad_shape(self, cols):
        if not self.fast:
            return jax.ShapeDtypeStruct((2, self.n_dp * self.rows, cols), bf16)
        return jax.ShapeDtypeStruct((self.half, self.rows, cols), bf16)


def gather_plain(cube, piece):
    rows, cols = piece.shape
    whole = lax.all_gather(piece, AXES, axis=0, tiled=False)
    whole = whole.reshape(cube.n_dp, cube.n_t, rows, cols).transpose(1, 0, 2, 3)
    whole = whole.reshape(cube.n_t, cube.n_dp * rows, cols)
    return [jnp.take(whole, lax.axis_index("tensor") ^ jnp.arange(cube.n_t), axis=0)]


def scatter_plain(cube, own, other):
    n_t, n_dp, rows, cols = cube.n_t, cube.n_dp, cube.rows, own.shape[2]
    part = jnp.stack((own, other), axis=1).reshape(n_t, n_dp * rows, cols)
    part = jnp.take(part, lax.axis_index("tensor") ^ jnp.arange(n_t), axis=0)
    part = part.reshape(n_t, n_dp, rows, cols).transpose(1, 0, 2, 3)
    part = part.reshape(n_dp * n_t * rows, cols)
    return lax.psum_scatter(part, AXES, scatter_dimension=0, tiled=True).astype(f32)


def join(pairs, after=()):
    def kernel(*refs):
        outs = refs[2 * len(pairs) + len(after) :]
        for i, out in enumerate(outs):
            size = pairs[i][0].shape[0]
            out[:size] = refs[2 * i][...]
            out[size:] = refs[2 * i + 1][...]

    shapes = [
        jax.ShapeDtypeStruct((2 * p[0].shape[0],) + p[0].shape[1:], p[0].dtype) for p in pairs
    ]
    return plain_call(kernel, shapes, [x for p in pairs for x in p], after)


def fold(pairs, after=()):
    shapes = []
    for a, _ in pairs:
        shapes += [jax.ShapeDtypeStruct((a.shape[0] // 2,) + a.shape[1:], bf16)] * 2
    n_in = 2 * len(pairs)

    def kernel(*refs):
        outs = refs[n_in + len(after) :]
        for i in range(len(pairs)):
            size = shapes[2 * i].shape[0]
            for part in range(2):
                add_rows(outs[2 * i + part], refs[2 * i : 2 * i + 2], (1 - part) * size)

    found = vmem_call(kernel, shapes, [x for p in pairs for x in p], after)
    return [found[2 * i : 2 * i + 2] for i in range(len(pairs))]


def add_rows(out_ref, refs, start):
    size, rows, _ = out_ref.shape

    def step(i, carry):
        for c in range(0, rows, ROWS):
            at = (i, slice(c, c + ROWS), slice(None))
            source = (start + i, slice(c, c + ROWS), slice(None))
            value = refs[0][source].astype(f32)
            for ref in refs[1:]:
                value = value + ref[source].astype(f32)
            out_ref[at] = value.astype(out_ref.dtype)
        return carry

    lax.fori_loop(0, size, step, 0)


def vmem_call(kernel, shapes, inputs, after, ids=None, scratch=()):
    specs = [pl.BlockSpec(memory_space=pltpu.VMEM)] * len(inputs)
    specs += [pl.BlockSpec(memory_space=pl.ANY)] * len(after)
    values = [*inputs, *after]
    if ids is not None:
        specs = [pl.BlockSpec(memory_space=pltpu.SMEM), *specs]
        values = [ids, *values]
    return pl.pallas_call(
        kernel,
        out_shape=shapes,
        in_specs=specs,
        out_specs=[pl.BlockSpec(memory_space=pltpu.VMEM)] * len(shapes),
        scratch_shapes=list(scratch),
        compiler_params=pltpu.CompilerParams(vmem_limit_bytes=24 * MIB),
        cost_estimate=pl.CostEstimate(flops=0, bytes_accessed=1024, transcendentals=0),
    )(*values)


def plain_call(kernel, shapes, inputs, after):
    specs = [pl.BlockSpec(x.shape, lambda i: (0, 0, 0)) for x in inputs]
    return pl.pallas_call(
        kernel,
        grid=(1,),
        out_shape=shapes,
        in_specs=specs + [pl.BlockSpec(memory_space=pl.ANY)] * len(after),
        out_specs=[pl.BlockSpec(x.shape, lambda i, n=len(x.shape): (0,) * n) for x in shapes],
        compiler_params=pltpu.CompilerParams(vmem_limit_bytes=48 * MIB),
        cost_estimate=pl.CostEstimate(flops=0, bytes_accessed=1024, transcendentals=0),
    )(*inputs, *after)


def fold_with_small(cube, kept, came, small, pairs, finals, ids, after=()):
    first = len(small) > 1
    size, d = kept.shape[0] // 2, kept.shape[1]
    shapes = [
        jax.ShapeDtypeStruct((size + ROWS, d), bf16),
        jax.ShapeDtypeStruct((size, d), bf16),
        jax.ShapeDtypeStruct((ROWS, d), bf16),
    ]
    for a, _ in pairs:
        shapes += [jax.ShapeDtypeStruct((a.shape[0] // 2,) + a.shape[1:], bf16)] * 2
    shapes += [jax.ShapeDtypeStruct(a.shape[1:], f32) for a, _ in finals]
    others = [x for p in [*pairs, *finals] for x in p]

    def kernel(ids_ref, kept_ref, came_ref, *refs):
        extra, refs = refs[: len(small)], refs[len(small) :]
        ins, outs = refs[: len(others)], refs[len(others) + len(after) :]
        send_ref, keep_ref, low_ref = outs[:3]
        total_ref = outs[-1]
        for n in range(len(pairs)):
            for part in range(2):
                out_ref = outs[3 + 2 * n + part]
                add_rows(out_ref, ins[2 * n : 2 * n + 2], (1 - part) * out_ref.shape[0])
        for n in range(len(pairs), len(pairs) + len(finals)):
            total = ins[2 * n][0].astype(f32) + ins[2 * n + 1][0].astype(f32)
            outs[3 + len(pairs) + n][...] = total

        def step(i, carry):
            at = pl.ds(pl.multiple_of(i * ROWS, ROWS), ROWS)
            there = pl.ds(pl.multiple_of(size + i * ROWS, ROWS), ROWS)
            sent = kept_ref[there, :].astype(f32) + came_ref[there, :].astype(f32)
            send_ref[at, :] = sent.astype(bf16)
            keep_ref[at, :] = (kept_ref[at, :].astype(f32) + came_ref[at, :].astype(f32)).astype(bf16)
            return carry

        lax.fori_loop(0, size // ROWS, step, 0)
        if first:
            gather_small(cube, ids_ref, extra, total_ref)
        else:
            total_ref[...] = extra[0][...].astype(f32) + came_ref[2 * size :, :].astype(f32)
        low = total_ref[...].astype(bf16)
        send_ref[size:, :] = low
        low_ref[...] = low

    return vmem_call(
        kernel, shapes, [kept, came, *small, *others], after, ids, [pltpu.VMEM((ROWS, d), f32)]
    )


def gather_small(cube, ids_ref, refs, out_ref):
    attn_ref, mlp_ref = refs[:2]
    out_ref[...] = jnp.zeros_like(out_ref)
    for i in range(2):
        out_ref[i : i + 1, :] = attn_ref[i]
    for i in range(4):
        out_ref[2 + i : 3 + i, :] = mlp_ref[i]
    n_t = cube.n_t
    for relative in range(n_t):
        t = relative ^ ids_ref[1]
        dbias = refs[2][relative]
        width = dbias.shape[1] // 3
        out_ref[pl.ds(6 + t, 1), :] = refs[3][relative]
        out_ref[pl.ds(6 + n_t + t, 1), :width] = dbias[:, :width]
        out_ref[pl.ds(6 + 2 * n_t + t, 1), :width] = dbias[:, 2 * width :]


def finish_with_small(kept, came, small, after=()):
    rows, d = kept.shape

    def kernel(kept_ref, came_ref, small_ref, *refs):
        outs = refs[len(after) :]
        outs[0][...] = kept_ref[...].astype(f32) + came_ref[:rows, :].astype(f32)
        outs[1][...] = (small_ref[...].astype(f32) + came_ref[rows:, :].astype(f32)).astype(bf16)

    shapes = [jax.ShapeDtypeStruct((rows, d), f32), jax.ShapeDtypeStruct(small.shape, bf16)]
    return vmem_call(kernel, shapes, [kept, came, small], after)


def hold(values, after):
    n = len(values)

    def kernel(*refs):
        pass

    return pl.pallas_call(
        kernel,
        out_shape=[jax.ShapeDtypeStruct(v.shape, v.dtype) for v in values],
        in_specs=[pl.BlockSpec(memory_space=pl.ANY)] * (n + len(after)),
        out_specs=[pl.BlockSpec(memory_space=pl.ANY)] * n,
        input_output_aliases={i: i for i in range(n)},
        cost_estimate=pl.CostEstimate(flops=0, bytes_accessed=1024, transcendentals=0),
    )(*values, *after)


def place_images(cube, pieces, length, after=()):
    if not cube.fast:
        return lax.all_gather(pieces[0][:, :length], "tensor", axis=0, tiled=True)
    count = pieces[0].shape[0]
    index = lax.axis_index("tensor").astype(jnp.int32).reshape(1)

    def kernel(index_ref, *refs):
        out_ref, ordered = refs[4:]
        for r in range(4):
            for i in range(count):
                ordered[(index_ref[0] ^ r) * count + i] = refs[r][i]
        out_ref[...] = jnp.swapaxes(ordered[...], 0, 1)[:length]

    shape = (length, 4 * count, pieces[0].shape[2])
    ordered = pltpu.VMEM((4 * count,) + pieces[0].shape[1:], bf16)
    out = call(kernel, [jax.ShapeDtypeStruct(shape, bf16)], index, pieces, [], [ordered], after)[0]
    return out.transpose(1, 0, 2)


def call(kernel, out_shapes, index, inputs, weights, scratch, after=(), grads=()):
    out_shapes = [*out_shapes, jax.ShapeDtypeStruct((8, 128), f32)]
    n_in, n_w, n_out = len(inputs), len(weights), len(out_shapes)
    spots = [pl.BlockSpec(memory_space=pltpu.VMEM)] * n_out
    spots += [pl.BlockSpec(memory_space=pltpu.HBM)] * len(grads)

    def body(index_ref, *refs):
        rest = refs[n_in + n_w + len(after) :]
        rest[n_out - 1][...] = jnp.zeros((8, 128), f32)
        kernel(index_ref, *refs[: n_in + n_w], *rest[: n_out - 1], *rest[n_out:])

    return pl.pallas_call(
        body,
        out_shape=[*out_shapes, *grads],
        in_specs=[pl.BlockSpec(memory_space=pltpu.SMEM)]
        + [pl.BlockSpec(memory_space=pltpu.VMEM)] * n_in
        + [pl.BlockSpec(memory_space=pltpu.HBM)] * n_w
        + [pl.BlockSpec(memory_space=pl.ANY)] * len(after),
        out_specs=spots,
        scratch_shapes=scratch,
        compiler_params=pltpu.CompilerParams(vmem_limit_bytes=56 * MIB),
        cost_estimate=pl.CostEstimate(flops=0, bytes_accessed=1024, transcendentals=0),
    )(index, *inputs, *weights, *after)


def nn(left, right):
    return lax.dot_general(left, right, (((1,), (0,)), ((), ())), preferred_element_type=f32)


def nt(left, right):
    return lax.dot_general(left, right, (((1,), (1,)), ((), ())), preferred_element_type=f32)


def tn(left, right):
    return lax.dot_general(left, right, (((0,), (0,)), ((), ())), preferred_element_type=f32)


def normed_of(values):
    centre = values - jnp.mean(values, -1, keepdims=True)
    inverse = lax.rsqrt(jnp.mean(centre * centre, -1, keepdims=True) + EPS)
    return (centre * inverse, inverse)


def norm_back(upstream, normed, inverse, gain):
    scaled = upstream * gain
    inner = (
        scaled
        - jnp.mean(scaled, -1, keepdims=True)
        - normed * jnp.mean(scaled * normed, -1, keepdims=True)
    )
    return inverse * inner


def column_sum(values):
    return jnp.sum(values, 0, keepdims=True)


def attend_kernel(cube, count, length, width, n_w, ids_ref, *refs):
    x_ref, vec_ref, bias_ref = refs[:3]
    w_refs = refs[3 : 3 + n_w]
    n1_ref, qkv_ref, att_ref, sum_ref, n2_ref = refs[3 + n_w : 8 + n_w]
    scratch = refs[8 + n_w :]
    wait = cube.fetch(w_refs, scratch)
    x = x_ref[...].astype(f32)
    normed, _ = normed_of(x)
    n1_ref[...] = (normed * vec_ref[0:1] + vec_ref[1:2]).astype(bf16)
    sum_ref[...] = x + vec_ref[2:3]
    tokens = x_ref.shape[0] // count
    heads = width // HEAD_DIM
    keep = lax.broadcasted_iota(jnp.int32, (tokens, tokens), 1) < length
    w_ref = scratch[1]

    for core in range(2):
        wait(core)

        def step(y, carry):
            t = 2 * y + core
            cube.load(0, ids_ref, w_refs, scratch, core, y)
            qkv = nn(n1_ref[...], w_ref[:, : 3 * width]) + bias_ref[t]
            qkv_ref[t] = qkv.astype(bf16)
            for b in range(count):
                rows = slice(b * tokens, (b + 1) * tokens)
                found = []
                for h in range(heads):
                    q = qkv_ref[t, rows, h * HEAD_DIM : (h + 1) * HEAD_DIM]
                    k = qkv_ref[t, rows, width + h * HEAD_DIM : width + (h + 1) * HEAD_DIM]
                    v = qkv_ref[t, rows, 2 * width + h * HEAD_DIM : 2 * width + (h + 1) * HEAD_DIM]
                    scores = jnp.where(keep, nt(q, k) * FACTOR, -1e30)
                    weights = jnp.exp(scores - jnp.max(scores, -1, keepdims=True))
                    probs = weights * (1.0 / jnp.sum(weights, -1, keepdims=True))
                    found.append(nn(probs.astype(bf16), v).astype(bf16))
                att_ref[t, rows, :] = jnp.concatenate(found, axis=1)
            sum_ref[...] += nt(att_ref[t], w_ref[:, 3 * width :])
            return carry

        lax.fori_loop(0, cube.n_t // 2, step, 0)
    normed, _ = normed_of(sum_ref[...])
    n2_ref[...] = (normed * vec_ref[3:4] + vec_ref[4:5]).astype(bf16)


def gelu_kernel(cube, n_w, ids_ref, *refs):
    n2_ref, cot_ref, bias_ref = refs[:3]
    w_refs = refs[3 : 3 + n_w]
    act_ref, slope_ref = refs[3 + n_w : 5 + n_w]
    grad_refs = refs[5 + n_w : 7 + n_w]
    scratch, grads = refs[7 + n_w : 10 + n_w], refs[10 + n_w :]
    wait = cube.fetch(w_refs, scratch)
    copies = []
    for core in range(2):
        wait(core)

        def step(y, carry):
            t = 2 * y + core
            cube.load(1, ids_ref, w_refs, scratch, core, y)
            pre = nn(n2_ref[...], scratch[1][...]) + bias_ref[t]
            cdf = 0.5 * (1.0 + lax.erf(pre * (0.5**0.5)))
            slope = cdf + pre * (jnp.exp(-0.5 * pre * pre) * 0.3989422804014327)
            act_ref[t] = (pre * cdf).astype(bf16)
            slope_ref[t] = slope.astype(bf16)
            cube.store(2, ids_ref, grads, core, y, tn(cot_ref[...], act_ref[t]).astype(bf16))
            return carry

        lax.fori_loop(0, cube.n_t // 2, step, 0)
        copies.append(cube.send_out(grads, core, grad_refs[core]))
    for copy in copies:
        copy.wait()


def mlp_kernel(cube, n_w, ids_ref, *refs):
    n2_ref, cot_ref, act_ref, slope_ref, hidden_ref, vec_ref = refs[:6]
    one_refs, two_refs = refs[6 : 6 + n_w], refs[6 + n_w : 6 + 2 * n_w]
    outs = refs[6 + 2 * n_w :]
    sums_ref, enc_ref, dhidden_ref, small_ref = outs[:4]
    grad_refs = outs[4:6]
    one, two, grads = outs[6:9], outs[9:12], outs[12:14]
    mlp_ref, dnorm_ref = outs[14:]
    waits = [cube.fetch(one_refs, one), cube.fetch(two_refs, two)]
    mlp_ref[...] = hidden_ref[...] + vec_ref[5:6]
    dnorm_ref[...] = jnp.zeros_like(dnorm_ref)
    copies = []
    for core in range(2):
        for wait in waits:
            wait(core)

        def step(y, carry):
            t = 2 * y + core
            cube.load(1, ids_ref, one_refs, one, core, y)
            cube.load(2, ids_ref, two_refs, two, core, y)
            dact = nn(cot_ref[...], two[1][...])
            dpre = (slope_ref[t].astype(f32) * dact).astype(bf16)
            sums_ref[pl.ds(t, 1)] = column_sum(dpre.astype(f32))[None]
            cube.store(1, ids_ref, grads, core, y, tn(n2_ref[...], dpre).astype(bf16))
            dnorm_ref[...] += nt(dpre, one[1][...])
            mlp_ref[...] += nt(act_ref[t], two[1][...])
            return carry

        lax.fori_loop(0, cube.n_t // 2, step, 0)
        copies.append(cube.send_out(grads, core, grad_refs[core]))
    enc_ref[...] = mlp_ref[...].astype(bf16)
    normed, inverse = normed_of(hidden_ref[...])
    dnorm = dnorm_ref[...]
    cot = cot_ref[...].astype(f32)
    dhidden = cot + norm_back(dnorm, normed, inverse, vec_ref[3:4])
    dhidden_ref[...] = dhidden
    small_ref[0] = column_sum(dnorm * normed)
    small_ref[1] = column_sum(dnorm)
    small_ref[2] = column_sum(cot)
    small_ref[3] = column_sum(dhidden)
    for copy in copies:
        copy.wait()


def attend_back_kernel(cube, count, length, width, n_w, ids_ref, *refs):
    x_ref, n1_ref, qkv_ref, att_ref, dhidden_ref, vec_ref = refs[:6]
    w_refs = refs[6 : 6 + n_w]
    outs = refs[6 + n_w :]
    dbias_ref, dnorm_ref, small_ref = outs[:3]
    grad_refs = outs[3:5]
    scratch, grads = outs[5:8], outs[8:10]
    low_ref, dqkv_ref = outs[10:]
    wait = cube.fetch(w_refs, scratch)
    low_ref[...] = dhidden_ref[...].astype(bf16)
    dnorm_ref[...] = jnp.zeros_like(dnorm_ref)
    tokens = x_ref.shape[0] // count
    heads = width // HEAD_DIM
    keep = lax.broadcasted_iota(jnp.int32, (tokens, tokens), 0) < length
    w_ref = scratch[1]
    copies = []
    for core in (1, 0):
        wait(core)

        def step(y, carry):
            t = 2 * y + core
            cube.load(0, ids_ref, w_refs, scratch, core, y)
            datt = nn(low_ref[...], w_ref[:, 3 * width :]).astype(bf16)
            for b in range(count):
                rows = slice(b * tokens, (b + 1) * tokens)
                dqs, dks, dvs = [], [], []
                for h in range(heads):
                    q = qkv_ref[t, rows, h * HEAD_DIM : (h + 1) * HEAD_DIM]
                    k = qkv_ref[t, rows, width + h * HEAD_DIM : width + (h + 1) * HEAD_DIM]
                    v = qkv_ref[t, rows, 2 * width + h * HEAD_DIM : 2 * width + (h + 1) * HEAD_DIM]
                    do = datt[rows, h * HEAD_DIM : (h + 1) * HEAD_DIM]
                    scores = jnp.where(keep, nt(k, q) * FACTOR, -1e30)
                    weights = jnp.exp(scores - jnp.max(scores, 0, keepdims=True))
                    probs = weights * (1.0 / jnp.sum(weights, 0, keepdims=True))
                    dvs.append(nn(probs.astype(bf16), do))
                    dprobs = nt(v, do)
                    inner = jnp.sum(dprobs * probs, 0, keepdims=True)
                    dscores = (probs * (dprobs - inner)).astype(bf16)
                    dks.append(nn(dscores, q) * FACTOR)
                    dqs.append(tn(dscores, k) * FACTOR)
                dqkv_ref[rows, :] = jnp.concatenate(dqs + dks + dvs, axis=1).astype(bf16)
            dqkv = dqkv_ref[...]
            dbias_ref[pl.ds(t, 1)] = column_sum(dqkv.astype(f32))[None]
            dnorm_ref[...] += nt(dqkv, w_ref[:, : 3 * width])
            grad = jnp.concatenate((tn(n1_ref[...], dqkv), tn(low_ref[...], att_ref[t])), axis=1)
            cube.store(0, ids_ref, grads, core, y, grad.astype(bf16))
            return carry

        lax.fori_loop(0, cube.n_t // 2, step, 0)
        copies.append(cube.send_out(grads, core, grad_refs[core]))
    normed, _ = normed_of(x_ref[...].astype(f32))
    dnorm = dnorm_ref[...]
    small_ref[0] = column_sum(dnorm * normed)
    small_ref[1] = column_sum(dnorm)
    for copy in copies:
        copy.wait()


def patch_kernel(ids_ref, x_ref, dhidden_ref, dnorm_ref, vec_ref, patch_ref):
    normed, inverse = normed_of(x_ref[...].astype(f32))
    patch = dhidden_ref[...] + norm_back(dnorm_ref[...], normed, inverse, vec_ref[0:1])
    patch_ref[...] = patch.astype(bf16)


def on_device(
    n_dp,
    n_t,
    patches,
    attn_gain,
    attn_shift,
    qkv_weight,
    qv_bias,
    out_weight,
    out_bias,
    mlp_gain,
    mlp_shift,
    fc1_weight,
    fc1_bias,
    fc2_weight,
    fc2_bias,
    cotangent,
):
    t_me = lax.axis_index("tensor")
    cube = Cube(n_dp, n_t, qkv_weight.shape[1])
    order = t_me ^ jnp.arange(n_t)
    width = qkv_weight.shape[2]
    f_width = fc1_weight.shape[1]
    d = patches.shape[2]
    ids = jnp.stack((lax.axis_index("dp"), t_me)).astype(jnp.int32)
    count = patches.shape[0] // n_t
    length = patches.shape[1]
    padded = -(-length // TILE) * TILE
    tokens = count * padded

    def own_images(values):
        mine = lax.dynamic_slice_in_dim(values, t_me * count, count, 0)
        return jnp.pad(mine, ((0, 0), (0, padded - length), (0, 0))).reshape(tokens, d)

    def shape(*dims, dtype=bf16):
        return jax.ShapeDtypeStruct(dims, dtype)

    attn_piece = jnp.concatenate(
        (qkv_weight[0], qkv_weight[1], qkv_weight[2], out_weight.T), axis=1
    )
    two_piece = fc2_weight.T
    biases = jnp.concatenate((qv_bias.reshape(-1), fc1_bias))[None]
    x = own_images(patches)
    cot = own_images(cotangent)
    vecs = jnp.stack((attn_gain, attn_shift, out_bias, mlp_gain, mlp_shift, fc2_bias)).astype(f32)

    def bias_parts(biases):
        biases = biases.astype(f32)
        zeros = jnp.zeros((n_t, width), f32)
        qkv = (biases[:, :width], zeros, biases[:, width : 2 * width])
        return (jnp.concatenate(qkv, axis=1)[:, None], biases[:, None, 2 * width :])

    last = cube.steps - 1
    if cube.fast:
        held = attn_piece[None]
        one = fc1_weight[None]
        two = two_piece[None]
        (biases,) = hold([biases], (x,))
        biases = [biases] + [cube.flip(biases, r) for r in range(1, n_t)]
        qkv_bias, f_bias = bias_parts(jnp.concatenate(biases))
        for k in range(last, 0, -1):
            pairs = [(held, cube.swap(cube.gather[0], held, k))]
            if k < last:
                pairs.append((one, cube.swap(cube.gather[1], one, k + 1)))
            if k < last - 1:
                pairs.append((two, cube.swap(cube.gather[2], two, k + 2)))
            tokens_in = ((x, cot), (qkv_bias, f_bias), (vecs,))[min(last - k, 2)]
            found = join(pairs, tokens_in)
            held = found[0]
            one = found[1] if k < last else one
            two = found[2] if k < last - 1 else two
        came = cube.swap(cube.gather[0], held, 0)
        pairs = [(one, cube.swap(cube.gather[1], one, 1)), (two, cube.swap(cube.gather[2], two, 2))]
        w_attn = [held, came, cube.flip(held, 1), cube.flip(came, 1)]
        one, two = join(pairs, (came,))
        slot = (one, two)
    else:
        w_attn = gather_plain(cube, attn_piece)
        w_one = gather_plain(cube, fc1_weight)
        w_two = gather_plain(cube, two_piece)
        biases = jnp.take(lax.all_gather(biases[0], "tensor", axis=0, tiled=False), order, axis=0)
        qkv_bias, f_bias = bias_parts(biases)
        slot = ()
    n_w = len(w_attn)
    buffers = cube.buffers(d)
    grad_buffers = cube.grad_buffers(d)
    grad_shapes = [cube.grad_shape(d)] * 2

    n1, qkv, att, hidden, n2, done = call(
        partial(attend_kernel, cube, count, length, width, n_w),
        [
            shape(tokens, d),
            shape(n_t, tokens, 3 * width),
            shape(n_t, tokens, width),
            shape(tokens, d, dtype=f32),
            shape(tokens, d),
        ],
        ids,
        [x, vecs, qkv_bias],
        w_attn,
        buffers,
        slot,
    )
    if cube.fast:
        came, there = hold(
            [cube.swap(cube.gather[1], one, 0), cube.swap(cube.gather[2], two, 1)], (done,)
        )
        w_one = [one, came, cube.flip(one, 1), cube.flip(came, 1)]
        (two,) = join([(two, there)])
        slot = (two,)
    act, slope, done, *two_grads = call(
        partial(gelu_kernel, cube, n_w),
        [shape(n_t, tokens, f_width)] * 2,
        ids,
        [n2, cot, f_bias],
        w_one,
        buffers + grad_buffers,
        slot,
        grad_shapes,
    )
    if cube.fast:
        came, other = hold([cube.swap(cube.gather[2], two, 0), two_grads[1]], (done,))
        w_two = [two, came, cube.flip(two, 1), cube.flip(came, 1)]
        ((s_two, k_two),) = fold([(two_grads[0], cube.flip(other, 1))])
        c_two = cube.swap(cube.scatter[2], s_two, 0)
        slot = (s_two,)
    f_sums, enc, dhidden, mlp_small, done, *one_grads = call(
        partial(mlp_kernel, cube, n_w),
        [
            shape(n_t, 1, f_width, dtype=f32),
            shape(tokens, d),
            shape(tokens, d, dtype=f32),
            shape(4, 1, d, dtype=f32),
        ],
        ids,
        [n2, cot, act, slope, hidden, vecs],
        [*w_one, *w_two],
        buffers * 2 + grad_buffers + [pltpu.VMEM((tokens, d), f32)] * 2,
        slot,
        grad_shapes,
    )
    slot = ()
    if cube.fast:
        images = enc.reshape(count, padded, d)
        c_two, other, images = hold([c_two, one_grads[1], images], (done,))
        ((s_two, k_two),) = fold([(k_two, c_two)])
        c_two = cube.swap(cube.scatter[2], s_two, 1)
        ((s_one, k_one),) = fold([(one_grads[0], cube.flip(other, 1))], (s_two,))
        slot = (s_two, s_one)
    dbias, dnorm, attn_small, done, *attn_grads = call(
        partial(attend_back_kernel, cube, count, length, width, n_w),
        [
            shape(n_t, 1, 3 * width, dtype=f32),
            shape(tokens, d, dtype=f32),
            shape(2, 1, d, dtype=f32),
        ],
        ids,
        [x, n1, qkv, att, dhidden, vecs],
        w_attn,
        buffers
        + grad_buffers
        + [pltpu.VMEM((tokens, d), bf16), pltpu.VMEM((tokens, 3 * width), bf16)],
        slot,
        grad_shapes,
    )

    def patch_of(after):
        patch = call(
            patch_kernel, [shape(tokens, d)], ids, [x, dhidden, dnorm, vecs], [], [], after
        )[0]
        return patch.reshape(count, padded, d)

    sums = (attn_small, mlp_small, dbias, f_sums)
    if cube.fast:

        def spread(images, there):
            return [images, cube.flip(images, 1), there, cube.flip(there, 1)]

        c_one = cube.swap(cube.scatter[1], s_one, 0)
        there = cube.flip(images, 2)
        flat = (cube.half * cube.rows, d)
        other, images, there, c_two, c_one = hold(
            [attn_grads[1].reshape(flat), images, there, c_two, c_one], (done,)
        )
        k_attn, c_attn = attn_grads[0].reshape(flat), cube.flip(other, 1)
        waiting = {2: [2, k_two, c_two], 1: [1, k_one, c_one]}
        grads = {}
        found = fold([(k, c) for _, k, c in waiting.values()])
        for (group, state), (sent, kept) in zip(waiting.items(), found):
            state[1:] = [kept, cube.swap(cube.scatter[group], sent, state[0])]
            state[0] += 1
        small, after = sums, (found[0][0],)
        for k in range(cube.steps):
            more = [g for g in waiting if k > 0 and waiting[g][0] <= last]
            ended = [g for g in waiting if k > 0 and waiting[g][0] > last]
            pairs = [waiting[g][1:] for g in more]
            finals = [waiting.pop(g)[1:] for g in ended]
            s_attn, k_attn, small, *found = fold_with_small(
                cube, k_attn, c_attn, small, pairs, finals, ids, after
            )
            c_attn = cube.swap(cube.scatter[0], s_attn, k)
            for n, g in enumerate(more):
                came = cube.swap(cube.scatter[g], found[2 * n], waiting[g][0])
                waiting[g] = [waiting[g][0] + 1, found[2 * n + 1], came]
            grads.update(zip(ended, found[2 * len(more) :]))
            after = ()
            if k == 0:
                images, there = hold([images, there], (small,))
                encoded = place_images(cube, spread(images, there), length)
                after = (encoded,)
            if k == 1:
                images = patch_of((small,))
                after = (images,)
            if k == last - 1:
                (images,) = hold([images], (small,))
                there = cube.flip(images, 2)
            if k == last:
                images, there = hold([images, there], (small,))
                patch_grad = place_images(cube, spread(images, there), length)
            small = (small,)
        two_grad, one_grad = grads[2], grads[1]
        attn_grad, small = finish_with_small(k_attn, c_attn, small[0], (patch_grad,))
        small = small.astype(f32) + cube.flip(small, 1).astype(f32)
    else:
        two_grad = scatter_plain(cube, *two_grads)
        one_grad = scatter_plain(cube, *one_grads)
        attn_grad = scatter_plain(cube, *attn_grads)
        encoded = place_images(cube, [enc.reshape(count, padded, d)], length)
        patch_grad = place_images(cube, [patch_of(())], length)

        def collect(ids_ref, *refs):
            gather_small(cube, ids_ref, refs[:4], refs[4])

        small = call(collect, [shape(ROWS, d, dtype=f32)], ids, sums, [], [])[0]
        small = lax.psum(small, AXES)

    def shard_row(at):
        return lax.dynamic_slice_in_dim(small, at + t_me, 1, 0)

    return (
        encoded,
        patch_grad,
        small[0],
        small[1],
        jnp.stack([attn_grad[:, i * width : (i + 1) * width] for i in range(3)]),
        jnp.concatenate((shard_row(6 + n_t), shard_row(6 + 2 * n_t)))[:, :width],
        attn_grad[:, 3 * width :].T,
        small[5],
        small[2],
        small[3],
        one_grad,
        shard_row(6)[0],
        two_grad.T,
        small[4],
    )


def solution(mesh):
    return jax.shard_map(
        partial(on_device, mesh.shape["dp"], mesh.shape["tensor"]),
        mesh=mesh,
        in_specs=(
            P("dp", None, None),
            P(),
            P(),
            P(None, "dp", "tensor"),
            P(None, "tensor"),
            P("tensor", "dp"),
            P(),
            P(),
            P(),
            P("dp", "tensor"),
            P("tensor"),
            P("tensor", "dp"),
            P(),
            P("dp", None, None),
        ),
        out_specs=(
            P("dp", None, None),
            P("dp", None, None),
            P(),
            P(),
            P(None, "dp", "tensor"),
            P(None, "tensor"),
            P("tensor", "dp"),
            P(),
            P(),
            P(),
            P("dp", "tensor"),
            P("tensor"),
            P("tensor", "dp"),
            P(),
        ),
        check_vma=False,
    )
```

```python
from functools import partial

import jax
import jax.numpy as jnp
from jax import lax
from jax.experimental import pallas as pl
from jax.experimental.pallas import tpu as pltpu
from jax.sharding import PartitionSpec as P

HEAD_DIM = 64
EPS = 1e-06
AXES = ("dp", "tensor")
TILE = 16
ROWS = 32
MIB = 1024 * 1024
FACTOR = HEAD_DIM ** (-0.5)
bf16 = jnp.bfloat16
f32 = jnp.float32


class Cube:
    def __init__(self, n_dp, n_t, rows):
        self.n_dp, self.n_t, self.rows = n_dp, n_t, rows
        self.n = n_dp * n_t
        n_bits = self.n.bit_length() - 1
        self.fast = (1 << n_bits) == self.n and n_bits >= 4 and rows % TILE == 0
        far = list(range(n_bits - 1, 3, -1))
        self.gather = [
            ([2, 3, 1] + far, [1, 2, 3] + far),
            ([2, 3, 1] + far, [1, 3, 2] + far),
            ([2, 3, 1] + far, [1, 3, 2] + far),
        ]
        self.scatter = [
            ([2, 1, 3] + far, [1, 3, 2] + far),
            ([2, 3, 1] + far, [1, 3, 2] + far),
            ([2, 3, 1] + far, [1, 3, 2] + far),
        ]
        self.steps = 3 + len(far)
        self.half = self.n // 2

    def swap(self, orders, value, k):
        return lax.ppermute(value, AXES, [(i, i ^ (1 << orders[i & 1][k])) for i in range(self.n)])

    def flip(self, value, bits):
        return lax.ppermute(value, AXES, [(i, i ^ bits) for i in range(self.n)])

    def at(self, orders, ids_ref, core, y, block):
        relative = ((ids_ref[0] ^ block) << 2) | (y << 1)
        found = []
        for order in orders:
            place = 0
            for k, bit in enumerate(order[::-1]):
                place = place | (((relative >> bit) & 1) << k)
            found.append(place)
        return jnp.where((ids_ref[1] & 1) == core, found[0], found[1])

    def buffers(self, cols):
        blocks = (2, self.half, self.rows, cols) if self.fast else (1, 1, 8, 128)
        shard = pltpu.VMEM((self.n_dp * self.rows, cols), bf16)
        return [pltpu.VMEM(blocks, bf16), shard, pltpu.SemaphoreType.DMA((4,))]

    def fetch(self, refs, scratch):
        if not self.fast:
            return lambda core: None
        held, _, sems = scratch
        part = self.half // 2
        copies = [
            pltpu.make_async_copy(refs[i], held.at[i // 2, pl.ds(i % 2 * part, part)], sems.at[i])
            for i in range(4)
        ]
        for copy in copies:
            copy.start()

        def wait(core):
            copies[2 * core].wait()
            copies[2 * core + 1].wait()

        return wait

    def load(self, group, ids_ref, refs, scratch, core, y):
        held, shard, sems = scratch
        if not self.fast:
            copy = pltpu.make_async_copy(refs[0].at[2 * y + core], shard, sems.at[0])
            copy.start()
            copy.wait()
            return
        for d in range(self.n_dp):
            rows = slice(d * self.rows, (d + 1) * self.rows)
            shard[rows, :] = held[core, self.at(self.gather[group], ids_ref, core, y, d)]

    def grad_buffers(self, cols):
        shape = self.grad_shape(cols).shape
        return [pltpu.VMEM((2,) + shape, bf16), pltpu.SemaphoreType.DMA((2,))]

    def store(self, group, ids_ref, scratch, core, y, value):
        if not self.fast:
            scratch[0][core, y] = value
            return
        for d in range(self.n_dp):
            rows = value[d * self.rows : (d + 1) * self.rows]
            scratch[0][core, self.at(self.scatter[group], ids_ref, core, y, d)] = rows

    def send_out(self, scratch, core, ref):
        copy = pltpu.make_async_copy(scratch[0].at[core], ref, scratch[1].at[core])
        copy.start()
        return copy

    def grad_shape(self, cols):
        if not self.fast:
            return jax.ShapeDtypeStruct((2, self.n_dp * self.rows, cols), bf16)
        return jax.ShapeDtypeStruct((self.half, self.rows, cols), bf16)


def gather_plain(cube, piece):
    rows, cols = piece.shape
    whole = lax.all_gather(piece, AXES, axis=0, tiled=False)
    whole = whole.reshape(cube.n_dp, cube.n_t, rows, cols).transpose(1, 0, 2, 3)
    whole = whole.reshape(cube.n_t, cube.n_dp * rows, cols)
    return [jnp.take(whole, lax.axis_index("tensor") ^ jnp.arange(cube.n_t), axis=0)]


def scatter_plain(cube, own, other):
    n_t, n_dp, rows, cols = cube.n_t, cube.n_dp, cube.rows, own.shape[2]
    part = jnp.stack((own, other), axis=1).reshape(n_t, n_dp * rows, cols)
    part = jnp.take(part, lax.axis_index("tensor") ^ jnp.arange(n_t), axis=0)
    part = part.reshape(n_t, n_dp, rows, cols).transpose(1, 0, 2, 3)
    part = part.reshape(n_dp * n_t * rows, cols)
    return lax.psum_scatter(part, AXES, scatter_dimension=0, tiled=True).astype(f32)


def join(pairs, after=()):
    def kernel(*refs):
        outs = refs[2 * len(pairs) + len(after) :]
        for i, out in enumerate(outs):
            size = pairs[i][0].shape[0]
            out[:size] = refs[2 * i][...]
            out[size:] = refs[2 * i + 1][...]

    shapes = [
        jax.ShapeDtypeStruct((2 * p[0].shape[0],) + p[0].shape[1:], p[0].dtype) for p in pairs
    ]
    return plain_call(kernel, shapes, [x for p in pairs for x in p], after)


def fold(pairs, after=()):
    shapes = []
    for a, _ in pairs:
        shapes += [jax.ShapeDtypeStruct((a.shape[0] // 2,) + a.shape[1:], bf16)] * 2
    n_in = 2 * len(pairs)

    def kernel(*refs):
        outs = refs[n_in + len(after) :]
        for i in range(len(pairs)):
            size = shapes[2 * i].shape[0]
            for part in range(2):
                add_rows(outs[2 * i + part], refs[2 * i : 2 * i + 2], (1 - part) * size)

    found = vmem_call(kernel, shapes, [x for p in pairs for x in p], after)
    return [found[2 * i : 2 * i + 2] for i in range(len(pairs))]


def add_rows(out_ref, refs, start):
    size, rows, _ = out_ref.shape

    def step(i, carry):
        for c in range(0, rows, ROWS):
            at = (i, slice(c, c + ROWS), slice(None))
            source = (start + i, slice(c, c + ROWS), slice(None))
            value = refs[0][source].astype(f32)
            for ref in refs[1:]:
                value = value + ref[source].astype(f32)
            out_ref[at] = value.astype(out_ref.dtype)
        return carry

    lax.fori_loop(0, size, step, 0)


def vmem_call(kernel, shapes, inputs, after, ids=None, scratch=()):
    specs = [pl.BlockSpec(memory_space=pltpu.VMEM)] * len(inputs)
    specs += [pl.BlockSpec(memory_space=pl.ANY)] * len(after)
    values = [*inputs, *after]
    if ids is not None:
        specs = [pl.BlockSpec(memory_space=pltpu.SMEM), *specs]
        values = [ids, *values]
    return pl.pallas_call(
        kernel,
        out_shape=shapes,
        in_specs=specs,
        out_specs=[pl.BlockSpec(memory_space=pltpu.VMEM)] * len(shapes),
        scratch_shapes=list(scratch),
        compiler_params=pltpu.CompilerParams(vmem_limit_bytes=24 * MIB),
        cost_estimate=pl.CostEstimate(flops=0, bytes_accessed=1024, transcendentals=0),
    )(*values)


def plain_call(kernel, shapes, inputs, after):
    specs = [pl.BlockSpec(x.shape, lambda i: (0, 0, 0)) for x in inputs]
    return pl.pallas_call(
        kernel,
        grid=(1,),
        out_shape=shapes,
        in_specs=specs + [pl.BlockSpec(memory_space=pl.ANY)] * len(after),
        out_specs=[pl.BlockSpec(x.shape, lambda i, n=len(x.shape): (0,) * n) for x in shapes],
        compiler_params=pltpu.CompilerParams(vmem_limit_bytes=48 * MIB),
        cost_estimate=pl.CostEstimate(flops=0, bytes_accessed=1024, transcendentals=0),
    )(*inputs, *after)


def fold_with_small(cube, kept, came, small, pairs, finals, ids, after=()):
    first = len(small) > 1
    size, d = kept.shape[0] // 2, kept.shape[1]
    shapes = [
        jax.ShapeDtypeStruct((size + ROWS, d), bf16),
        jax.ShapeDtypeStruct((size, d), bf16),
        jax.ShapeDtypeStruct((ROWS, d), bf16),
    ]
    for a, _ in pairs:
        shapes += [jax.ShapeDtypeStruct((a.shape[0] // 2,) + a.shape[1:], bf16)] * 2
    shapes += [jax.ShapeDtypeStruct(a.shape[1:], f32) for a, _ in finals]
    others = [x for p in [*pairs, *finals] for x in p]

    def kernel(ids_ref, kept_ref, came_ref, *refs):
        extra, refs = refs[: len(small)], refs[len(small) :]
        ins, outs = refs[: len(others)], refs[len(others) + len(after) :]
        send_ref, keep_ref, low_ref = outs[:3]
        total_ref = outs[-1]
        for n in range(len(pairs)):
            for part in range(2):
                out_ref = outs[3 + 2 * n + part]
                add_rows(out_ref, ins[2 * n : 2 * n + 2], (1 - part) * out_ref.shape[0])
        for n in range(len(pairs), len(pairs) + len(finals)):
            total = ins[2 * n][0].astype(f32) + ins[2 * n + 1][0].astype(f32)
            outs[3 + len(pairs) + n][...] = total

        def step(i, carry):
            at = pl.ds(pl.multiple_of(i * ROWS, ROWS), ROWS)
            there = pl.ds(pl.multiple_of(size + i * ROWS, ROWS), ROWS)
            sent = kept_ref[there, :].astype(f32) + came_ref[there, :].astype(f32)
            send_ref[at, :] = sent.astype(bf16)
            keep_ref[at, :] = (kept_ref[at, :].astype(f32) + came_ref[at, :].astype(f32)).astype(bf16)
            return carry

        lax.fori_loop(0, size // ROWS, step, 0)
        if first:
            gather_small(cube, ids_ref, extra, total_ref)
        else:
            total_ref[...] = extra[0][...].astype(f32) + came_ref[2 * size :, :].astype(f32)
        low = total_ref[...].astype(bf16)
        send_ref[size:, :] = low
        low_ref[...] = low

    return vmem_call(
        kernel, shapes, [kept, came, *small, *others], after, ids, [pltpu.VMEM((ROWS, d), f32)]
    )


def gather_small(cube, ids_ref, refs, out_ref):
    attn_ref, mlp_ref = refs[:2]
    out_ref[...] = jnp.zeros_like(out_ref)
    for i in range(2):
        out_ref[i : i + 1, :] = attn_ref[i]
    for i in range(4):
        out_ref[2 + i : 3 + i, :] = mlp_ref[i]
    n_t = cube.n_t
    for relative in range(n_t):
        t = relative ^ ids_ref[1]
        dbias = refs[2][relative]
        width = dbias.shape[1] // 3
        out_ref[pl.ds(6 + t, 1), :] = refs[3][relative]
        out_ref[pl.ds(6 + n_t + t, 1), :width] = dbias[:, :width]
        out_ref[pl.ds(6 + 2 * n_t + t, 1), :width] = dbias[:, 2 * width :]


def finish_with_small(kept, came, small, width, after=()):
    rows, d = kept.shape

    def kernel(kept_ref, came_ref, small_ref, *refs):
        qkv_ref, out_ref, low_ref = refs[len(after) :]
        value = kept_ref[...].astype(f32) + came_ref[:rows, :].astype(f32)
        for i in range(3):
            qkv_ref[i] = value[:, i * width : (i + 1) * width]
        out_ref[...] = value[:, 3 * width :].T
        low_ref[...] = (small_ref[...].astype(f32) + came_ref[rows:, :].astype(f32)).astype(bf16)

    shapes = [
        jax.ShapeDtypeStruct((3, rows, width), f32),
        jax.ShapeDtypeStruct((width, rows), f32),
        jax.ShapeDtypeStruct(small.shape, bf16),
    ]
    return vmem_call(kernel, shapes, [kept, came, small], after)


def hold(values, after):
    n = len(values)

    def kernel(*refs):
        pass

    return pl.pallas_call(
        kernel,
        out_shape=[jax.ShapeDtypeStruct(v.shape, v.dtype) for v in values],
        in_specs=[pl.BlockSpec(memory_space=pl.ANY)] * (n + len(after)),
        out_specs=[pl.BlockSpec(memory_space=pl.ANY)] * n,
        input_output_aliases={i: i for i in range(n)},
        cost_estimate=pl.CostEstimate(flops=0, bytes_accessed=1024, transcendentals=0),
    )(*values, *after)


def place_images(cube, pieces, length, after=()):
    if not cube.fast:
        return lax.all_gather(pieces[0][:, :length], "tensor", axis=0, tiled=True)
    count = pieces[0].shape[0]
    index = lax.axis_index("tensor").astype(jnp.int32).reshape(1)

    def kernel(index_ref, *refs):
        out_ref, ordered = refs[4:]
        for r in range(4):
            for i in range(count):
                ordered[(index_ref[0] ^ r) * count + i] = refs[r][i]
        out_ref[...] = jnp.swapaxes(ordered[...], 0, 1)[:length]

    shape = (length, 4 * count, pieces[0].shape[2])
    ordered = pltpu.VMEM((4 * count,) + pieces[0].shape[1:], bf16)
    out = call(kernel, [jax.ShapeDtypeStruct(shape, bf16)], index, pieces, [], [ordered], after)[0]
    return out.transpose(1, 0, 2)


def call(kernel, out_shapes, index, inputs, weights, scratch, after=(), grads=()):
    out_shapes = [*out_shapes, jax.ShapeDtypeStruct((8, 128), f32)]
    n_in, n_w, n_out = len(inputs), len(weights), len(out_shapes)
    spots = [pl.BlockSpec(memory_space=pltpu.VMEM)] * n_out
    spots += [pl.BlockSpec(memory_space=pltpu.HBM)] * len(grads)

    def body(index_ref, *refs):
        rest = refs[n_in + n_w + len(after) :]
        rest[n_out - 1][...] = jnp.zeros((8, 128), f32)
        kernel(index_ref, *refs[: n_in + n_w], *rest[: n_out - 1], *rest[n_out:])

    return pl.pallas_call(
        body,
        out_shape=[*out_shapes, *grads],
        in_specs=[pl.BlockSpec(memory_space=pltpu.SMEM)]
        + [pl.BlockSpec(memory_space=pltpu.VMEM)] * n_in
        + [pl.BlockSpec(memory_space=pltpu.HBM)] * n_w
        + [pl.BlockSpec(memory_space=pl.ANY)] * len(after),
        out_specs=spots,
        scratch_shapes=scratch,
        compiler_params=pltpu.CompilerParams(vmem_limit_bytes=56 * MIB),
        cost_estimate=pl.CostEstimate(flops=0, bytes_accessed=1024, transcendentals=0),
    )(index, *inputs, *weights, *after)


def nn(left, right):
    return lax.dot_general(left, right, (((1,), (0,)), ((), ())), preferred_element_type=f32)


def nt(left, right):
    return lax.dot_general(left, right, (((1,), (1,)), ((), ())), preferred_element_type=f32)


def tn(left, right):
    return lax.dot_general(left, right, (((0,), (0,)), ((), ())), preferred_element_type=f32)


def normed_of(values):
    centre = values - jnp.mean(values, -1, keepdims=True)
    inverse = lax.rsqrt(jnp.mean(centre * centre, -1, keepdims=True) + EPS)
    return (centre * inverse, inverse)


def norm_back(upstream, normed, inverse, gain):
    scaled = upstream * gain
    inner = (
        scaled
        - jnp.mean(scaled, -1, keepdims=True)
        - normed * jnp.mean(scaled * normed, -1, keepdims=True)
    )
    return inverse * inner


def column_sum(values):
    return jnp.sum(values, 0, keepdims=True)


def attend_kernel(cube, count, length, width, n_w, ids_ref, *refs):
    x_ref, vec_ref, bias_ref = refs[:3]
    w_refs = refs[3 : 3 + n_w]
    n1_ref, qkv_ref, att_ref, sum_ref, n2_ref = refs[3 + n_w : 8 + n_w]
    scratch = refs[8 + n_w :]
    wait = cube.fetch(w_refs, scratch)
    x = x_ref[...].astype(f32)
    normed, _ = normed_of(x)
    n1_ref[...] = (normed * vec_ref[0:1] + vec_ref[1:2]).astype(bf16)
    sum_ref[...] = x + vec_ref[2:3]
    tokens = x_ref.shape[0] // count
    heads = width // HEAD_DIM
    keep = lax.broadcasted_iota(jnp.int32, (tokens, tokens), 1) < length
    w_ref = scratch[1]

    for core in range(2):
        wait(core)

        def step(y, carry):
            t = 2 * y + core
            cube.load(0, ids_ref, w_refs, scratch, core, y)
            qkv = nn(n1_ref[...], w_ref[:, : 3 * width]) + bias_ref[t]
            qkv_ref[t] = qkv.astype(bf16)
            for b in range(count):
                rows = slice(b * tokens, (b + 1) * tokens)
                found = []
                for h in range(heads):
                    q = qkv_ref[t, rows, h * HEAD_DIM : (h + 1) * HEAD_DIM]
                    k = qkv_ref[t, rows, width + h * HEAD_DIM : width + (h + 1) * HEAD_DIM]
                    v = qkv_ref[t, rows, 2 * width + h * HEAD_DIM : 2 * width + (h + 1) * HEAD_DIM]
                    scores = jnp.where(keep, nt(q, k) * FACTOR, -1e30)
                    weights = jnp.exp(scores - jnp.max(scores, -1, keepdims=True))
                    probs = weights * (1.0 / jnp.sum(weights, -1, keepdims=True))
                    found.append(nn(probs.astype(bf16), v).astype(bf16))
                att_ref[t, rows, :] = jnp.concatenate(found, axis=1)
            sum_ref[...] += nt(att_ref[t], w_ref[:, 3 * width :])
            return carry

        lax.fori_loop(0, cube.n_t // 2, step, 0)
    normed, _ = normed_of(sum_ref[...])
    n2_ref[...] = (normed * vec_ref[3:4] + vec_ref[4:5]).astype(bf16)


def gelu_kernel(cube, n_w, ids_ref, *refs):
    n2_ref, cot_ref, bias_ref = refs[:3]
    w_refs = refs[3 : 3 + n_w]
    act_ref, slope_ref = refs[3 + n_w : 5 + n_w]
    grad_refs = refs[5 + n_w : 7 + n_w]
    scratch, grads = refs[7 + n_w : 10 + n_w], refs[10 + n_w :]
    wait = cube.fetch(w_refs, scratch)
    copies = []
    for core in range(2):
        wait(core)

        def step(y, carry):
            t = 2 * y + core
            cube.load(1, ids_ref, w_refs, scratch, core, y)
            pre = nn(n2_ref[...], scratch[1][...]) + bias_ref[t]
            cdf = 0.5 * (1.0 + lax.erf(pre * (0.5**0.5)))
            slope = cdf + pre * (jnp.exp(-0.5 * pre * pre) * 0.3989422804014327)
            act_ref[t] = (pre * cdf).astype(bf16)
            slope_ref[t] = slope.astype(bf16)
            cube.store(2, ids_ref, grads, core, y, tn(cot_ref[...], act_ref[t]).astype(bf16))
            return carry

        lax.fori_loop(0, cube.n_t // 2, step, 0)
        copies.append(cube.send_out(grads, core, grad_refs[core]))
    for copy in copies:
        copy.wait()


def mlp_kernel(cube, n_w, ids_ref, *refs):
    n2_ref, cot_ref, act_ref, slope_ref, hidden_ref, vec_ref = refs[:6]
    one_refs, two_refs = refs[6 : 6 + n_w], refs[6 + n_w : 6 + 2 * n_w]
    outs = refs[6 + 2 * n_w :]
    sums_ref, enc_ref, dhidden_ref, small_ref = outs[:4]
    grad_refs = outs[4:6]
    one, two, grads = outs[6:9], outs[9:12], outs[12:14]
    mlp_ref, dnorm_ref = outs[14:]
    waits = [cube.fetch(one_refs, one), cube.fetch(two_refs, two)]
    mlp_ref[...] = hidden_ref[...] + vec_ref[5:6]
    dnorm_ref[...] = jnp.zeros_like(dnorm_ref)
    copies = []
    for core in range(2):
        for wait in waits:
            wait(core)

        def step(y, carry):
            t = 2 * y + core
            cube.load(1, ids_ref, one_refs, one, core, y)
            cube.load(2, ids_ref, two_refs, two, core, y)
            dact = nn(cot_ref[...], two[1][...])
            dpre = (slope_ref[t].astype(f32) * dact).astype(bf16)
            sums_ref[pl.ds(t, 1)] = column_sum(dpre.astype(f32))[None]
            cube.store(1, ids_ref, grads, core, y, tn(n2_ref[...], dpre).astype(bf16))
            dnorm_ref[...] += nt(dpre, one[1][...])
            mlp_ref[...] += nt(act_ref[t], two[1][...])
            return carry

        lax.fori_loop(0, cube.n_t // 2, step, 0)
        copies.append(cube.send_out(grads, core, grad_refs[core]))
    enc_ref[...] = mlp_ref[...].astype(bf16)
    normed, inverse = normed_of(hidden_ref[...])
    dnorm = dnorm_ref[...]
    cot = cot_ref[...].astype(f32)
    dhidden = cot + norm_back(dnorm, normed, inverse, vec_ref[3:4])
    dhidden_ref[...] = dhidden
    small_ref[0] = column_sum(dnorm * normed)
    small_ref[1] = column_sum(dnorm)
    small_ref[2] = column_sum(cot)
    small_ref[3] = column_sum(dhidden)
    for copy in copies:
        copy.wait()


def attend_back_kernel(cube, count, length, width, n_w, ids_ref, *refs):
    x_ref, n1_ref, qkv_ref, att_ref, dhidden_ref, vec_ref = refs[:6]
    w_refs = refs[6 : 6 + n_w]
    outs = refs[6 + n_w :]
    dbias_ref, dnorm_ref, small_ref = outs[:3]
    grad_refs = outs[3:5]
    scratch, grads = outs[5:8], outs[8:10]
    low_ref, dqkv_ref = outs[10:]
    wait = cube.fetch(w_refs, scratch)
    low_ref[...] = dhidden_ref[...].astype(bf16)
    dnorm_ref[...] = jnp.zeros_like(dnorm_ref)
    tokens = x_ref.shape[0] // count
    heads = width // HEAD_DIM
    keep = lax.broadcasted_iota(jnp.int32, (tokens, tokens), 0) < length
    w_ref = scratch[1]
    copies = []
    for core in (1, 0):
        wait(core)

        def step(y, carry):
            t = 2 * y + core
            cube.load(0, ids_ref, w_refs, scratch, core, y)
            datt = nn(low_ref[...], w_ref[:, 3 * width :]).astype(bf16)
            for b in range(count):
                rows = slice(b * tokens, (b + 1) * tokens)
                dqs, dks, dvs = [], [], []
                for h in range(heads):
                    q = qkv_ref[t, rows, h * HEAD_DIM : (h + 1) * HEAD_DIM]
                    k = qkv_ref[t, rows, width + h * HEAD_DIM : width + (h + 1) * HEAD_DIM]
                    v = qkv_ref[t, rows, 2 * width + h * HEAD_DIM : 2 * width + (h + 1) * HEAD_DIM]
                    do = datt[rows, h * HEAD_DIM : (h + 1) * HEAD_DIM]
                    scores = jnp.where(keep, nt(k, q) * FACTOR, -1e30)
                    weights = jnp.exp(scores - jnp.max(scores, 0, keepdims=True))
                    probs = weights * (1.0 / jnp.sum(weights, 0, keepdims=True))
                    dvs.append(nn(probs.astype(bf16), do))
                    dprobs = nt(v, do)
                    inner = jnp.sum(dprobs * probs, 0, keepdims=True)
                    dscores = (probs * (dprobs - inner)).astype(bf16)
                    dks.append(nn(dscores, q) * FACTOR)
                    dqs.append(tn(dscores, k) * FACTOR)
                dqkv_ref[rows, :] = jnp.concatenate(dqs + dks + dvs, axis=1).astype(bf16)
            dqkv = dqkv_ref[...]
            dbias_ref[pl.ds(t, 1)] = column_sum(dqkv.astype(f32))[None]
            dnorm_ref[...] += nt(dqkv, w_ref[:, : 3 * width])
            grad = jnp.concatenate((tn(n1_ref[...], dqkv), tn(low_ref[...], att_ref[t])), axis=1)
            cube.store(0, ids_ref, grads, core, y, grad.astype(bf16))
            return carry

        lax.fori_loop(0, cube.n_t // 2, step, 0)
        copies.append(cube.send_out(grads, core, grad_refs[core]))
    normed, _ = normed_of(x_ref[...].astype(f32))
    dnorm = dnorm_ref[...]
    small_ref[0] = column_sum(dnorm * normed)
    small_ref[1] = column_sum(dnorm)
    for copy in copies:
        copy.wait()


def patch_kernel(ids_ref, x_ref, dhidden_ref, dnorm_ref, vec_ref, patch_ref):
    normed, inverse = normed_of(x_ref[...].astype(f32))
    patch = dhidden_ref[...] + norm_back(dnorm_ref[...], normed, inverse, vec_ref[0:1])
    patch_ref[...] = patch.astype(bf16)


def on_device(
    n_dp,
    n_t,
    patches,
    attn_gain,
    attn_shift,
    qkv_weight,
    qv_bias,
    out_weight,
    out_bias,
    mlp_gain,
    mlp_shift,
    fc1_weight,
    fc1_bias,
    fc2_weight,
    fc2_bias,
    cotangent,
):
    t_me = lax.axis_index("tensor")
    cube = Cube(n_dp, n_t, qkv_weight.shape[1])
    order = t_me ^ jnp.arange(n_t)
    width = qkv_weight.shape[2]
    f_width = fc1_weight.shape[1]
    d = patches.shape[2]
    ids = jnp.stack((lax.axis_index("dp"), t_me)).astype(jnp.int32)
    count = patches.shape[0] // n_t
    length = patches.shape[1]
    padded = -(-length // TILE) * TILE
    tokens = count * padded

    def own_images(values):
        mine = lax.dynamic_slice_in_dim(values, t_me * count, count, 0)
        return jnp.pad(mine, ((0, 0), (0, padded - length), (0, 0))).reshape(tokens, d)

    def shape(*dims, dtype=bf16):
        return jax.ShapeDtypeStruct(dims, dtype)

    attn_piece = jnp.concatenate(
        (qkv_weight[0], qkv_weight[1], qkv_weight[2], out_weight.T), axis=1
    )
    two_piece = fc2_weight.T
    biases = jnp.concatenate((qv_bias.reshape(-1), fc1_bias))[None]
    x = own_images(patches)
    cot = own_images(cotangent)
    vecs = jnp.stack((attn_gain, attn_shift, out_bias, mlp_gain, mlp_shift, fc2_bias)).astype(f32)

    def bias_parts(biases):
        biases = biases.astype(f32)
        zeros = jnp.zeros((n_t, width), f32)
        qkv = (biases[:, :width], zeros, biases[:, width : 2 * width])
        return (jnp.concatenate(qkv, axis=1)[:, None], biases[:, None, 2 * width :])

    last = cube.steps - 1
    if cube.fast:
        held = attn_piece[None]
        one = fc1_weight[None]
        two = two_piece[None]
        (biases,) = hold([biases], (x,))
        biases = [biases] + [cube.flip(biases, r) for r in range(1, n_t)]
        qkv_bias, f_bias = bias_parts(jnp.concatenate(biases))
        for k in range(last, 0, -1):
            pairs = [(held, cube.swap(cube.gather[0], held, k))]
            if k < last:
                pairs.append((one, cube.swap(cube.gather[1], one, k + 1)))
            if k < last - 1:
                pairs.append((two, cube.swap(cube.gather[2], two, k + 2)))
            tokens_in = ((x, cot), (qkv_bias, f_bias), (vecs,))[min(last - k, 2)]
            found = join(pairs, tokens_in)
            held = found[0]
            one = found[1] if k < last else one
            two = found[2] if k < last - 1 else two
        came = cube.swap(cube.gather[0], held, 0)
        pairs = [(one, cube.swap(cube.gather[1], one, 1)), (two, cube.swap(cube.gather[2], two, 2))]
        w_attn = [held, came, cube.flip(held, 1), cube.flip(came, 1)]
        one, two = join(pairs, (came,))
        slot = (one, two)
    else:
        w_attn = gather_plain(cube, attn_piece)
        w_one = gather_plain(cube, fc1_weight)
        w_two = gather_plain(cube, two_piece)
        biases = jnp.take(lax.all_gather(biases[0], "tensor", axis=0, tiled=False), order, axis=0)
        qkv_bias, f_bias = bias_parts(biases)
        slot = ()
    n_w = len(w_attn)
    buffers = cube.buffers(d)
    grad_buffers = cube.grad_buffers(d)
    grad_shapes = [cube.grad_shape(d)] * 2

    n1, qkv, att, hidden, n2, done = call(
        partial(attend_kernel, cube, count, length, width, n_w),
        [
            shape(tokens, d),
            shape(n_t, tokens, 3 * width),
            shape(n_t, tokens, width),
            shape(tokens, d, dtype=f32),
            shape(tokens, d),
        ],
        ids,
        [x, vecs, qkv_bias],
        w_attn,
        buffers,
        slot,
    )
    if cube.fast:
        came, there = hold(
            [cube.swap(cube.gather[1], one, 0), cube.swap(cube.gather[2], two, 1)], (done,)
        )
        w_one = [one, came, cube.flip(one, 1), cube.flip(came, 1)]
        (two,) = join([(two, there)])
        slot = (two,)
    act, slope, done, *two_grads = call(
        partial(gelu_kernel, cube, n_w),
        [shape(n_t, tokens, f_width)] * 2,
        ids,
        [n2, cot, f_bias],
        w_one,
        buffers + grad_buffers,
        slot,
        grad_shapes,
    )
    if cube.fast:
        came, other = hold([cube.swap(cube.gather[2], two, 0), two_grads[1]], (done,))
        w_two = [two, came, cube.flip(two, 1), cube.flip(came, 1)]
        ((s_two, k_two),) = fold([(two_grads[0], cube.flip(other, 1))])
        c_two = cube.swap(cube.scatter[2], s_two, 0)
        slot = (s_two,)
    f_sums, enc, dhidden, mlp_small, done, *one_grads = call(
        partial(mlp_kernel, cube, n_w),
        [
            shape(n_t, 1, f_width, dtype=f32),
            shape(tokens, d),
            shape(tokens, d, dtype=f32),
            shape(4, 1, d, dtype=f32),
        ],
        ids,
        [n2, cot, act, slope, hidden, vecs],
        [*w_one, *w_two],
        buffers * 2 + grad_buffers + [pltpu.VMEM((tokens, d), f32)] * 2,
        slot,
        grad_shapes,
    )
    slot = ()
    if cube.fast:
        images = enc.reshape(count, padded, d)
        c_two, other, images = hold([c_two, one_grads[1], images], (done,))
        ((s_two, k_two),) = fold([(k_two, c_two)])
        c_two = cube.swap(cube.scatter[2], s_two, 1)
        ((s_one, k_one),) = fold([(one_grads[0], cube.flip(other, 1))], (s_two,))
        slot = (s_two, s_one)
    dbias, dnorm, attn_small, done, *attn_grads = call(
        partial(attend_back_kernel, cube, count, length, width, n_w),
        [
            shape(n_t, 1, 3 * width, dtype=f32),
            shape(tokens, d, dtype=f32),
            shape(2, 1, d, dtype=f32),
        ],
        ids,
        [x, n1, qkv, att, dhidden, vecs],
        w_attn,
        buffers
        + grad_buffers
        + [pltpu.VMEM((tokens, d), bf16), pltpu.VMEM((tokens, 3 * width), bf16)],
        slot,
        grad_shapes,
    )

    def patch_of(after):
        patch = call(
            patch_kernel, [shape(tokens, d)], ids, [x, dhidden, dnorm, vecs], [], [], after
        )[0]
        return patch.reshape(count, padded, d)

    sums = (attn_small, mlp_small, dbias, f_sums)
    if cube.fast:

        def spread(images, there):
            return [images, cube.flip(images, 1), there, cube.flip(there, 1)]

        c_one = cube.swap(cube.scatter[1], s_one, 0)
        there = cube.flip(images, 2)
        flat = (cube.half * cube.rows, d)
        other, images, there, c_two, c_one = hold(
            [attn_grads[1].reshape(flat), images, there, c_two, c_one], (done,)
        )
        k_attn, c_attn = attn_grads[0].reshape(flat), cube.flip(other, 1)
        waiting = {2: [2, k_two, c_two], 1: [1, k_one, c_one]}
        grads = {}
        found = fold([(k, c) for _, k, c in waiting.values()])
        for (group, state), (sent, kept) in zip(waiting.items(), found):
            state[1:] = [kept, cube.swap(cube.scatter[group], sent, state[0])]
            state[0] += 1
        small, after = sums, (found[0][0],)
        for k in range(cube.steps):
            more = [g for g in waiting if k > 0 and waiting[g][0] <= last]
            ended = [g for g in waiting if k > 0 and waiting[g][0] > last]
            pairs = [waiting[g][1:] for g in more]
            finals = [waiting.pop(g)[1:] for g in ended]
            s_attn, k_attn, small, *found = fold_with_small(
                cube, k_attn, c_attn, small, pairs, finals, ids, after
            )
            c_attn = cube.swap(cube.scatter[0], s_attn, k)
            for n, g in enumerate(more):
                came = cube.swap(cube.scatter[g], found[2 * n], waiting[g][0])
                waiting[g] = [waiting[g][0] + 1, found[2 * n + 1], came]
            grads.update(zip(ended, found[2 * len(more) :]))
            after = ()
            if k == 0:
                images, there = hold([images, there], (small,))
                encoded = place_images(cube, spread(images, there), length)
                after = (encoded,)
            if k == 1:
                images = patch_of((small,))
                after = (images,)
            if k == last - 1:
                (images,) = hold([images], (small,))
                there = cube.flip(images, 2)
            if k == last:
                images, there = hold([images, there], (small,))
                patch_grad = place_images(cube, spread(images, there), length)
            small = (small,)
        two_grad, one_grad = grads[2], grads[1]
        qkv_grad, out_grad, small = finish_with_small(
            k_attn, c_attn, small[0], width
        )
        small = small.astype(f32) + cube.flip(small, 1).astype(f32)
    else:
        two_grad = scatter_plain(cube, *two_grads)
        one_grad = scatter_plain(cube, *one_grads)
        attn_grad = scatter_plain(cube, *attn_grads)
        qkv_grad = jnp.stack([attn_grad[:, i * width : (i + 1) * width] for i in range(3)])
        out_grad = attn_grad[:, 3 * width :].T
        encoded = place_images(cube, [enc.reshape(count, padded, d)], length)
        patch_grad = place_images(cube, [patch_of(())], length)

        def collect(ids_ref, *refs):
            gather_small(cube, ids_ref, refs[:4], refs[4])

        small = call(collect, [shape(ROWS, d, dtype=f32)], ids, sums, [], [])[0]
        small = lax.psum(small, AXES)

    def shard_row(at):
        return lax.dynamic_slice_in_dim(small, at + t_me, 1, 0)

    return (
        encoded,
        patch_grad,
        small[0],
        small[1],
        qkv_grad,
        jnp.concatenate((shard_row(6 + n_t), shard_row(6 + 2 * n_t)))[:, :width],
        out_grad,
        small[5],
        small[2],
        small[3],
        one_grad,
        shard_row(6)[0],
        two_grad.T,
        small[4],
    )


def solution(mesh):
    return jax.shard_map(
        partial(on_device, mesh.shape["dp"], mesh.shape["tensor"]),
        mesh=mesh,
        in_specs=(
            P("dp", None, None),
            P(),
            P(),
            P(None, "dp", "tensor"),
            P(None, "tensor"),
            P("tensor", "dp"),
            P(),
            P(),
            P(),
            P("dp", "tensor"),
            P("tensor"),
            P("tensor", "dp"),
            P(),
            P("dp", None, None),
        ),
        out_specs=(
            P("dp", None, None),
            P("dp", None, None),
            P(),
            P(),
            P(None, "dp", "tensor"),
            P(None, "tensor"),
            P("tensor", "dp"),
            P(),
            P(),
            P(),
            P("dp", "tensor"),
            P("tensor"),
            P("tensor", "dp"),
            P(),
        ),
        check_vma=False,
    )
```
